512 devices in a mesh: gx: 4 (over x), gy: 8 (over z_lo), gz: 16 (over y, z_hi, core).
Axes of the slice: x: 4, y: 4, z: 16 (z_hi: 2, z_lo: 8; z = z_hi * 8 + z_lo), core: 2. Of those that a mesh axis runs over, the one named last changes fastest.
Arguments:
- volume: bfloat16 [32, 64, 128, 128], P('gx', 'gy', 'gz'), may hold values from -6 to 6
- fine_weight: bfloat16 [27, 128, 128], replicated, may hold values from -0.109375 to 0.109375
- coarse_weight: bfloat16 [27, 128, 128], replicated, may hold values from -0.3125 to 0.3125
- cotangent: bfloat16 [16, 32, 64, 128], P('gx', 'gy', 'gz'), may hold values from -144 to 144
Outputs:
- coarse_out: bfloat16 [16, 32, 64, 128], P('gx', 'gy', 'gz')
- grad_volume: bfloat16 [32, 64, 128, 128], P('gx', 'gy', 'gz')
- grad_fine_weight: bfloat16 [27, 128, 128], replicated
- grad_coarse_weight: bfloat16 [27, 128, 128], replicated
The draws below stay inside these ranges and needn't reach their ends.
All inputs are finite; a program needn't handle non-finite values.
Results may differ from the reference program's by a relative error of at most 0.018.
Values may be sent and summed in bfloat16 or wider, within the bound.
No kernel may reach another device: no remote copies, remote signals or barrier semaphores. Data moves between devices by JAX's collectives and lax.ppermute only.
A program may use at most 64 MiB of HBM per device.

```python
import math
import jax
import jax.numpy as jnp
from jax import lax

C = 128
C2 = 128
BX = 8
BY = 8
BZ = 8
NX = 32
NY = 64
NZ = 128


def draw_cotangent(key, part):
    key = jax.random.fold_in(key, 7)
    key_base, key_shift = jax.random.split(key)
    shape = (NX // 2, NY // 2, NZ // 2, C2)
    base = 4.0 * jax.random.truncated_normal(key_base, -6.0, 6.0, shape, jnp.float32)
    offset = jax.random.randint(key_shift, (), 0, C2)
    brick_x = (jnp.arange(NX // 2) // (BX // 2))[:, None, None, None]
    brick_y = (jnp.arange(NY // 2) // (BY // 2))[None, :, None, None]
    brick_z = (jnp.arange(NZ // 2) // (BZ // 2))[None, None, :, None]
    brick = (brick_x * (NY // BY) + brick_y) * (NZ // BZ) + brick_z
    channel = jnp.arange(C2)[None, None, None, :]
    heavy = (brick + offset) % C2 == channel
    return (base * jnp.where(heavy, 6.0, 1.0)).astype(jnp.bfloat16)


def block_levels(key, shape, cuts, least, largest):
    factor_of = 1.0
    for axis_at, parts in cuts:
        draws = jax.random.uniform(jax.random.fold_in(jax.random.fold_in(key, 6), axis_at), (parts,), jnp.float32, least / len(cuts), largest / len(cuts))
        factor_of = factor_of * jnp.repeat(jnp.exp(draws), shape[axis_at] // parts).reshape((-1,) + (1,) * (len(shape) - 1 - axis_at))
    return factor_of


def noise(rng, extent, scale, reach, shards=(), held_as=jnp.bfloat16):
    drawn = jax.random.normal(rng, extent, jnp.float32) * scale
    if len(shards) > 0:
        drawn = block_levels(rng, extent, shards, -0.22, 0.18) * drawn
    return jnp.clip(drawn, min=-reach, max=reach).astype(held_as)


def setup_inputs(seed: int = 0) -> dict:
    keys = jax.random.split(jax.random.key(seed), 5)
    volume = noise(keys[0], (NX, NY, NZ, C), 1.0, 6.0, ((0, 4), (1, 8), (2, 16)))
    fine_weight = noise(keys[1], (27, C, C), (27 * C) ** -0.5, 0.109375)
    coarse_weight = noise(keys[2], (27, C, C2), (27 * C // 8) ** -0.5, 0.3125)
    cotangent = draw_cotangent(jax.random.fold_in(keys[4], 71), 0)
    return {"volume": volume, "fine_weight": fine_weight, "coarse_weight": coarse_weight, "cotangent": cotangent}


def conv_cells(volume, weights):
    kernel = weights.reshape(3, 3, 3, weights.shape[1], weights.shape[2])
    result = lax.conv_general_dilated(volume[None], kernel, (1, 1, 1), 'SAME', dimension_numbers=('NDHWC', 'DHWIO', 'NDHWC'), precision=lax.Precision.HIGHEST)
    return result[0]

def silu_slope(values):
    sigma = jax.nn.sigmoid(values)
    return sigma * (1.0 + values * (1.0 - sigma))

def pool_mean(values):
    sx, sy, sz, chans = values.shape
    blocks = values.reshape(sx // 2, 2, sy // 2, 2, sz // 2, 2, chans)
    return lax.optimization_barrier(jnp.mean(blocks, axis=(1, 3, 5)))

def spread_back(values):
    sx, sy, sz, chans = values.shape
    wide = jnp.broadcast_to(values[:, None, :, None, :, None, :], (sx, 2, sy, 2, sz, 2, chans))
    return wide.reshape(sx * 2, sy * 2, sz * 2, chans)

def settle(values):
    return lax.optimization_barrier(values.astype(jnp.bfloat16)).astype(jnp.float32)

def reference(volume, fine_weight, coarse_weight, cotangent):
    volume_f = volume.astype(jnp.float32)
    fine_f = fine_weight.astype(jnp.float32)
    coarse_f = coarse_weight.astype(jnp.float32)
    hidden = conv_cells(volume_f, fine_f)
    pooled = settle(pool_mean(jax.nn.silu(hidden)))
    coarse = conv_cells(pooled, coarse_f)
    coarse_out = jax.nn.silu(coarse).astype(jnp.bfloat16)
    coarse_grad = settle(cotangent.astype(jnp.float32) * silu_slope(coarse))
    coarse_pull = jax.vjp(conv_cells, pooled, coarse_f)[1]
    back_pooled, coarse_sum = coarse_pull(coarse_grad)
    cells_fine = NX * NY * NZ
    grad_coarse_weight = (coarse_sum / math.sqrt(cells_fine // 8)).astype(jnp.bfloat16)
    fine_grad = settle(spread_back(back_pooled) * 0.125 * silu_slope(hidden))
    fine_pull = jax.vjp(conv_cells, volume_f, fine_f)[1]
    back_volume, fine_sum = fine_pull(fine_grad)
    grad_fine_weight = (fine_sum / math.sqrt(cells_fine)).astype(jnp.bfloat16)
    grad_volume = back_volume.astype(jnp.bfloat16)
    return (coarse_out, grad_volume, grad_fine_weight, grad_coarse_weight)
```

```python
import math

import jax
import jax.numpy as jnp
from jax import lax
from jax.sharding import Mesh, PartitionSpec as P

AXES = ("gx", "gy", "y", "zh", "core")
WIDTH = ("y", "zh", "core")
PLANE = ("gx", "y")
LINE = ("gy", "zh")


def line(count, step):
    return [(i, i + step) for i in range(count) if 0 <= i + step < count]


def beside(last, leading, axis, count):
    before = lax.ppermute(last, axis, line(count, 1))
    after = lax.ppermute(leading, axis, line(count, -1))
    return before, after


def extended(x, axis, count, dim, width):
    length = x.shape[dim]
    last = lax.slice_in_dim(x, length - width, length, axis=dim)
    leading = lax.slice_in_dim(x, 0, width, axis=dim)
    before, after = beside(last, leading, axis, count)
    return jnp.concatenate([before, x, after], axis=dim)


def valid_conv(x, weights):
    kernel = weights.reshape(3, 3, 3, weights.shape[1], weights.shape[2])
    result = lax.conv_general_dilated(
        x[None],
        kernel,
        (1, 1, 1),
        "VALID",
        dimension_numbers=("NDHWC", "DHWIO", "NDHWC"),
        preferred_element_type=jnp.float32,
    )
    return result[0]


def valid_conv_back(x, weights):
    return valid_conv(x, jnp.transpose(weights[::-1], (0, 2, 1)))


def gather_taps(padded, extent):
    rows_x, rows_y, rows_z = extent
    pieces = []
    for i in range(3):
        for j in range(3):
            for k in range(3):
                pieces.append(padded[i : i + rows_x, j : j + rows_y, k : k + rows_z, :])
    stacked = jnp.concatenate(pieces, axis=3)
    return stacked.reshape(rows_x * rows_y * rows_z, stacked.shape[3])


def weight_terms(padded, grads):
    patches = gather_taps(padded, grads.shape[:3])
    flat = grads.reshape(-1, grads.shape[3])
    return lax.dot_general(
        patches, flat, (((0,), (0,)), ((), ())), preferred_element_type=jnp.float32
    )


def silu_slope(values):
    sigma = jax.nn.sigmoid(values)
    return sigma * (1.0 + values * (1.0 - sigma))


def pool_mean(values):
    sx, sy, sz, chans = values.shape
    blocks = values.reshape(sx // 2, 2, sy // 2, 2, sz // 2, 2, chans)
    return jnp.mean(blocks, axis=(1, 3, 5))


def spread_back(values):
    sx, sy, sz, chans = values.shape
    wide = jnp.broadcast_to(values[:, None, :, None, :, None, :], (sx, 2, sy, 2, sz, 2, chans))
    return wide.reshape(sx * 2, sy * 2, sz * 2, chans)


def inside(extent, starts, sizes):
    keep = None
    for dim in range(3):
        at = starts[dim] + lax.broadcasted_iota(jnp.int32, extent + (1,), dim)
        ok = (at >= 0) & (at < sizes[dim])
        keep = ok if keep is None else keep & ok
    return keep


def spread_rows(terms, axes, peers):
    rows, chans = terms.shape
    parts = terms.astype(jnp.bfloat16).reshape(peers, rows // peers, chans)
    got = lax.all_to_all(parts, axes, 0, 0, tiled=True)
    return jnp.sum(got.astype(jnp.float32), axis=0)


def gathered_rows(part, axes, peers):
    rows, chans = part.shape
    parts = jnp.broadcast_to(part[None], (peers, rows, chans))
    return lax.all_to_all(parts, axes, 0, 0, tiled=True).reshape(peers * rows, chans)


def total_over_slice(terms, scale, plane, along):
    rows, chans = terms.shape
    half = rows // 2
    core = lax.axis_index("core")
    swap = [(0, 1), (1, 0)]
    halves = terms.reshape(2, half, chans)
    mine = lax.dynamic_index_in_dim(halves, core, 0, keepdims=False)
    other = lax.dynamic_index_in_dim(halves, 1 - core, 0, keepdims=False)
    mine = mine + lax.ppermute(other.astype(jnp.bfloat16), "core", swap).astype(jnp.float32)

    part = spread_rows(mine, PLANE, plane)
    length = half // plane
    padded = -(-length // (16 * along)) * 16 * along
    part = jnp.pad(part, ((0, padded - length), (0, 0)))
    part = spread_rows(part, LINE, along)

    part = gathered_rows(part.astype(jnp.bfloat16), LINE, along)[:length].astype(jnp.float32)
    part = (part * scale).astype(jnp.bfloat16)
    mine = gathered_rows(part, PLANE, plane)
    other = lax.ppermute(mine, "core", swap)
    first = jnp.where(core == 0, mine, other)
    second = jnp.where(core == 0, other, mine)
    return jnp.concatenate([first, second], axis=0)


def local(volume, fine_weight, coarse_weight, cotangent):
    chans = volume.shape[3]
    sizes = {axis: lax.axis_size(axis) for axis in AXES}
    plane, along = (sizes["gx"] * sizes["y"], sizes["gy"] * sizes["zh"])
    place = [lax.axis_index("gx"), lax.axis_index("gy"), lax.axis_index(WIDTH)]
    peers = [sizes["gx"], sizes["gy"], sizes["y"] * sizes["zh"] * 2]
    fine_sizes = [8 * n for n in peers]
    coarse_sizes = [4 * n for n in peers]

    packed = jnp.concatenate([volume.reshape(512, chans), cotangent.reshape(64, chans)], axis=0)
    first = lax.axis_index("core") == 0
    near = [(i, i ^ 1) for i in range(peers[2])]
    far = [(i, i - 1 + 2 * (i % 2)) for i in range(1, peers[2] - 1)]
    inner = lax.ppermute(packed, WIDTH, near)
    outer = lax.ppermute(packed, WIDTH, far)
    before = jnp.where(first, outer, inner)
    after = jnp.where(first, inner, outer)
    wide = jnp.concatenate(
        [
            before[:512].reshape(8, 8, 8, chans)[:, :, 1:],
            volume,
            after[:512].reshape(8, 8, 8, chans)[:, :, :7],
        ],
        axis=2,
    )
    incoming = jnp.concatenate(
        [
            before[512:].reshape(4, 4, 4, chans)[:, :, 2:],
            cotangent,
            after[512:].reshape(4, 4, 4, chans)[:, :, :2],
        ],
        axis=2,
    ).astype(jnp.float32)
    wide = extended(wide, "gy", peers[1], 1, 3)
    wide = extended(wide, "gx", peers[0], 0, 3)

    hidden = valid_conv(wide, fine_weight)
    pooled = pool_mean(jax.nn.silu(hidden))
    starts = [4 * place[0] - 1, 4 * place[1] - 1, 4 * place[2] - 3]
    keep = inside((6, 6, 10), starts, coarse_sizes)
    pooled = jnp.where(keep, pooled, 0.0).astype(jnp.bfloat16)
    coarse = valid_conv(pooled, coarse_weight)
    coarse_out = jax.nn.silu(coarse[:, :, 2:6]).astype(jnp.bfloat16)
    coarse_grad = (incoming * silu_slope(coarse)).astype(jnp.bfloat16)
    coarse_sum = weight_terms(pooled[:, :, 2:8], coarse_grad[:, :, 2:6])

    around = extended(coarse_grad, "gy", peers[1], 1, 2)
    around = extended(around, "gx", peers[0], 0, 2)
    back_pooled = valid_conv_back(around, coarse_weight)
    spread = spread_back(back_pooled)[1:11, 1:11, 1:11] * 0.125
    fine_grad = spread * silu_slope(hidden[1:11, 1:11, 5:15])
    keep = inside((10, 10, 10), [8 * p - 1 for p in place], fine_sizes)
    fine_grad = jnp.where(keep, fine_grad, 0.0).astype(jnp.bfloat16)
    fine_sum = weight_terms(wide[2:12, 2:12, 6:16], fine_grad[1:9, 1:9, 1:9])
    grad_volume = valid_conv_back(fine_grad, fine_weight).astype(jnp.bfloat16)

    cells_fine = fine_sizes[0] * fine_sizes[1] * fine_sizes[2]
    fine_scale = 1.0 / math.sqrt(cells_fine)
    coarse_scale = 1.0 / math.sqrt(cells_fine // 8)
    pieces = 2 * plane
    rows = fine_sum.shape[0] // pieces
    both = jnp.concatenate(
        [fine_sum.reshape(pieces, rows, chans), coarse_sum.reshape(pieces, rows, chans)], axis=1
    )
    scale = jnp.where(
        lax.broadcasted_iota(jnp.int32, (2 * rows, 1), 0) < rows, fine_scale, coarse_scale
    )
    done = total_over_slice(both.reshape(-1, chans), scale, plane, along)
    done = done.reshape(pieces, 2 * rows, chans)
    grad_fine_weight = done[:, :rows].reshape(fine_weight.shape)
    grad_coarse_weight = done[:, rows:].reshape(coarse_weight.shape)
    return (coarse_out, grad_volume, grad_fine_weight, grad_coarse_weight)


def solution(mesh):
    shape = mesh.devices.shape
    inner = Mesh(mesh.devices.reshape(shape[0], shape[1], shape[2] // 4, 2, 2), AXES)
    cells = P("gx", "gy", WIDTH, None)
    return jax.shard_map(
        local,
        mesh=inner,
        in_specs=(cells, P(), P(), cells),
        out_specs=(cells, cells, P(), P()),
        check_vma=False,
    )
```

```python
import math

import jax
import jax.numpy as jnp
from jax import lax
from jax.experimental import pallas as pl
from jax.experimental.pallas import tpu as pltpu
from jax.sharding import Mesh, PartitionSpec as P

AXES = ("gx", "gy", "y", "zh", "core")
WIDTH = ("y", "zh", "core")
PLANE = ("gx", "y")
LINE = ("gy", "zh")
C = 128
F32 = jnp.float32
BF16 = jnp.bfloat16


def silu_slope(values):
    sigma = 1.0 / (1.0 + jnp.exp(-values))
    return sigma * (1.0 + values * (1.0 - sigma))


def inside(shape, starts, sizes):
    keep = None
    for dim in range(3):
        at = starts[dim] + lax.broadcasted_iota(jnp.int32, shape, dim)
        ok = (at >= 0) & (at < sizes[dim])
        keep = ok if keep is None else keep & ok
    return keep


def taps():
    return [(i, j, k) for i in range(3) for j in range(3) for k in range(3)]


def flat(values):
    return values.reshape(-1, C).astype(BF16)


def front_kernel(
    sizes, place, own, below, above, left, right, weights, coarse_weights, incoming,
    coarse_ref, grad_ref, pooled_ref, hidden_ref, core_ref,
    wide, patches, hidden, pairs,
):
    for x in range(8):
        wide[3 + x, 3:11, :24] = own[x].astype(F32).reshape(8, 24, C)
        wide[3 + x, :3, :24] = below[x].astype(F32).reshape(3, 24, C)
        wide[3 + x, 11:, :24] = above[x].astype(F32).reshape(3, 24, C)
    for x in range(3):
        wide[x, :, :24] = left[x].astype(F32).reshape(14, 24, C)
        wide[11 + x, :, :24] = right[x].astype(F32).reshape(14, 24, C)

    def gather(x, carry):
        for k in range(3):
            line = wide[x, :, k + 1 : k + 25]
            for j in range(3):
                at = (3 * j + k) * C
                patches[x, :, at : at + C] = flat(line[j : j + 12])
        return carry

    lax.fori_loop(0, 14, gather, 0)

    def convolve(part, carry):
        total = jnp.zeros((1152, C), F32)
        for i in range(3):
            cells = patches[pl.ds(part * 4 + i, 4)].reshape(1152, 9 * C)
            total = total + jnp.dot(
                cells, weights[9 * C * i : 9 * C * (i + 1)], preferred_element_type=F32
            )
        hidden[pl.ds(part * 4, 4)] = total.reshape(4, 12, 24, C)
        return carry

    lax.fori_loop(0, 3, convolve, 0)

    for x in range(6):
        value = hidden[2 * x : 2 * x + 2]
        active = value / (1.0 + jnp.exp(-value))
        active = active[0] + active[1]
        active = active.reshape(6, 2, 24, C)
        pairs[...] = active[:, 0] + active[:, 1]
        mean = (pairs[:, pl.ds(0, 12, 2)] + pairs[:, pl.ds(1, 12, 2)]) * 0.125
        starts = [4 * place[0] - 1 + x, 4 * place[1] - 1, 4 * place[2] - 3]
        keep = inside((1, 6, 12, C), starts, sizes)[0]
        pooled_ref[x, :, :12] = jnp.where(keep, mean, 0.0)
        pooled_ref[x, :, 12:] = jnp.zeros((6, 4, C), F32)

    cells = jnp.concatenate(
        [flat(pooled_ref[i : i + 4, j : j + 4, k : k + 8]) for i, j, k in taps()], axis=1
    )
    coarse = jnp.dot(cells, coarse_weights[...], preferred_element_type=F32)
    coarse_ref[...] = coarse
    grad_ref[...] = (incoming[...] * silu_slope(coarse)).astype(BF16)

    for x in range(10):
        hidden_ref[x] = hidden[1 + x, 1:11, 4:20]
        core_ref[x] = wide[2 + x, 2:12, 7:23]


def side_kernel(sizes, place, pooled, grad, hidden, sum_ref, slope_ref):
    at = lax.broadcasted_iota(jnp.int32, (C, C), 0) % 8
    mine = jnp.where((at >= 2) & (at < 6), grad[...].astype(F32), 0.0)
    turned = mine.T.astype(BF16)
    for i in range(3):
        cells = jnp.concatenate(
            [
                flat(pooled[i : i + 4, j : j + 4, k : k + 8])
                for j in range(3)
                for k in range(3)
            ],
            axis=1,
        )
        terms = jnp.dot(turned, cells, preferred_element_type=F32)
        for t in range(9):
            row = (9 * i + t) * C
            sum_ref[row : row + C] = terms[:, t * C : (t + 1) * C].T.astype(BF16)
    for x in range(10):
        starts = [8 * place[0] - 1 + x, 8 * place[1] - 1, 8 * place[2] - 2]
        keep = inside((1, 10, 16, C), starts, sizes)[0]
        slope_ref[x] = jnp.where(keep, silu_slope(hidden[x]) * 0.125, 0.0)


def back_kernel(around, coarse_weights, slope, core, sum_ref, grad_ref, wide, spread):
    for x in range(8):
        wide[x, :, :8] = around[64 * x : 64 * x + 64].astype(F32).reshape(8, 8, C)
    cells = jnp.concatenate(
        [flat(wide[2 - i : 8 - i, 2 - j : 8 - j, 2 - k : 10 - k]) for i, j, k in taps()], axis=1
    )
    turned = jnp.concatenate([coarse_weights[t] for t in range(27)], axis=1)
    back = lax.dot_general(cells, turned, (((1,), (1,)), ((), ())), preferred_element_type=F32)
    back = back.reshape(6, 6, 8, C)
    spread[:, :, pl.ds(0, 8, 2)] = back
    spread[:, :, pl.ds(1, 8, 2)] = back
    for x in range(10):
        for y in range(10):
            grad_ref[x, y] = spread[(x + 1) // 2, (y + 1) // 2] * slope[x, y]
    turned = grad_ref[1:9, 1:9, 2:10].reshape(512, C).T.astype(BF16)
    for i in range(3):
        cells = jnp.concatenate(
            [
                flat(core[i : i + 8, j : j + 8, k : k + 8])
                for j in range(3)
                for k in range(3)
            ],
            axis=1,
        )
        terms = jnp.dot(turned, cells, preferred_element_type=F32)
        for t in range(9):
            row = (9 * i + t) * C
            sum_ref[row : row + C] = terms[:, t * C : (t + 1) * C].T.astype(BF16)


def volume_kernel(grad, weights, out_ref):
    total = jnp.zeros((512, C), F32)
    for i in range(3):
        cells = jnp.concatenate(
            [
                flat(grad[2 - i : 10 - i, 2 - j : 10 - j, 3 - k : 11 - k])
                for j in range(3)
                for k in range(3)
            ],
            axis=1,
        )
        turned = jnp.concatenate([weights[9 * i + t] for t in range(9)], axis=1)
        total = total + lax.dot_general(
            cells, turned, (((1,), (1,)), ((), ())), preferred_element_type=F32
        )
    out_ref[...] = total.astype(BF16)


def call(kernel, outs, inputs, scratch=(), scalars=0, flops=0):
    in_specs = [
        pl.BlockSpec(memory_space=pltpu.SMEM if n < scalars else pltpu.VMEM)
        for n in range(len(inputs))
    ]
    moved = sum(a.size * a.dtype.itemsize for a in inputs)
    moved += sum(math.prod(s) * jnp.dtype(t).itemsize for s, t in outs)
    return pl.pallas_call(
        kernel,
        out_shape=[jax.ShapeDtypeStruct(s, t) for s, t in outs],
        in_specs=in_specs,
        out_specs=[pl.BlockSpec(memory_space=pltpu.VMEM) for _ in outs],
        scratch_shapes=[pltpu.VMEM(s, t) for s, t in scratch],
        compiler_params=pltpu.CompilerParams(vmem_limit_bytes=40 * 1024 * 1024),
        cost_estimate=pl.CostEstimate(flops=flops, bytes_accessed=moved, transcendentals=0),
    )(*inputs)


def line(count, step):
    return [(i, i + step) for i in range(count) if 0 <= i + step < count]


def beside(last, leading, axis, count):
    before = lax.ppermute(last, axis, line(count, 1))
    after = lax.ppermute(leading, axis, line(count, -1))
    return before, after


def spread_rows(terms, axes, peers):
    rows = terms.shape[0]
    parts = terms.astype(BF16).reshape(peers, rows // peers, C)
    got = lax.all_to_all(parts, axes, 0, 0, tiled=True)
    return jnp.sum(got.astype(F32), axis=0)


def gathered_rows(part, axes, peers):
    rows = part.shape[0]
    parts = jnp.broadcast_to(part[None], (peers, rows, C))
    return lax.all_to_all(parts, axes, 0, 0, tiled=True).reshape(peers * rows, C)


def totals(fine_sum, coarse_sum, fine_scale, coarse_scale, plane, along):
    first = lax.axis_index("core") == 0
    swap = [(0, 1), (1, 0)]
    mine = jnp.where(first, fine_sum, coarse_sum).astype(F32)
    other = jnp.where(first, coarse_sum, fine_sum)
    mine = mine + lax.ppermute(other, "core", swap).astype(F32)

    part = spread_rows(mine, PLANE, plane)
    length = part.shape[0]
    padded = -(-length // (16 * along)) * 16 * along
    part = jnp.pad(part, ((0, padded - length), (0, 0)))
    part = spread_rows(part, LINE, along) * jnp.where(first, fine_scale, coarse_scale)

    part = gathered_rows(part.astype(BF16), LINE, along)[:length]
    mine = gathered_rows(part, PLANE, plane)
    other = lax.ppermute(mine, "core", swap)
    return jnp.where(first, mine, other), jnp.where(first, other, mine)


def local(volume, fine_weight, coarse_weight, cotangent):
    sizes = {axis: lax.axis_size(axis) for axis in AXES}
    plane, along = (sizes["gx"] * sizes["y"], sizes["gy"] * sizes["zh"])
    peers = [sizes["gx"], sizes["gy"], sizes["y"] * sizes["zh"] * 2]
    place = [lax.axis_index("gx"), lax.axis_index("gy"), lax.axis_index(WIDTH)]
    place = jnp.stack([p.astype(jnp.int32) for p in place])
    fine_sizes = [8 * n for n in peers]
    coarse_sizes = [4 * n for n in peers]
    fine_rows = fine_weight.reshape(27 * C, C)
    coarse_rows = coarse_weight.reshape(27 * C, C)

    packed = jnp.concatenate([volume.reshape(512, C), cotangent.reshape(64, C)], axis=0)
    first = lax.axis_index("core") == 0
    near = [(i, i ^ 1) for i in range(peers[2])]
    far = [(i, i - 1 + 2 * (i % 2)) for i in range(1, peers[2] - 1)]
    inner = lax.ppermute(packed, WIDTH, near)
    outer = lax.ppermute(packed, WIDTH, far)
    before = jnp.where(first, outer, inner)
    after = jnp.where(first, inner, outer)
    own = jnp.concatenate(
        [before[:512].reshape(8, 8, 8, C), volume, after[:512].reshape(8, 8, 8, C)], axis=2
    )
    incoming = jnp.concatenate(
        [
            before[512:].reshape(4, 4, 4, C)[:, :, 2:],
            cotangent,
            after[512:].reshape(4, 4, 4, C)[:, :, :2],
        ],
        axis=2,
    ).astype(F32)
    below, above = beside(own[:, 5:], own[:, :3], "gy", peers[1])
    sides = [
        jnp.concatenate([below[at], own[at], above[at]], axis=1)
        for at in (slice(5, 8), slice(0, 3))
    ]
    left, right = beside(sides[0], sides[1], "gx", peers[0])

    coarse, coarse_grad, pooled, hidden, core = call(
        lambda *refs: front_kernel(coarse_sizes, *refs),
        [
            ((128, C), F32),
            ((128, C), BF16),
            ((6, 6, 16, C), F32),
            ((10, 10, 16, C), F32),
            ((10, 10, 16, C), F32),
        ],
        [
            place,
            own.reshape(8, 192, C),
            below.reshape(8, 72, C),
            above.reshape(8, 72, C),
            left.reshape(3, 336, C),
            right.reshape(3, 336, C),
            fine_rows,
            coarse_rows,
            incoming.reshape(128, C),
        ],
        scratch=[
            ((14, 14, 32, C), F32),
            ((14, 288, 9 * C), BF16),
            ((12, 12, 24, C), F32),
            ((6, 24, C), F32),
        ],
        scalars=1,
        flops=2 * 3600 * 27 * C * C,
    )
    coarse_out = jax.nn.silu(coarse.reshape(4, 4, 8, C)[:, :, 2:6]).astype(BF16)

    grads = coarse_grad.reshape(4, 4, 8, C)
    below, above = beside(grads[:, 2:], grads[:, :2], "gy", peers[1])
    grads = jnp.concatenate([below, grads, above], axis=1)
    left, right = beside(grads[2:], grads[:2], "gx", peers[0])
    around = jnp.concatenate([left, grads, right], axis=0)

    coarse_sum, slope = call(
        lambda *refs: side_kernel(fine_sizes, *refs),
        [((27 * C, C), BF16), ((10, 10, 16, C), F32)],
        [place, pooled, coarse_grad, hidden],
        scalars=1,
        flops=2 * 128 * 27 * C * C,
    )
    fine_sum, fine_grad = call(
        back_kernel,
        [((27 * C, C), BF16), ((10, 10, 16, C), F32)],
        [around.reshape(512, C), coarse_weight, slope, core],
        scratch=[((8, 8, 16, C), F32), ((6, 6, 16, C), F32)],
        flops=2 * 800 * 27 * C * C,
    )
    (grad_volume,) = call(
        volume_kernel, [((512, C), BF16)], [fine_grad, fine_weight], flops=2 * 512 * 27 * C * C
    )

    cells_fine = fine_sizes[0] * fine_sizes[1] * fine_sizes[2]
    fine_scale = 1.0 / math.sqrt(cells_fine)
    coarse_scale = 1.0 / math.sqrt(cells_fine // 8)
    fine_done, coarse_done = totals(
        fine_sum, coarse_sum, fine_scale, coarse_scale, plane, along
    )
    return (
        coarse_out,
        grad_volume.reshape(8, 8, 8, C),
        fine_done.reshape(27, C, C),
        coarse_done.reshape(27, C, C),
    )


def solution(mesh):
    shape = mesh.devices.shape
    inner = Mesh(mesh.devices.reshape(shape[0], shape[1], shape[2] // 4, 2, 2), AXES)
    cells = P("gx", "gy", WIDTH, None)
    return jax.shard_map(
        local,
        mesh=inner,
        in_specs=(cells, P(), P(), cells),
        out_specs=(cells, cells, P(), P()),
        check_vma=False,
    )
```

```python
import math

import jax
import jax.numpy as jnp
from jax import lax
from jax.experimental import pallas as pl
from jax.experimental.pallas import tpu as pltpu
from jax.sharding import Mesh, PartitionSpec as P

AXES = ("gx", "gy", "y", "zh", "core")
WIDTH = ("y", "zh", "core")
PLANE = ("gx", "y")
LINE = ("gy", "zh")
C = 128
F32 = jnp.float32
BF16 = jnp.bfloat16


def silu_slope(values):
    sigma = 1.0 / (1.0 + jnp.exp(-values))
    return sigma * (1.0 + values * (1.0 - sigma))


def inside(shape, starts, sizes):
    keep = None
    for dim in range(3):
        at = starts[dim] + lax.broadcasted_iota(jnp.int32, shape, dim)
        ok = (at >= 0) & (at < sizes[dim])
        keep = ok if keep is None else keep & ok
    return keep


def taps():
    return [(i, j, k) for i in range(3) for j in range(3) for k in range(3)]


def flat(values):
    return values.reshape(-1, C).astype(BF16)


def weight_terms(turned, cells, sum_ref, at):
    terms = jnp.dot(turned, cells, preferred_element_type=F32)
    for t in range(9):
        row = (at + t) * C
        sum_ref[row : row + C] = terms[:, t * C : (t + 1) * C].T.astype(BF16)


def back_conv(grads, weights):
    cells = jnp.concatenate(
        [flat(grads[2 - i : 8 - i, 2 - j : 8 - j, 2 - k : 10 - k]) for i, j, k in taps()], axis=1
    )
    turned = jnp.concatenate([weights[t] for t in range(27)], axis=1)
    back = lax.dot_general(cells, turned, (((1,), (1,)), ((), ())), preferred_element_type=F32)
    return back.reshape(6, 6, 8, C)


def front_kernel(
    fine_sizes, coarse_sizes, place, own, below, above, left, right, weights, coarse_weights, incoming,
    coarse_ref, grad_ref, slope_ref, fine_ref, coarse_sum_ref,
    wide, patches, hidden, pairs, pooled, grads, spread, shares,
):
    wide[:, :, 16:] = jnp.zeros((14, 14, 8, C), F32)
    for x in range(8):
        wide[3 + x, 3:11, :16] = own[x].astype(F32).reshape(8, 16, C)
        wide[3 + x, :3, :16] = below[x].astype(F32).reshape(3, 16, C)
        wide[3 + x, 11:, :16] = above[x].astype(F32).reshape(3, 16, C)
    for x in range(3):
        wide[x, :, :16] = left[x].astype(F32).reshape(14, 16, C)
        wide[11 + x, :, :16] = right[x].astype(F32).reshape(14, 16, C)

    def gather(x, carry):
        for k in range(3):
            line = wide[x, :, k + 1 : k + 17]
            for j in range(3):
                at = (3 * j + k) * C
                patches[x, :, at : at + C] = flat(line[j : j + 12])
        return carry

    lax.fori_loop(0, 14, gather, 0)

    def convolve(part, carry):
        total = jnp.zeros((768, C), F32)
        for i in range(3):
            cells = patches[pl.ds(part * 4 + i, 4)].reshape(768, 9 * C)
            total = total + jnp.dot(
                cells, weights[9 * C * i : 9 * C * (i + 1)], preferred_element_type=F32
            )
        hidden[pl.ds(part * 4, 4)] = total.reshape(4, 12, 16, C)
        return carry

    lax.fori_loop(0, 3, convolve, 0)

    used = lax.broadcasted_iota(jnp.int32, (1, 12, 16, C), 2) < 12
    for x in range(6):
        active = None
        for half in range(2):
            value = hidden[2 * x + half]
            sigma = 1.0 / (1.0 + jnp.exp(-value))
            slope = sigma * (1.0 + value * (1.0 - sigma)) * 0.125
            starts = [8 * place[0] - 2 + 2 * x + half, 8 * place[1] - 2, 8 * place[2] - 2]
            keep = (inside((1, 12, 16, C), starts, fine_sizes) & used)[0]
            slope_ref[2 * x + half] = jnp.where(keep, slope, 0.0)
            value = value * sigma
            active = value if active is None else active + value
        active = active.reshape(6, 2, 16, C)
        pairs[...] = active[:, 0] + active[:, 1]
        mean = (pairs[:, pl.ds(0, 8, 2)] + pairs[:, pl.ds(1, 8, 2)]) * 0.125
        starts = [4 * place[0] - 1 + x, 4 * place[1] - 1, 4 * place[2] - 1]
        keep = inside((1, 6, 8, C), starts, coarse_sizes)[0]
        pooled[x, :, :8] = jnp.where(keep, mean, 0.0)
        pooled[x, :, 8:] = jnp.zeros((6, 8, C), F32)

    cells = [flat(pooled[i : i + 4, j : j + 4, k : k + 8]) for i, j, k in taps()]
    coarse = jnp.dot(
        jnp.concatenate(cells, axis=1), coarse_weights[...].reshape(27 * C, C), preferred_element_type=F32
    )
    coarse_ref[...] = coarse
    grad = (incoming[...] * silu_slope(coarse)).astype(BF16)
    grad_ref[...] = grad
    grad = grad.astype(F32)

    grads[...] = jnp.zeros((8, 8, 16, C), F32)
    grads[2:6, 2:6, 2:10] = grad.reshape(4, 4, 8, C)
    back = back_conv(grads, coarse_weights)
    spread[:, :, pl.ds(0, 8, 2)] = back
    spread[:, :, pl.ds(1, 8, 2)] = back
    for x in range(12):
        for y in range(12):
            shares[x, y] = spread[x // 2, y // 2] * slope_ref[x, y]
    turned = shares[...].reshape(2304, C).T.astype(BF16)
    for i in range(3):
        weight_terms(turned, patches[i : i + 12].reshape(2304, 9 * C), fine_ref, 9 * i)
    turned = grad.T.astype(BF16)
    for i in range(3):
        weight_terms(
            turned, jnp.concatenate(cells[9 * i : 9 * i + 9], axis=1), coarse_sum_ref, 9 * i
        )


def volume_kernel(around, coarse_weights, slope, weights, out_ref, grads, spread, fine):
    for x in range(8):
        grads[x, :, :8] = around[64 * x : 64 * x + 64].astype(F32).reshape(8, 8, C)
    back = back_conv(grads, coarse_weights)
    spread[:, :, pl.ds(0, 8, 2)] = back
    spread[:, :, pl.ds(1, 8, 2)] = back
    for x in range(10):
        for y in range(10):
            fine[x, y] = spread[(x + 1) // 2, (y + 1) // 2] * slope[x + 1, y + 1]
    total = jnp.zeros((512, C), F32)
    for i in range(3):
        cells = jnp.concatenate(
            [
                flat(fine[2 - i : 10 - i, 2 - j : 10 - j, 3 - k : 11 - k])
                for j in range(3)
                for k in range(3)
            ],
            axis=1,
        )
        turned = jnp.concatenate([weights[9 * i + t] for t in range(9)], axis=1)
        total = total + lax.dot_general(
            cells, turned, (((1,), (1,)), ((), ())), preferred_element_type=F32
        )
    out_ref[...] = total.astype(BF16)


def call(kernel, outs, inputs, scratch=(), scalars=0, flops=0):
    in_specs = [
        pl.BlockSpec(memory_space=pltpu.SMEM if n < scalars else pltpu.VMEM)
        for n in range(len(inputs))
    ]
    moved = sum(a.size * a.dtype.itemsize for a in inputs)
    moved += sum(math.prod(s) * jnp.dtype(t).itemsize for s, t in outs)
    return pl.pallas_call(
        kernel,
        out_shape=[jax.ShapeDtypeStruct(s, t) for s, t in outs],
        in_specs=in_specs,
        out_specs=[pl.BlockSpec(memory_space=pltpu.VMEM) for _ in outs],
        scratch_shapes=[pltpu.VMEM(s, t) for s, t in scratch],
        compiler_params=pltpu.CompilerParams(vmem_limit_bytes=40 * 1024 * 1024),
        cost_estimate=pl.CostEstimate(flops=flops, bytes_accessed=moved, transcendentals=0),
    )(*inputs)


def line(count, step):
    return [(i, i + step) for i in range(count) if 0 <= i + step < count]


def beside(last, leading, axis, count):
    before = lax.ppermute(last, axis, line(count, 1))
    after = lax.ppermute(leading, axis, line(count, -1))
    return before, after


def along_width(x, count):
    outer = lax.ppermute(x, WIDTH, [(i, i - 1 + 2 * (i % 2)) for i in range(1, count - 1)])
    inner = lax.ppermute(x, WIDTH, [(i, i ^ 1) for i in range(count)])
    return outer, inner


def in_order(outer, inner):
    first = lax.axis_index("core") == 0
    return jnp.where(first, outer, inner), jnp.where(first, inner, outer)


def spread_rows(terms, axes, peers):
    rows = terms.shape[0]
    parts = terms.astype(BF16).reshape(peers, rows // peers, C)
    return lax.all_to_all(parts, axes, 0, 0, tiled=True)


def gathered_rows(part, axes, peers):
    rows = part.shape[0]
    parts = jnp.broadcast_to(part[None], (peers, rows, C))
    return lax.all_to_all(parts, axes, 0, 0, tiled=True)


def summed(parts):
    return jnp.sum(parts.astype(F32), axis=0)


def joined(parts):
    return parts.reshape(-1, C)


def local(volume, fine_weight, coarse_weight, cotangent):
    sizes = {axis: lax.axis_size(axis) for axis in AXES}
    plane, along = (sizes["gx"] * sizes["y"], sizes["gy"] * sizes["zh"])
    peers = [sizes["gx"], sizes["gy"], sizes["y"] * sizes["zh"] * 2]
    place = [lax.axis_index("gx"), lax.axis_index("gy"), lax.axis_index(WIDTH)]
    place = jnp.stack([p.astype(jnp.int32) for p in place])
    fine_sizes = [8 * n for n in peers]
    coarse_sizes = [4 * n for n in peers]

    before, after = in_order(*along_width(volume, peers[2]))
    own = jnp.concatenate([before[:, :, 4:], volume, after[:, :, :4]], axis=2)
    below, above = beside(own[:, 5:], own[:, :3], "gy", peers[1])
    sides = [
        jnp.concatenate([below[at], own[at], above[at]], axis=1)
        for at in (slice(5, 8), slice(0, 3))
    ]
    left, right = beside(sides[0], sides[1], "gx", peers[0])
    incoming = jnp.pad(cotangent.astype(F32), ((0, 0), (0, 0), (0, 4), (0, 0)))

    coarse, coarse_grad, slope, fine_sum, coarse_sum = call(
        lambda *refs: front_kernel(fine_sizes, coarse_sizes, *refs),
        [
            ((128, C), F32),
            ((128, C), BF16),
            ((12, 12, 16, C), F32),
            ((27 * C, C), BF16),
            ((27 * C, C), BF16),
        ],
        [
            place,
            own.reshape(8, 128, C),
            below.reshape(8, 48, C),
            above.reshape(8, 48, C),
            left.reshape(3, 224, C),
            right.reshape(3, 224, C),
            fine_weight.reshape(27 * C, C),
            coarse_weight,
            incoming.reshape(128, C),
        ],
        scratch=[
            ((14, 14, 24, C), F32),
            ((14, 192, 9 * C), BF16),
            ((12, 12, 16, C), F32),
            ((6, 16, C), F32),
            ((6, 6, 16, C), F32),
            ((8, 8, 16, C), F32),
            ((6, 6, 16, C), F32),
            ((12, 12, 16, C), F32),
        ],
        scalars=1,
        flops=2 * 5000 * 27 * C * C,
    )
    coarse_out = jax.nn.silu(coarse.reshape(4, 4, 8, C)[:, :, :4]).astype(BF16)

    first = lax.axis_index("core") == 0
    swap = [(0, 1), (1, 0)]
    cells_fine = fine_sizes[0] * fine_sizes[1] * fine_sizes[2]
    scale = jnp.where(first, 1.0 / math.sqrt(cells_fine), 1.0 / math.sqrt(cells_fine // 8))
    grads = coarse_grad.reshape(4, 4, 8, C)[:, :, :4]
    mine = jnp.where(first, fine_sum, coarse_sum).astype(F32)
    other = jnp.where(first, coarse_sum, fine_sum)
    mine = mine + lax.ppermute(other, "core", swap).astype(F32)

    halo = along_width(grads, peers[2])
    parts = spread_rows(mine, PLANE, plane)
    parts, halo = lax.optimization_barrier((parts, halo))
    part = summed(parts)
    length = part.shape[0]
    padded = -(-length // (16 * along)) * 16 * along
    part = jnp.pad(part, ((0, padded - length), (0, 0)))
    before, after = in_order(*halo)
    grads = jnp.concatenate([before[:, :, 2:], grads, after[:, :, :2]], axis=2)

    halo = beside(grads[:, 2:], grads[:, :2], "gy", peers[1])
    parts = spread_rows(part, LINE, along)
    parts, halo = lax.optimization_barrier((parts, halo))
    part = (summed(parts) * scale).astype(BF16)
    grads = jnp.concatenate([halo[0], grads, halo[1]], axis=1)

    halo = beside(grads[2:], grads[:2], "gx", peers[0])
    parts = gathered_rows(part, LINE, along)
    parts, halo = lax.optimization_barrier((parts, halo))
    part = joined(parts)[:length]
    around = jnp.concatenate([halo[0], grads, halo[1]], axis=0)
    (grad_volume,) = call(
        volume_kernel,
        [((512, C), BF16)],
        [around.reshape(512, C), coarse_weight, slope, fine_weight],
        scratch=[((8, 8, 16, C), F32), ((6, 6, 16, C), F32), ((10, 10, 16, C), F32)],
        flops=2 * 800 * 27 * C * C,
    )

    mine = joined(gathered_rows(part, PLANE, plane))
    other = lax.ppermute(mine, "core", swap)
    fine_done = jnp.where(first, mine, other)
    coarse_done = jnp.where(first, other, mine)
    return (
        coarse_out,
        grad_volume.reshape(8, 8, 8, C),
        fine_done.reshape(27, C, C),
        coarse_done.reshape(27, C, C),
    )


def solution(mesh):
    shape = mesh.devices.shape
    inner = Mesh(mesh.devices.reshape(shape[0], shape[1], shape[2] // 4, 2, 2), AXES)
    cells = P("gx", "gy", WIDTH, None)
    return jax.shard_map(
        local,
        mesh=inner,
        in_specs=(cells, P(), P(), cells),
        out_specs=(cells, cells, P(), P()),
        check_vma=False,
    )
```

```python
import math

import jax
import jax.numpy as jnp
from jax import lax
from jax.experimental import pallas as pl
from jax.experimental.pallas import tpu as pltpu
from jax.sharding import Mesh, PartitionSpec as P

AXES = ("gx", "gy", "y", "zh", "core")
WIDTH = ("y", "zh", "core")
PLANE = ("gx", "y")
LINE = ("gy", "zh")
C = 128
F32 = jnp.float32
BF16 = jnp.bfloat16


def silu_slope(values):
    sigma = 1.0 / (1.0 + jnp.exp(-values))
    return sigma * (1.0 + values * (1.0 - sigma))


def inside(shape, starts, sizes):
    keep = None
    for dim in range(3):
        at = starts[dim] + lax.broadcasted_iota(jnp.int32, shape, dim)
        ok = (at >= 0) & (at < sizes[dim])
        keep = ok if keep is None else keep & ok
    return keep


def taps():
    return [(i, j, k) for i in range(3) for j in range(3) for k in range(3)]


def flat(values):
    return values.reshape(-1, C).astype(BF16)


def weight_terms(turned, cells, sum_ref, at):
    terms = jnp.dot(turned, cells, preferred_element_type=F32)
    for t in range(9):
        row = (at + t) * C
        sum_ref[row : row + C] = terms[:, t * C : (t + 1) * C].T.astype(BF16)


def back_conv(grads, weights):
    cells = jnp.concatenate(
        [flat(grads[2 - i : 8 - i, 2 - j : 8 - j, 2 - k : 10 - k]) for i, j, k in taps()], axis=1
    )
    turned = jnp.concatenate([weights[t] for t in range(27)], axis=1)
    back = lax.dot_general(cells, turned, (((1,), (1,)), ((), ())), preferred_element_type=F32)
    return back.reshape(6, 6, 8, C)


def gather(wide, patches, planes, start, length):
    def plane(x, carry):
        for k in range(3):
            line = wide[x, :, start + k : start + k + length]
            for j in range(3):
                at = (3 * j + k) * C
                patches[x, :, at : at + C] = flat(line[j : j + 12])
        return carry

    lax.fori_loop(0, planes, plane, 0)


def fine_conv(patches, weights, at, planes):
    rows = planes * 288
    total = jnp.zeros((rows, C), F32)
    for i in range(3):
        cells = patches[pl.ds(at + i, planes)].reshape(rows, 9 * C)
        total = total + jnp.dot(
            cells, weights[9 * C * i : 9 * C * (i + 1)], preferred_element_type=F32
        )
    return total.reshape(planes, 12, 24, C)


def fill(wide, at, x, own, below, above):
    wide[at, 3:11, :24] = own[x].astype(F32).reshape(8, 24, C)
    wide[at, :3, :24] = below[x].astype(F32).reshape(3, 24, C)
    wide[at, 11:, :24] = above[x].astype(F32).reshape(3, 24, C)


def inner_kernel(own, below, above, weights, hidden_ref, wide, patches):
    for x in range(8):
        fill(wide, x, x, own, below, above)
    gather(wide, patches, 8, 1, 24)
    for part in range(2):
        hidden_ref[3 * part : 3 * part + 3] = fine_conv(patches, weights, 3 * part, 3)


def front_kernel(
    fine_sizes, coarse_sizes, place, own, below, above, left, right, weights, coarse_weights, incoming, inner,
    coarse_ref, grad_ref, slope_ref, pooled,
    wide, patches, outer, pairs,
):
    for x in range(3):
        wide[x, :, :24] = left[x].astype(F32).reshape(14, 24, C)
        wide[7 + x, :, :24] = right[x].astype(F32).reshape(14, 24, C)
    for x in range(2):
        fill(wide, 3 + x, x, own, below, above)
        fill(wide, 5 + x, 6 + x, own, below, above)
    gather(wide, patches, 10, 1, 24)
    for part in range(2):
        outer[3 * part : 3 * part + 3] = fine_conv(patches, weights, 5 * part, 3)

    for x in range(6):
        active = None
        for at in (2 * x, 2 * x + 1):
            value = inner[at - 3] if 3 <= at < 9 else outer[at if at < 3 else at - 6]
            sigma = 1.0 / (1.0 + jnp.exp(-value))
            slope = sigma * (1.0 + value * (1.0 - sigma)) * 0.125
            starts = [8 * place[0] - 2 + at, 8 * place[1] - 2, 8 * place[2] - 6]
            keep = inside((1, 12, 24, C), starts, fine_sizes)[0]
            slope_ref[at] = jnp.where(keep, slope, 0.0)
            value = value * sigma
            active = value if active is None else active + value
        active = active.reshape(6, 2, 24, C)
        pairs[...] = active[:, 0] + active[:, 1]
        mean = (pairs[:, pl.ds(0, 12, 2)] + pairs[:, pl.ds(1, 12, 2)]) * 0.125
        starts = [4 * place[0] - 1 + x, 4 * place[1] - 1, 4 * place[2] - 3]
        keep = inside((1, 6, 12, C), starts, coarse_sizes)[0]
        pooled[x, :, :12] = jnp.where(keep, mean, 0.0)
        pooled[x, :, 12:] = jnp.zeros((6, 4, C), F32)

    cells = [flat(pooled[i : i + 4, j : j + 4, k : k + 8]) for i, j, k in taps()]
    coarse = jnp.dot(
        jnp.concatenate(cells, axis=1), coarse_weights[...], preferred_element_type=F32
    )
    coarse_ref[...] = coarse
    grad_ref[...] = (incoming[...] * silu_slope(coarse)).astype(BF16)


def share_kernel(grad_in, pooled, coarse_weights, slope, turned_ref, sum_ref, grads, spread, shares):
    grad = grad_in[...].astype(F32)
    grads[...] = jnp.zeros((8, 8, 16, C), F32)
    grads[2:6, 2:6, :8] = grad.reshape(4, 4, 8, C)
    back = back_conv(grads, coarse_weights)
    spread[:, :, pl.ds(0, 8, 2)] = back
    spread[:, :, pl.ds(1, 8, 2)] = back
    for x in range(12):
        for y in range(12):
            shares[x, y] = spread[x // 2, y // 2, 2:10] * slope[x, y, 6:14]
    turned_ref[...] = shares[...].reshape(1152, C).T.astype(BF16)

    at = lax.broadcasted_iota(jnp.int32, (C, C), 0) % 8
    turned = jnp.where((at >= 2) & (at < 6), grad, 0.0).T.astype(BF16)
    for i in range(3):
        cells = [
            flat(pooled[i : i + 4, j : j + 4, k : k + 8]) for j in range(3) for k in range(3)
        ]
        weight_terms(turned, jnp.concatenate(cells, axis=1), sum_ref, 9 * i)


def fine_kernel(own, below, above, left, right, turned, sum_ref, wide, patches):
    for x in range(8):
        fill(wide, 3 + x, x, own, below, above)
    for x in range(3):
        wide[x, :, :24] = left[x].astype(F32).reshape(14, 24, C)
        wide[11 + x, :, :24] = right[x].astype(F32).reshape(14, 24, C)
    gather(wide, patches, 14, 7, 8)
    shares = turned[...]
    for i in range(3):
        weight_terms(shares, patches[i : i + 12].reshape(1152, 9 * C), sum_ref, 9 * i)


def volume_kernel(around, coarse_weights, slope, weights, out_ref, grads, spread, fine):
    for x in range(8):
        grads[x, :, :8] = around[64 * x : 64 * x + 64].astype(F32).reshape(8, 8, C)
    back = back_conv(grads, coarse_weights)
    spread[:, :, pl.ds(0, 8, 2)] = back
    spread[:, :, pl.ds(1, 8, 2)] = back
    for x in range(10):
        for y in range(10):
            fine[x, y] = spread[(x + 1) // 2, (y + 1) // 2] * slope[x + 1, y + 1, 4:20]
    total = jnp.zeros((512, C), F32)
    for i in range(3):
        cells = jnp.concatenate(
            [
                flat(fine[2 - i : 10 - i, 2 - j : 10 - j, 3 - k : 11 - k])
                for j in range(3)
                for k in range(3)
            ],
            axis=1,
        )
        turned = jnp.concatenate([weights[9 * i + t] for t in range(9)], axis=1)
        total = total + lax.dot_general(
            cells, turned, (((1,), (1,)), ((), ())), preferred_element_type=F32
        )
    out_ref[...] = total.astype(BF16)


def call(kernel, outs, inputs, scratch=(), scalars=0, flops=0):
    in_specs = [
        pl.BlockSpec(memory_space=pltpu.SMEM if n < scalars else pltpu.VMEM)
        for n in range(len(inputs))
    ]
    moved = sum(a.size * a.dtype.itemsize for a in inputs)
    moved += sum(math.prod(s) * jnp.dtype(t).itemsize for s, t in outs)
    return pl.pallas_call(
        kernel,
        out_shape=[jax.ShapeDtypeStruct(s, t) for s, t in outs],
        in_specs=in_specs,
        out_specs=[pl.BlockSpec(memory_space=pltpu.VMEM) for _ in outs],
        scratch_shapes=[pltpu.VMEM(s, t) for s, t in scratch],
        compiler_params=pltpu.CompilerParams(vmem_limit_bytes=40 * 1024 * 1024),
        cost_estimate=pl.CostEstimate(flops=flops, bytes_accessed=moved, transcendentals=0),
    )(*inputs)


def line(count, step):
    return [(i, i + step) for i in range(count) if 0 <= i + step < count]


def beside(last, leading, axis, count):
    before = lax.ppermute(last, axis, line(count, 1))
    after = lax.ppermute(leading, axis, line(count, -1))
    return before, after


def along_width(x, count):
    outer = lax.ppermute(x, WIDTH, [(i, i - 1 + 2 * (i % 2)) for i in range(1, count - 1)])
    inner = lax.ppermute(x, WIDTH, [(i, i ^ 1) for i in range(count)])
    return outer, inner


def in_order(outer, inner):
    first = lax.axis_index("core") == 0
    return jnp.where(first, outer, inner), jnp.where(first, inner, outer)


def spread_rows(terms, axes, peers):
    rows = terms.shape[0]
    parts = terms.astype(BF16).reshape(peers, rows // peers, C)
    return lax.all_to_all(parts, axes, 0, 0, tiled=True)


def gathered_rows(part, axes, peers):
    rows = part.shape[0]
    parts = jnp.broadcast_to(part[None], (peers, rows, C))
    return lax.all_to_all(parts, axes, 0, 0, tiled=True)


def summed(parts):
    return jnp.sum(parts.astype(F32), axis=0)


def joined(parts):
    return parts.reshape(-1, C)


def local(volume, fine_weight, coarse_weight, cotangent):
    sizes = {axis: lax.axis_size(axis) for axis in AXES}
    plane, along = (sizes["gx"] * sizes["y"], sizes["gy"] * sizes["zh"])
    peers = [sizes["gx"], sizes["gy"], sizes["y"] * sizes["zh"] * 2]
    place = [lax.axis_index("gx"), lax.axis_index("gy"), lax.axis_index(WIDTH)]
    place = jnp.stack([p.astype(jnp.int32) for p in place])
    fine_sizes = [8 * n for n in peers]
    coarse_sizes = [4 * n for n in peers]

    fine_rows = fine_weight.reshape(27 * C, C)
    coarse_rows = coarse_weight.reshape(27 * C, C)

    packed = jnp.concatenate([volume.reshape(512, C), cotangent.reshape(64, C)], axis=0)
    before, after = in_order(*along_width(packed, peers[2]))
    own = jnp.concatenate(
        [before[:512].reshape(8, 8, 8, C), volume, after[:512].reshape(8, 8, 8, C)], axis=2
    )
    incoming = jnp.concatenate(
        [
            before[512:].reshape(4, 4, 4, C)[:, :, 2:],
            cotangent,
            after[512:].reshape(4, 4, 4, C)[:, :, :2],
        ],
        axis=2,
    ).astype(F32)
    below, above = beside(own[:, 5:], own[:, :3], "gy", peers[1])
    sides = [
        jnp.concatenate([below[at], own[at], above[at]], axis=1)
        for at in (slice(5, 8), slice(0, 3))
    ]
    left, right = beside(sides[0], sides[1], "gx", peers[0])
    across = [own.reshape(8, 192, C), below.reshape(8, 72, C), above.reshape(8, 72, C)]
    (inner,) = call(
        inner_kernel,
        [((6, 12, 24, C), F32)],
        across + [fine_rows],
        scratch=[((8, 14, 32, C), F32), ((8, 288, 9 * C), BF16)],
        flops=2 * 1728 * 27 * C * C,
    )
    across = across + [left.reshape(3, 336, C), right.reshape(3, 336, C)]
    coarse, coarse_grad, slope, pooled = call(
        lambda *refs: front_kernel(fine_sizes, coarse_sizes, *refs),
        [((128, C), F32), ((128, C), BF16), ((12, 12, 24, C), F32), ((6, 6, 16, C), F32)],
        [place, *across, fine_rows, coarse_rows, incoming.reshape(128, C), inner],
        scratch=[
            ((10, 14, 32, C), F32),
            ((10, 288, 9 * C), BF16),
            ((6, 12, 24, C), F32),
            ((6, 24, C), F32),
        ],
        scalars=1,
        flops=2 * 1900 * 27 * C * C,
    )

    grads = coarse_grad.reshape(4, 4, 8, C)
    halo = beside(grads[:, 2:], grads[:, :2], "gy", peers[1])
    turned, coarse_sum = call(
        share_kernel,
        [((C, 1152), BF16), ((27 * C, C), BF16)],
        [coarse_grad, pooled, coarse_weight, slope],
        scratch=[((8, 8, 16, C), F32), ((6, 6, 16, C), F32), ((12, 12, 8, C), F32)],
        flops=2 * 1000 * 27 * C * C,
    )
    halo, turned = lax.optimization_barrier((halo, turned))
    grads = jnp.concatenate([halo[0], grads, halo[1]], axis=1)
    halo = beside(grads[2:], grads[:2], "gx", peers[0])
    (fine_sum,) = call(
        fine_kernel,
        [((27 * C, C), BF16)],
        [*across, turned],
        scratch=[((14, 14, 32, C), F32), ((14, 96, 9 * C), BF16)],
        flops=2 * 1152 * 27 * C * C,
    )
    halo, fine_sum = lax.optimization_barrier((halo, fine_sum))
    around = jnp.concatenate([halo[0], grads, halo[1]], axis=0)

    first = lax.axis_index("core") == 0
    swap = [(0, 1), (1, 0)]
    cells_fine = fine_sizes[0] * fine_sizes[1] * fine_sizes[2]
    scale = jnp.where(first, 1.0 / math.sqrt(cells_fine), 1.0 / math.sqrt(cells_fine // 8))
    mine = jnp.where(first, fine_sum, coarse_sum).astype(F32)
    other = jnp.where(first, coarse_sum, fine_sum)
    mine = mine + lax.ppermute(other, "core", swap).astype(F32)

    parts = spread_rows(mine, PLANE, plane)
    (grad_volume,) = call(
        volume_kernel,
        [((512, C), BF16)],
        [around.reshape(512, C), coarse_weight, slope, fine_weight],
        scratch=[((8, 8, 16, C), F32), ((6, 6, 16, C), F32), ((10, 10, 16, C), F32)],
        flops=2 * 800 * 27 * C * C,
    )
    coarse_out = jax.nn.silu(coarse.reshape(4, 4, 8, C)[:, :, 2:6]).astype(BF16)
    parts, grad_volume, coarse_out = lax.optimization_barrier((parts, grad_volume, coarse_out))
    part = summed(parts)
    length = part.shape[0]
    padded = -(-length // (16 * along)) * 16 * along
    part = jnp.pad(part, ((0, padded - length), (0, 0)))
    part = (summed(spread_rows(part, LINE, along)) * scale).astype(BF16)
    part = joined(gathered_rows(part, LINE, along))[:length]
    mine = joined(gathered_rows(part, PLANE, plane))
    other = lax.ppermute(mine, "core", swap)
    fine_done = jnp.where(first, mine, other)
    coarse_done = jnp.where(first, other, mine)
    return (
        coarse_out,
        grad_volume.reshape(8, 8, 8, C),
        fine_done.reshape(27, C, C),
        coarse_done.reshape(27, C, C),
    )


def solution(mesh):
    shape = mesh.devices.shape
    inner = Mesh(mesh.devices.reshape(shape[0], shape[1], shape[2] // 4, 2, 2), AXES)
    cells = P("gx", "gy", WIDTH, None)
    return jax.shard_map(
        local,
        mesh=inner,
        in_specs=(cells, P(), P(), cells),
        out_specs=(cells, cells, P(), P()),
        check_vma=False,
    )
```

```python
import math

import jax
import jax.numpy as jnp
from jax import lax
from jax.experimental import pallas as pl
from jax.experimental.pallas import tpu as pltpu
from jax.sharding import Mesh, PartitionSpec as P

AXES = ("gx", "gy", "y", "zh", "core")
WIDTH = ("y", "zh", "core")
PLANE = ("gx", "y")
LINE = ("gy", "zh")
C = 128
F32 = jnp.float32
BF16 = jnp.bfloat16


def silu_slope(values):
    sigma = 1.0 / (1.0 + jnp.exp(-values))
    return sigma * (1.0 + values * (1.0 - sigma))


def inside(shape, starts, sizes):
    keep = None
    for dim in range(3):
        at = starts[dim] + lax.broadcasted_iota(jnp.int32, shape, dim)
        ok = (at >= 0) & (at < sizes[dim])
        keep = ok if keep is None else keep & ok
    return keep


def taps():
    return [(i, j, k) for i in range(3) for j in range(3) for k in range(3)]


def flat(values):
    return values.reshape(-1, C).astype(BF16)


def weight_terms(turned, cells, sum_ref, at):
    terms = jnp.dot(turned, cells, preferred_element_type=F32)
    for t in range(9):
        row = (at + t) * C
        sum_ref[row : row + C] = terms[:, t * C : (t + 1) * C].T.astype(BF16)


def back_conv(grads, weights):
    cells = jnp.concatenate(
        [flat(grads[2 - i : 8 - i, 2 - j : 8 - j, 2 - k : 10 - k]) for i, j, k in taps()], axis=1
    )
    turned = jnp.concatenate([weights[t] for t in range(27)], axis=1)
    back = lax.dot_general(cells, turned, (((1,), (1,)), ((), ())), preferred_element_type=F32)
    return back.reshape(6, 6, 8, C)


def gather(wide, patches, planes, start, length):
    def plane(x, carry):
        for k in range(3):
            line = wide[x, :, start + k : start + k + length]
            for j in range(3):
                at = (3 * j + k) * C
                patches[x, :, at : at + C] = flat(line[j : j + 12])
        return carry

    lax.fori_loop(0, planes, plane, 0)


def fine_conv(patches, weights, at, planes):
    rows = planes * 288
    total = jnp.zeros((rows, C), F32)
    for i in range(3):
        cells = patches[pl.ds(at + i, planes)].reshape(rows, 9 * C)
        total = total + jnp.dot(
            cells, weights[9 * C * i : 9 * C * (i + 1)], preferred_element_type=F32
        )
    return total.reshape(planes, 12, 24, C)


def fill(wide, at, x, own, below, above):
    wide[at, 3:11, :24] = own[x].astype(F32).reshape(8, 24, C)
    wide[at, :3, :24] = below[x].astype(F32).reshape(3, 24, C)
    wide[at, 11:, :24] = above[x].astype(F32).reshape(3, 24, C)


def inner_kernel(own, below, above, weights, hidden_ref, wide, patches):
    for x in range(8):
        fill(wide, x, x, own, below, above)
    gather(wide, patches, 8, 1, 24)
    for part in range(2):
        hidden_ref[3 * part : 3 * part + 3] = fine_conv(patches, weights, 3 * part, 3)


def front_kernel(
    fine_sizes, coarse_sizes, place, own, below, above, left, right, weights, coarse_weights, incoming, inner,
    coarse_ref, grad_ref, slope_ref, fine_ref, coarse_sum_ref,
    wide, patches, outer, pairs, pooled, grads, spread, shares, near,
):
    order = [0, 1, 2, 3, 4, 10, 11, 12, 13, 5, 6, 7, 8, 9]
    for x in range(3):
        wide[x, :, :24] = left[x].astype(F32).reshape(14, 24, C)
        wide[order[11 + x], :, :24] = right[x].astype(F32).reshape(14, 24, C)
    for x in range(8):
        fill(wide, order[3 + x], x, own, below, above)
    gather(wide, patches, 10, 1, 24)
    for part in range(2):
        outer[3 * part : 3 * part + 3] = fine_conv(patches, weights, 5 * part, 3)

    for x in range(6):
        active = None
        for at in (2 * x, 2 * x + 1):
            value = inner[at - 3] if 3 <= at < 9 else outer[at if at < 3 else at - 6]
            sigma = 1.0 / (1.0 + jnp.exp(-value))
            slope = sigma * (1.0 + value * (1.0 - sigma)) * 0.125
            starts = [8 * place[0] - 2 + at, 8 * place[1] - 2, 8 * place[2] - 6]
            keep = inside((1, 12, 24, C), starts, fine_sizes)[0]
            slope_ref[at] = jnp.where(keep, slope, 0.0)
            value = value * sigma
            active = value if active is None else active + value
        active = active.reshape(6, 2, 24, C)
        pairs[...] = active[:, 0] + active[:, 1]
        mean = (pairs[:, pl.ds(0, 12, 2)] + pairs[:, pl.ds(1, 12, 2)]) * 0.125
        starts = [4 * place[0] - 1 + x, 4 * place[1] - 1, 4 * place[2] - 3]
        keep = inside((1, 6, 12, C), starts, coarse_sizes)[0]
        pooled[x, :, :12] = jnp.where(keep, mean, 0.0)
        pooled[x, :, 12:] = jnp.zeros((6, 4, C), F32)

    cells = [flat(pooled[i : i + 4, j : j + 4, k : k + 8]) for i, j, k in taps()]
    coarse = jnp.dot(
        jnp.concatenate(cells, axis=1),
        coarse_weights[...].reshape(27 * C, C),
        preferred_element_type=F32,
    )
    coarse_ref[...] = coarse
    grad = (incoming[...] * silu_slope(coarse)).astype(BF16)
    grad_ref[...] = grad
    grad = grad.astype(F32)

    grads[...] = jnp.zeros((8, 8, 16, C), F32)
    grads[2:6, 2:6, :8] = grad.reshape(4, 4, 8, C)
    back = back_conv(grads, coarse_weights)
    spread[:, :, pl.ds(0, 8, 2)] = back
    spread[:, :, pl.ds(1, 8, 2)] = back
    for x in range(12):
        for y in range(12):
            shares[x, y] = spread[x // 2, y // 2, 2:10] * slope_ref[x, y, 6:14]
    turned = shares[...].reshape(1152, C).T.astype(BF16)
    for x in range(14):
        for k in range(3):
            line = wide[order[x], :, 7 + k : 15 + k]
            for j in range(3):
                at = (3 * j + k) * C
                near[x, :, at : at + C] = flat(line[j : j + 12])
    for i in range(3):
        weight_terms(turned, near[i : i + 12].reshape(1152, 9 * C), fine_ref, 9 * i)

    at = lax.broadcasted_iota(jnp.int32, (C, C), 0) % 8
    turned = jnp.where((at >= 2) & (at < 6), grad, 0.0).T.astype(BF16)
    for i in range(3):
        weight_terms(
            turned, jnp.concatenate(cells[9 * i : 9 * i + 9], axis=1), coarse_sum_ref, 9 * i
        )


def volume_kernel(around, coarse_weights, slope, weights, out_ref, grads, spread, fine):
    for x in range(8):
        grads[x, :, :8] = around[64 * x : 64 * x + 64].astype(F32).reshape(8, 8, C)
    back = back_conv(grads, coarse_weights)
    spread[:, :, pl.ds(0, 8, 2)] = back
    spread[:, :, pl.ds(1, 8, 2)] = back
    for x in range(10):
        for y in range(10):
            fine[x, y] = spread[(x + 1) // 2, (y + 1) // 2] * slope[x + 1, y + 1, 4:20]
    total = jnp.zeros((512, C), F32)
    for i in range(3):
        cells = jnp.concatenate(
            [
                flat(fine[2 - i : 10 - i, 2 - j : 10 - j, 3 - k : 11 - k])
                for j in range(3)
                for k in range(3)
            ],
            axis=1,
        )
        turned = jnp.concatenate([weights[9 * i + t] for t in range(9)], axis=1)
        total = total + lax.dot_general(
            cells, turned, (((1,), (1,)), ((), ())), preferred_element_type=F32
        )
    out_ref[...] = total.astype(BF16)


def call(kernel, outs, inputs, scratch=(), scalars=0, flops=0):
    in_specs = [
        pl.BlockSpec(memory_space=pltpu.SMEM if n < scalars else pltpu.VMEM)
        for n in range(len(inputs))
    ]
    moved = sum(a.size * a.dtype.itemsize for a in inputs)
    moved += sum(math.prod(s) * jnp.dtype(t).itemsize for s, t in outs)
    return pl.pallas_call(
        kernel,
        out_shape=[jax.ShapeDtypeStruct(s, t) for s, t in outs],
        in_specs=in_specs,
        out_specs=[pl.BlockSpec(memory_space=pltpu.VMEM) for _ in outs],
        scratch_shapes=[pltpu.VMEM(s, t) for s, t in scratch],
        compiler_params=pltpu.CompilerParams(vmem_limit_bytes=40 * 1024 * 1024),
        cost_estimate=pl.CostEstimate(flops=flops, bytes_accessed=moved, transcendentals=0),
    )(*inputs)


def line(count, step):
    return [(i, i + step) for i in range(count) if 0 <= i + step < count]


def beside(last, leading, axis, count):
    before = lax.ppermute(last, axis, line(count, 1))
    after = lax.ppermute(leading, axis, line(count, -1))
    return before, after


def along_width(x, count):
    outer = lax.ppermute(x, WIDTH, [(i, i - 1 + 2 * (i % 2)) for i in range(1, count - 1)])
    inner = lax.ppermute(x, WIDTH, [(i, i ^ 1) for i in range(count)])
    return outer, inner


def in_order(outer, inner):
    first = lax.axis_index("core") == 0
    return jnp.where(first, outer, inner), jnp.where(first, inner, outer)


def spread_rows(terms, axes, peers):
    rows = terms.shape[0]
    parts = terms.astype(BF16).reshape(peers, rows // peers, C)
    return lax.all_to_all(parts, axes, 0, 0, tiled=True)


def gathered_rows(part, axes, peers):
    rows = part.shape[0]
    parts = jnp.broadcast_to(part[None], (peers, rows, C))
    return lax.all_to_all(parts, axes, 0, 0, tiled=True)


def summed(parts):
    return jnp.sum(parts.astype(F32), axis=0)


def joined(parts):
    return parts.reshape(-1, C)


def local(volume, fine_weight, coarse_weight, cotangent):
    sizes = {axis: lax.axis_size(axis) for axis in AXES}
    plane, along = (sizes["gx"] * sizes["y"], sizes["gy"] * sizes["zh"])
    peers = [sizes["gx"], sizes["gy"], sizes["y"] * sizes["zh"] * 2]
    place = [lax.axis_index("gx"), lax.axis_index("gy"), lax.axis_index(WIDTH)]
    place = jnp.stack([p.astype(jnp.int32) for p in place])
    fine_sizes = [8 * n for n in peers]
    coarse_sizes = [4 * n for n in peers]

    fine_rows = fine_weight.reshape(27 * C, C)

    packed = jnp.concatenate([volume.reshape(512, C), cotangent.reshape(64, C)], axis=0)
    before, after = in_order(*along_width(packed, peers[2]))
    own = jnp.concatenate(
        [before[:512].reshape(8, 8, 8, C), volume, after[:512].reshape(8, 8, 8, C)], axis=2
    )
    incoming = jnp.concatenate(
        [
            before[512:].reshape(4, 4, 4, C)[:, :, 2:],
            cotangent,
            after[512:].reshape(4, 4, 4, C)[:, :, :2],
        ],
        axis=2,
    ).astype(F32)
    below, above = beside(own[:, 5:], own[:, :3], "gy", peers[1])
    sides = [
        jnp.concatenate([below[at], own[at], above[at]], axis=1)
        for at in (slice(5, 8), slice(0, 3))
    ]
    left, right = beside(sides[0], sides[1], "gx", peers[0])
    across = [own.reshape(8, 192, C), below.reshape(8, 72, C), above.reshape(8, 72, C)]
    (inner,) = call(
        inner_kernel,
        [((6, 12, 24, C), F32)],
        across + [fine_rows],
        scratch=[((8, 14, 32, C), F32), ((8, 288, 9 * C), BF16)],
        flops=2 * 1728 * 27 * C * C,
    )
    across = across + [left.reshape(3, 336, C), right.reshape(3, 336, C)]
    coarse, coarse_grad, slope, fine_sum, coarse_sum = call(
        lambda *refs: front_kernel(fine_sizes, coarse_sizes, *refs),
        [
            ((128, C), F32),
            ((128, C), BF16),
            ((12, 12, 24, C), F32),
            ((27 * C, C), BF16),
            ((27 * C, C), BF16),
        ],
        [place, *across, fine_rows, coarse_weight, incoming.reshape(128, C), inner],
        scratch=[
            ((14, 14, 32, C), F32),
            ((10, 288, 9 * C), BF16),
            ((6, 12, 24, C), F32),
            ((6, 24, C), F32),
            ((6, 6, 16, C), F32),
            ((8, 8, 16, C), F32),
            ((6, 6, 16, C), F32),
            ((12, 12, 8, C), F32),
            ((14, 96, 9 * C), BF16),
        ],
        scalars=1,
        flops=2 * 4000 * 27 * C * C,
    )

    first = lax.axis_index("core") == 0
    swap = [(0, 1), (1, 0)]
    cells_fine = fine_sizes[0] * fine_sizes[1] * fine_sizes[2]
    scale = jnp.where(first, 1.0 / math.sqrt(cells_fine), 1.0 / math.sqrt(cells_fine // 8))
    mine = jnp.where(first, fine_sum, coarse_sum).astype(F32)
    other = jnp.where(first, coarse_sum, fine_sum)
    mine = mine + lax.ppermute(other, "core", swap).astype(F32)

    grads = coarse_grad.reshape(4, 4, 8, C)
    halo = beside(grads[:, 2:], grads[:, :2], "gy", peers[1])
    coarse_out = jax.nn.silu(coarse.reshape(4, 4, 8, C)[:, :, 2:6]).astype(BF16)
    parts = spread_rows(mine, PLANE, plane)
    parts, halo, coarse_out = lax.optimization_barrier((parts, halo, coarse_out))
    part = summed(parts)
    length = part.shape[0]
    padded = -(-length // (16 * along)) * 16 * along
    part = jnp.pad(part, ((0, padded - length), (0, 0)))
    part = (summed(spread_rows(part, LINE, along)) * scale).astype(BF16)
    parts = gathered_rows(part, LINE, along)
    parts, halo = lax.optimization_barrier((parts, halo))
    part = joined(parts)[:length]
    grads = jnp.concatenate([halo[0], grads, halo[1]], axis=1)
    halo = beside(grads[2:], grads[:2], "gx", peers[0])
    around = jnp.concatenate([halo[0], grads, halo[1]], axis=0)
    (grad_volume,) = call(
        volume_kernel,
        [((512, C), BF16)],
        [around.reshape(512, C), coarse_weight, slope, fine_weight],
        scratch=[((8, 8, 16, C), F32), ((6, 6, 16, C), F32), ((10, 10, 16, C), F32)],
        flops=2 * 800 * 27 * C * C,
    )
    parts = gathered_rows(part, PLANE, plane)
    parts, grad_volume = lax.optimization_barrier((parts, grad_volume))
    mine = joined(parts)
    other = lax.ppermute(mine, "core", swap)
    fine_done = jnp.where(first, mine, other)
    coarse_done = jnp.where(first, other, mine)
    return (
        coarse_out,
        grad_volume.reshape(8, 8, 8, C),
        fine_done.reshape(27, C, C),
        coarse_done.reshape(27, C, C),
    )


def solution(mesh):
    shape = mesh.devices.shape
    inner = Mesh(mesh.devices.reshape(shape[0], shape[1], shape[2] // 4, 2, 2), AXES)
    cells = P("gx", "gy", WIDTH, None)
    return jax.shard_map(
        local,
        mesh=inner,
        in_specs=(cells, P(), P(), cells),
        out_specs=(cells, cells, P(), P()),
        check_vma=False,
    )
```

```python
import math

import jax
import jax.numpy as jnp
from jax import lax
from jax.experimental import pallas as pl
from jax.experimental.pallas import tpu as pltpu
from jax.sharding import Mesh, PartitionSpec as P

AXES = ("gx", "gy", "y", "zh", "core")
WIDTH = ("y", "zh", "core")
PLANE = ("gx", "y")
LINE = ("gy", "zh")
C = 128
F32 = jnp.float32
BF16 = jnp.bfloat16


def silu_slope(values):
    sigma = 1.0 / (1.0 + jnp.exp(-values))
    return sigma * (1.0 + values * (1.0 - sigma))


def inside(shape, starts, sizes):
    keep = None
    for dim in range(3):
        at = starts[dim] + lax.broadcasted_iota(jnp.int32, shape, dim)
        ok = (at >= 0) & (at < sizes[dim])
        keep = ok if keep is None else keep & ok
    return keep


def taps():
    return [(i, j, k) for i in range(3) for j in range(3) for k in range(3)]


def flat(values):
    return values.reshape(-1, C).astype(BF16)


def weight_terms(turned, cells, sum_ref, at):
    terms = jnp.dot(turned, cells, preferred_element_type=F32)
    for t in range(9):
        row = (at + t) * C
        sum_ref[row : row + C] = terms[:, t * C : (t + 1) * C].T.astype(BF16)


def back_conv(grads, weights):
    cells = jnp.concatenate(
        [flat(grads[2 - i : 8 - i, 2 - j : 8 - j, 2 - k : 10 - k]) for i, j, k in taps()], axis=1
    )
    turned = jnp.concatenate([weights[t] for t in range(27)], axis=1)
    back = lax.dot_general(cells, turned, (((1,), (1,)), ((), ())), preferred_element_type=F32)
    return back.reshape(6, 6, 8, C)


def gather(wide, patches, planes, columns=12):
    def plane(x, carry):
        for k in range(3):
            line = wide[x, :, 1 + k : 25 + k]
            for j in range(3):
                at = (3 * j + k) * C
                patches[x, :, at : at + C] = flat(line[j : j + columns])
        return carry

    lax.fori_loop(0, planes, plane, 0)


def fine_conv(patches, weights, at, planes, columns=12):
    rows = planes * columns * 24
    total = jnp.zeros((rows, C), F32)
    for i in range(3):
        cells = patches[pl.ds(at + i, planes)].reshape(rows, 9 * C)
        total = total + jnp.dot(
            cells, weights[9 * C * i : 9 * C * (i + 1)], preferred_element_type=F32
        )
    return total.reshape(planes, columns, 24, C)


def fill(wide, at, x, own, below, above):
    wide[at, 3:11, :24] = own[x].astype(F32).reshape(8, 24, C)
    wide[at, :3, :24] = below[x].astype(F32).reshape(3, 24, C)
    wide[at, 11:, :24] = above[x].astype(F32).reshape(3, 24, C)


def middle_kernel(own, weights, hidden_ref, wide, patches):
    for x in range(8):
        wide[x, :, :24] = own[x].astype(F32).reshape(8, 24, C)
    gather(wide, patches, 8, 6)
    hidden_ref[...] = fine_conv(patches, weights, 0, 6, 6)


def sides_kernel(own, below, above, weights, hidden_ref, wide, patches):
    for x in range(8):
        rows = own[x].astype(F32).reshape(8, 24, C)
        wide[x, :3, :24] = below[x].astype(F32).reshape(3, 24, C)
        wide[x, 3:5, :24] = rows[:2]
        wide[x, 5:7, :24] = rows[6:]
        wide[x, 7:, :24] = above[x].astype(F32).reshape(3, 24, C)

    def plane(x, carry):
        for k in range(3):
            line = wide[x, :, 1 + k : 25 + k]
            for j in range(3):
                at = (3 * j + k) * C
                cells = jnp.concatenate([line[j : j + 3], line[5 + j : 8 + j]], axis=0)
                patches[x, :, at : at + C] = flat(cells)
        return carry

    lax.fori_loop(0, 8, plane, 0)
    hidden_ref[...] = fine_conv(patches, weights, 0, 6, 6)


def front_kernel(
    fine_sizes, coarse_sizes, place, own, below, above, left, right, weights, coarse_weights, incoming,
    middle, sides,
    coarse_ref, grad_ref, slope_ref, fine_ref, coarse_sum_ref,
    wide, patches, outer, pairs, pooled, grads, spread, shares, near,
):
    order = [0, 1, 2, 3, 4, 10, 11, 12, 13, 5, 6, 7, 8, 9]
    for x in range(3):
        wide[x, :, :24] = left[x].astype(F32).reshape(14, 24, C)
        wide[order[11 + x], :, :24] = right[x].astype(F32).reshape(14, 24, C)
    for x in range(8):
        fill(wide, order[3 + x], x, own, below, above)
    gather(wide, patches, 10)
    for part in range(2):
        outer[3 * part : 3 * part + 3] = fine_conv(patches, weights, 5 * part, 3)

    for x in range(6):
        active = None
        for at in (2 * x, 2 * x + 1):
            if 3 <= at < 9:
                edges = sides[at - 3]
                value = jnp.concatenate([edges[:3], middle[at - 3], edges[3:]], axis=0)
            else:
                value = outer[at if at < 3 else at - 6]
            sigma = 1.0 / (1.0 + jnp.exp(-value))
            slope = sigma * (1.0 + value * (1.0 - sigma)) * 0.125
            starts = [8 * place[0] - 2 + at, 8 * place[1] - 2, 8 * place[2] - 6]
            keep = inside((1, 12, 24, C), starts, fine_sizes)[0]
            slope_ref[at] = jnp.where(keep, slope, 0.0)
            value = value * sigma
            active = value if active is None else active + value
        active = active.reshape(6, 2, 24, C)
        pairs[...] = active[:, 0] + active[:, 1]
        mean = (pairs[:, pl.ds(0, 12, 2)] + pairs[:, pl.ds(1, 12, 2)]) * 0.125
        starts = [4 * place[0] - 1 + x, 4 * place[1] - 1, 4 * place[2] - 3]
        keep = inside((1, 6, 12, C), starts, coarse_sizes)[0]
        pooled[x, :, :12] = jnp.where(keep, mean, 0.0)
        pooled[x, :, 12:] = jnp.zeros((6, 4, C), F32)

    cells = [flat(pooled[i : i + 4, j : j + 4, k : k + 8]) for i, j, k in taps()]
    coarse = jnp.dot(
        jnp.concatenate(cells, axis=1),
        coarse_weights[...].reshape(27 * C, C),
        preferred_element_type=F32,
    )
    coarse_ref[...] = coarse
    grad = (incoming[...] * silu_slope(coarse)).astype(BF16)
    grad_ref[...] = grad
    grad = grad.astype(F32)

    grads[...] = jnp.zeros((8, 8, 16, C), F32)
    grads[2:6, 2:6, :8] = grad.reshape(4, 4, 8, C)
    back = back_conv(grads, coarse_weights)
    spread[:, :, pl.ds(0, 8, 2)] = back
    spread[:, :, pl.ds(1, 8, 2)] = back
    for x in range(12):
        for y in range(12):
            shares[x, y] = spread[x // 2, y // 2, 2:10] * slope_ref[x, y, 6:14]
    turned = shares[...].reshape(1152, C).T.astype(BF16)
    for x in range(14):
        for k in range(3):
            line = wide[order[x], :, 7 + k : 15 + k]
            for j in range(3):
                at = (3 * j + k) * C
                near[x, :, at : at + C] = flat(line[j : j + 12])
    for i in range(3):
        weight_terms(turned, near[i : i + 12].reshape(1152, 9 * C), fine_ref, 9 * i)

    at = lax.broadcasted_iota(jnp.int32, (C, C), 0) % 8
    turned = jnp.where((at >= 2) & (at < 6), grad, 0.0).T.astype(BF16)
    for i in range(3):
        weight_terms(
            turned, jnp.concatenate(cells[9 * i : 9 * i + 9], axis=1), coarse_sum_ref, 9 * i
        )


def volume_kernel(around, coarse_weights, slope, weights, out_ref, grads, spread, fine):
    for x in range(8):
        grads[x, :, :8] = around[64 * x : 64 * x + 64].astype(F32).reshape(8, 8, C)
    back = back_conv(grads, coarse_weights)
    spread[:, :, pl.ds(0, 8, 2)] = back
    spread[:, :, pl.ds(1, 8, 2)] = back
    for x in range(10):
        for y in range(10):
            fine[x, y] = spread[(x + 1) // 2, (y + 1) // 2] * slope[x + 1, y + 1, 4:20]
    total = jnp.zeros((512, C), F32)
    for i in range(3):
        cells = jnp.concatenate(
            [
                flat(fine[2 - i : 10 - i, 2 - j : 10 - j, 3 - k : 11 - k])
                for j in range(3)
                for k in range(3)
            ],
            axis=1,
        )
        turned = jnp.concatenate([weights[9 * i + t] for t in range(9)], axis=1)
        total = total + lax.dot_general(
            cells, turned, (((1,), (1,)), ((), ())), preferred_element_type=F32
        )
    out_ref[...] = total.astype(BF16)


def plane_sum_kernel(parts, out_ref):
    total = parts[0].astype(F32)
    for at in range(1, parts.shape[0]):
        total = total + parts[at].astype(F32)
    rows = out_ref.shape[0] - total.shape[0]
    out_ref[...] = jnp.concatenate([total, jnp.zeros((rows, C), F32)], axis=0).astype(BF16)


def line_sum_kernel(scale, parts, out_ref):
    total = parts[0].astype(F32)
    for at in range(1, parts.shape[0]):
        total = total + parts[at].astype(F32)
    total = (total * scale[0]).astype(BF16)
    for at in range(out_ref.shape[0]):
        out_ref[at] = total


def keep_kernel(core, mine, fine_ref, coarse_ref, done):
    for at, ref in ((0, fine_ref), (1, coarse_ref)):

        @pl.when(core[0] == at)
        def _(ref=ref):
            copy = pltpu.make_async_copy(mine, ref, done)
            copy.start()
            copy.wait()


def take_kernel(core, other, fine_in, coarse_in, fine_ref, coarse_ref, done):
    for at, ref in ((1, fine_ref), (0, coarse_ref)):

        @pl.when(core[0] == at)
        def _(ref=ref):
            copy = pltpu.make_async_copy(other, ref, done)
            copy.start()
            copy.wait()


def copies(kernel, inputs, aliases):
    shape = jax.ShapeDtypeStruct((27 * C, C), BF16)
    return pl.pallas_call(
        kernel,
        out_shape=[shape, shape],
        in_specs=[pl.BlockSpec(memory_space=pltpu.SMEM)]
        + [pl.BlockSpec(memory_space=pl.ANY) for _ in inputs[1:]],
        out_specs=[pl.BlockSpec(memory_space=pl.ANY) for _ in range(2)],
        scratch_shapes=[pltpu.SemaphoreType.DMA],
        input_output_aliases=aliases,
        cost_estimate=pl.CostEstimate(flops=0, bytes_accessed=2 * 27 * C * C * 2, transcendentals=0),
    )(*inputs)


def call(kernel, outs, inputs, scratch=(), scalars=0, flops=0):
    in_specs = [
        pl.BlockSpec(memory_space=pltpu.SMEM if n < scalars else pltpu.VMEM)
        for n in range(len(inputs))
    ]
    moved = sum(a.size * a.dtype.itemsize for a in inputs)
    moved += sum(math.prod(s) * jnp.dtype(t).itemsize for s, t in outs)
    return pl.pallas_call(
        kernel,
        out_shape=[jax.ShapeDtypeStruct(s, t) for s, t in outs],
        in_specs=in_specs,
        out_specs=[pl.BlockSpec(memory_space=pltpu.VMEM) for _ in outs],
        scratch_shapes=[pltpu.VMEM(s, t) for s, t in scratch],
        compiler_params=pltpu.CompilerParams(vmem_limit_bytes=40 * 1024 * 1024),
        cost_estimate=pl.CostEstimate(flops=flops, bytes_accessed=moved, transcendentals=0),
    )(*inputs)


def line(count, step):
    return [(i, i + step) for i in range(count) if 0 <= i + step < count]


def beside(last, leading, axis, count):
    before = lax.ppermute(last, axis, line(count, 1))
    after = lax.ppermute(leading, axis, line(count, -1))
    return before, after


def along_width(x, count):
    outer = lax.ppermute(x, WIDTH, [(i, i - 1 + 2 * (i % 2)) for i in range(1, count - 1)])
    inner = lax.ppermute(x, WIDTH, [(i, i ^ 1) for i in range(count)])
    return outer, inner


def in_order(outer, inner):
    first = lax.axis_index("core") == 0
    return jnp.where(first, outer, inner), jnp.where(first, inner, outer)


def exchanged(parts, axes):
    return lax.all_to_all(parts, axes, 0, 0, tiled=True)


def joined(parts):
    return parts.reshape(-1, C)


def local(volume, fine_weight, coarse_weight, cotangent):
    sizes = {axis: lax.axis_size(axis) for axis in AXES}
    plane, along = (sizes["gx"] * sizes["y"], sizes["gy"] * sizes["zh"])
    peers = [sizes["gx"], sizes["gy"], sizes["y"] * sizes["zh"] * 2]
    place = [lax.axis_index(axis) for axis in ("gx", "gy", WIDTH, "core")]
    place = jnp.stack([p.astype(jnp.int32) for p in place])
    fine_sizes = [8 * n for n in peers]
    coarse_sizes = [4 * n for n in peers]

    fine_rows = fine_weight.reshape(27 * C, C)

    packed = jnp.concatenate([volume.reshape(512, C), cotangent.reshape(64, C)], axis=0)
    before, after = in_order(*along_width(packed, peers[2]))
    before_cells, after_cells = (b[:512].reshape(8, 8, 8, C) for b in (before, after))
    slabs = [
        jnp.concatenate([before_cells[:, at], volume[:, at], after_cells[:, at]], axis=2)
        for at in (slice(5, 8), slice(0, 3))
    ]
    below, above = beside(slabs[0], slabs[1], "gy", peers[1])
    own = jnp.concatenate([before_cells, volume, after_cells], axis=2)
    incoming = jnp.concatenate(
        [
            before[512:].reshape(4, 4, 4, C)[:, :, 2:],
            cotangent,
            after[512:].reshape(4, 4, 4, C)[:, :, :2],
        ],
        axis=2,
    ).astype(F32)
    sides = [
        jnp.concatenate([below[at], own[at], above[at]], axis=1)
        for at in (slice(5, 8), slice(0, 3))
    ]
    left, right = beside(sides[0], sides[1], "gx", peers[0])
    (middle,) = call(
        middle_kernel,
        [((6, 6, 24, C), F32)],
        [own.reshape(8, 192, C), fine_rows],
        scratch=[((8, 8, 32, C), F32), ((8, 144, 9 * C), BF16)],
        flops=2 * 864 * 27 * C * C,
    )
    across = [own.reshape(8, 192, C), below.reshape(8, 72, C), above.reshape(8, 72, C)]
    (edges,) = call(
        sides_kernel,
        [((6, 6, 24, C), F32)],
        across + [fine_rows],
        scratch=[((8, 10, 32, C), F32), ((8, 144, 9 * C), BF16)],
        flops=2 * 864 * 27 * C * C,
    )
    across = across + [left.reshape(3, 336, C), right.reshape(3, 336, C)]
    coarse, coarse_grad, slope, fine_sum, coarse_sum = call(
        lambda *refs: front_kernel(fine_sizes, coarse_sizes, *refs),
        [
            ((128, C), F32),
            ((128, C), BF16),
            ((12, 12, 24, C), F32),
            ((27 * C, C), BF16),
            ((27 * C, C), BF16),
        ],
        [place, *across, fine_rows, coarse_weight, incoming.reshape(128, C), middle, edges],
        scratch=[
            ((14, 14, 32, C), F32),
            ((10, 288, 9 * C), BF16),
            ((6, 12, 24, C), F32),
            ((6, 24, C), F32),
            ((6, 6, 16, C), F32),
            ((8, 8, 16, C), F32),
            ((6, 6, 16, C), F32),
            ((12, 12, 8, C), F32),
            ((14, 96, 9 * C), BF16),
        ],
        scalars=1,
        flops=2 * 4000 * 27 * C * C,
    )

    first = lax.axis_index("core") == 0
    swap = [(0, 1), (1, 0)]
    cells_fine = fine_sizes[0] * fine_sizes[1] * fine_sizes[2]
    scale = jnp.where(first, 1.0 / math.sqrt(cells_fine), 1.0 / math.sqrt(cells_fine // 8))
    scale = scale.astype(F32).reshape(1)
    mine = jnp.where(first, fine_sum, coarse_sum).astype(F32)
    other = jnp.where(first, coarse_sum, fine_sum)
    mine = mine + lax.ppermute(other, "core", swap).astype(F32)

    grads = coarse_grad.reshape(4, 4, 8, C)
    halo = beside(grads[:, 2:], grads[:, :2], "gy", peers[1])
    coarse_out = jax.nn.silu(coarse.reshape(4, 4, 8, C)[:, :, 2:6]).astype(BF16)
    parts = exchanged(mine.astype(BF16).reshape(plane, -1, C), PLANE)
    parts, halo, coarse_out = lax.optimization_barrier((parts, halo, coarse_out))
    length = parts.shape[1]
    padded = -(-length // (16 * along)) * 16 * along
    (part,) = call(plane_sum_kernel, [((padded, C), BF16)], [parts])
    parts = exchanged(part.reshape(along, padded // along, C), LINE)
    (parts,) = call(line_sum_kernel, [(parts.shape, BF16)], [scale, parts], scalars=1)
    parts = exchanged(parts, LINE)
    parts, halo = lax.optimization_barrier((parts, halo))
    part = joined(parts)[:length]
    grads = jnp.concatenate([halo[0], grads, halo[1]], axis=1)
    halo = beside(grads[2:], grads[:2], "gx", peers[0])
    around = jnp.concatenate([halo[0], grads, halo[1]], axis=0)
    (grad_volume,) = call(
        volume_kernel,
        [((512, C), BF16)],
        [around.reshape(512, C), coarse_weight, slope, fine_weight],
        scratch=[((8, 8, 16, C), F32), ((6, 6, 16, C), F32), ((10, 10, 16, C), F32)],
        flops=2 * 800 * 27 * C * C,
    )
    parts = exchanged(jnp.broadcast_to(part[None], (plane, length, C)), PLANE)
    parts, grad_volume = lax.optimization_barrier((parts, grad_volume))
    mine = joined(parts)
    other = lax.ppermute(mine, "core", swap)
    core = place[3:]
    fine_done, coarse_done = copies(keep_kernel, [core, mine], {})
    fine_done, coarse_done = copies(
        take_kernel, [core, other, fine_done, coarse_done], {2: 0, 3: 1}
    )
    return (
        coarse_out,
        grad_volume.reshape(8, 8, 8, C),
        fine_done.reshape(27, C, C),
        coarse_done.reshape(27, C, C),
    )


def solution(mesh):
    shape = mesh.devices.shape
    inner = Mesh(mesh.devices.reshape(shape[0], shape[1], shape[2] // 4, 2, 2), AXES)
    cells = P("gx", "gy", WIDTH, None)
    return jax.shard_map(
        local,
        mesh=inner,
        in_specs=(cells, P(), P(), cells),
        out_specs=(cells, cells, P(), P()),
        check_vma=False,
    )
```

```python
import math

import jax
import jax.numpy as jnp
from jax import lax
from jax.experimental import pallas as pl
from jax.experimental.pallas import tpu as pltpu
from jax.sharding import Mesh, PartitionSpec as P

AXES = ("gx", "gy", "y", "zh", "core")
WIDTH = ("y", "zh", "core")
PLANE = ("gx", "y")
LINE = ("gy", "zh")
C = 128
F32 = jnp.float32
BF16 = jnp.bfloat16


def silu_slope(values):
    sigma = 1.0 / (1.0 + jnp.exp(-values))
    return sigma * (1.0 + values * (1.0 - sigma))


def inside(shape, starts, sizes):
    keep = None
    for dim in range(3):
        at = starts[dim] + lax.broadcasted_iota(jnp.int32, shape, dim)
        ok = (at >= 0) & (at < sizes[dim])
        keep = ok if keep is None else keep & ok
    return keep


def taps():
    return [(i, j, k) for i in range(3) for j in range(3) for k in range(3)]


def flat(values):
    return values.reshape(-1, C).astype(BF16)


def weight_terms(turned, cells, sum_ref, at):
    terms = jnp.dot(turned, cells, preferred_element_type=F32)
    for t in range(9):
        row = (at + t) * C
        sum_ref[row : row + C] = terms[:, t * C : (t + 1) * C].T.astype(BF16)


def back_conv(grads, weights):
    cells = jnp.concatenate(
        [flat(grads[2 - i : 8 - i, 2 - j : 8 - j, 2 - k : 10 - k]) for i, j, k in taps()], axis=1
    )
    turned = jnp.concatenate([weights[t] for t in range(27)], axis=1)
    back = lax.dot_general(cells, turned, (((1,), (1,)), ((), ())), preferred_element_type=F32)
    return back.reshape(6, 6, 8, C)


def gather(wide, patches, planes, columns=12):
    def plane(x, carry):
        for k in range(3):
            line = wide[x, :, 1 + k : 25 + k]
            for j in range(3):
                at = (3 * j + k) * C
                patches[x, :, at : at + C] = flat(line[j : j + columns])
        return carry

    lax.fori_loop(0, planes, plane, 0)


def fine_conv(patches, weights, at, planes, columns=12):
    rows = planes * columns * 24
    total = jnp.zeros((rows, C), F32)
    for i in range(3):
        cells = patches[pl.ds(at + i, planes)].reshape(rows, 9 * C)
        total = total + jnp.dot(
            cells, weights[9 * C * i : 9 * C * (i + 1)], preferred_element_type=F32
        )
    return total.reshape(planes, columns, 24, C)


def fill(wide, at, x, own, below, above):
    wide[at, 3:11, :24] = own[x].astype(F32).reshape(8, 24, C)
    wide[at, :3, :24] = below[x].astype(F32).reshape(3, 24, C)
    wide[at, 11:, :24] = above[x].astype(F32).reshape(3, 24, C)


def middle_kernel(own, weights, hidden_ref, wide, patches):
    for x in range(8):
        wide[x, :, :24] = own[x].astype(F32).reshape(8, 24, C)
    gather(wide, patches, 8, 6)
    hidden_ref[...] = fine_conv(patches, weights, 0, 6, 6)


def sides_kernel(own, below, above, weights, hidden_ref, wide, patches):
    for x in range(8):
        rows = own[x].astype(F32).reshape(8, 24, C)
        wide[x, :3, :24] = below[x].astype(F32).reshape(3, 24, C)
        wide[x, 3:5, :24] = rows[:2]
        wide[x, 5:7, :24] = rows[6:]
        wide[x, 7:, :24] = above[x].astype(F32).reshape(3, 24, C)

    def plane(x, carry):
        for k in range(3):
            line = wide[x, :, 1 + k : 25 + k]
            for j in range(3):
                at = (3 * j + k) * C
                cells = jnp.concatenate([line[j : j + 3], line[5 + j : 8 + j]], axis=0)
                patches[x, :, at : at + C] = flat(cells)
        return carry

    lax.fori_loop(0, 8, plane, 0)
    hidden_ref[...] = fine_conv(patches, weights, 0, 6, 6)


def front_kernel(
    fine_sizes, coarse_sizes, place, own, below, above, left, right, weights, coarse_weights, incoming,
    middle, sides,
    coarse_ref, grad_ref, slope_ref, fine_ref, coarse_sum_ref,
    wide, patches, outer, pairs, pooled, grads, spread, shares, near,
):
    order = [0, 1, 2, 3, 4, 10, 11, 12, 13, 5, 6, 7, 8, 9]
    for x in range(3):
        wide[x, :, :24] = left[x].astype(F32).reshape(14, 24, C)
        wide[order[11 + x], :, :24] = right[x].astype(F32).reshape(14, 24, C)
    for x in range(8):
        fill(wide, order[3 + x], x, own, below, above)
    gather(wide, patches, 10)
    for part in range(2):
        outer[3 * part : 3 * part + 3] = fine_conv(patches, weights, 5 * part, 3)

    for x in range(6):
        active = None
        for at in (2 * x, 2 * x + 1):
            if 3 <= at < 9:
                edges = sides[at - 3]
                value = jnp.concatenate([edges[:3], middle[at - 3], edges[3:]], axis=0)
            else:
                value = outer[at if at < 3 else at - 6]
            sigma = 1.0 / (1.0 + jnp.exp(-value))
            slope = sigma * (1.0 + value * (1.0 - sigma)) * 0.125
            starts = [8 * place[0] - 2 + at, 8 * place[1] - 2, 8 * place[2] - 6]
            keep = inside((1, 12, 24, C), starts, fine_sizes)[0]
            slope_ref[at] = jnp.where(keep, slope, 0.0)
            value = value * sigma
            active = value if active is None else active + value
        active = active.reshape(6, 2, 24, C)
        pairs[...] = active[:, 0] + active[:, 1]
        mean = (pairs[:, pl.ds(0, 12, 2)] + pairs[:, pl.ds(1, 12, 2)]) * 0.125
        starts = [4 * place[0] - 1 + x, 4 * place[1] - 1, 4 * place[2] - 3]
        keep = inside((1, 6, 12, C), starts, coarse_sizes)[0]
        pooled[x, :, :12] = jnp.where(keep, mean, 0.0)
        pooled[x, :, 12:] = jnp.zeros((6, 4, C), F32)

    cells = [flat(pooled[i : i + 4, j : j + 4, k : k + 8]) for i, j, k in taps()]
    coarse = jnp.dot(
        jnp.concatenate(cells, axis=1),
        coarse_weights[...].reshape(27 * C, C),
        preferred_element_type=F32,
    )
    coarse_ref[...] = coarse
    grad = (incoming[...] * silu_slope(coarse)).astype(BF16)
    grad_ref[...] = grad
    grad = grad.astype(F32)

    grads[...] = jnp.zeros((8, 8, 16, C), F32)
    grads[2:6, 2:6, :8] = grad.reshape(4, 4, 8, C)
    back = back_conv(grads, coarse_weights)
    spread[:, :, pl.ds(0, 8, 2)] = back
    spread[:, :, pl.ds(1, 8, 2)] = back
    for x in range(12):
        for y in range(12):
            shares[x, y] = spread[x // 2, y // 2, 2:10] * slope_ref[x, y, 6:14]
    turned = shares[...].reshape(1152, C).T.astype(BF16)
    for x in range(14):
        for k in range(3):
            line = wide[order[x], :, 7 + k : 15 + k]
            for j in range(3):
                at = (3 * j + k) * C
                near[x, :, at : at + C] = flat(line[j : j + 12])
    for i in range(3):
        weight_terms(turned, near[i : i + 12].reshape(1152, 9 * C), fine_ref, 9 * i)

    at = lax.broadcasted_iota(jnp.int32, (C, C), 0) % 8
    turned = jnp.where((at >= 2) & (at < 6), grad, 0.0).T.astype(BF16)
    for i in range(3):
        weight_terms(
            turned, jnp.concatenate(cells[9 * i : 9 * i + 9], axis=1), coarse_sum_ref, 9 * i
        )


def volume_kernel(around, coarse_weights, slope, weights, out_ref, grads, spread, fine):
    for x in range(8):
        grads[x, :, :8] = around[64 * x : 64 * x + 64].astype(F32).reshape(8, 8, C)
    back = back_conv(grads, coarse_weights)
    spread[:, :, pl.ds(0, 8, 2)] = back
    spread[:, :, pl.ds(1, 8, 2)] = back
    for x in range(10):
        for y in range(10):
            fine[x, y] = spread[(x + 1) // 2, (y + 1) // 2] * slope[x + 1, y + 1, 4:20]
    total = jnp.zeros((512, C), F32)
    for i in range(3):
        cells = jnp.concatenate(
            [
                flat(fine[2 - i : 10 - i, 2 - j : 10 - j, 3 - k : 11 - k])
                for j in range(3)
                for k in range(3)
            ],
            axis=1,
        )
        turned = jnp.concatenate([weights[9 * i + t] for t in range(9)], axis=1)
        total = total + lax.dot_general(
            cells, turned, (((1,), (1,)), ((), ())), preferred_element_type=F32
        )
    out_ref[...] = total.astype(BF16)


def plane_sum_kernel(parts, out_ref):
    total = parts[0].astype(F32)
    for at in range(1, parts.shape[0]):
        total = total + parts[at].astype(F32)
    rows = out_ref.shape[0] - total.shape[0]
    out_ref[...] = jnp.concatenate([total, jnp.zeros((rows, C), F32)], axis=0).astype(BF16)


def line_sum_kernel(scale, parts, out_ref):
    total = parts[0].astype(F32)
    for at in range(1, parts.shape[0]):
        total = total + parts[at].astype(F32)
    total = (total * scale[0]).astype(BF16)
    for at in range(out_ref.shape[0]):
        out_ref[at] = total


def place_kernel(core, mine, other, fine_ref, coarse_ref, done):
    for at, first, second in ((0, fine_ref, coarse_ref), (1, coarse_ref, fine_ref)):

        @pl.when(core[0] == at)
        def _(first=first, second=second):
            moves = [
                pltpu.make_async_copy(mine, first, done.at[0]),
                pltpu.make_async_copy(other, second, done.at[1]),
            ]
            for move in moves:
                move.start()
            for move in moves:
                move.wait()


def placed(core, mine, other):
    shape = jax.ShapeDtypeStruct((27 * C, C), BF16)
    return pl.pallas_call(
        place_kernel,
        out_shape=[shape, shape],
        in_specs=[
            pl.BlockSpec(memory_space=pltpu.SMEM),
            pl.BlockSpec(memory_space=pltpu.VMEM),
            pl.BlockSpec(memory_space=pltpu.VMEM),
        ],
        out_specs=[pl.BlockSpec(memory_space=pl.ANY) for _ in range(2)],
        scratch_shapes=[pltpu.SemaphoreType.DMA((2,))],
        cost_estimate=pl.CostEstimate(flops=0, bytes_accessed=4 * 27 * C * C * 2, transcendentals=0),
    )(core, mine, other)


def call(kernel, outs, inputs, scratch=(), scalars=0, flops=0):
    in_specs = [
        pl.BlockSpec(memory_space=pltpu.SMEM if n < scalars else pltpu.VMEM)
        for n in range(len(inputs))
    ]
    moved = sum(a.size * a.dtype.itemsize for a in inputs)
    moved += sum(math.prod(s) * jnp.dtype(t).itemsize for s, t in outs)
    return pl.pallas_call(
        kernel,
        out_shape=[jax.ShapeDtypeStruct(s, t) for s, t in outs],
        in_specs=in_specs,
        out_specs=[pl.BlockSpec(memory_space=pltpu.VMEM) for _ in outs],
        scratch_shapes=[pltpu.VMEM(s, t) for s, t in scratch],
        compiler_params=pltpu.CompilerParams(vmem_limit_bytes=40 * 1024 * 1024),
        cost_estimate=pl.CostEstimate(flops=flops, bytes_accessed=moved, transcendentals=0),
    )(*inputs)


def line(count, step):
    return [(i, i + step) for i in range(count) if 0 <= i + step < count]


def beside(last, leading, axis, count):
    before = lax.ppermute(last, axis, line(count, 1))
    after = lax.ppermute(leading, axis, line(count, -1))
    return before, after


def along_width(x, count):
    outer = lax.ppermute(x, WIDTH, [(i, i - 1 + 2 * (i % 2)) for i in range(1, count - 1)])
    inner = lax.ppermute(x, WIDTH, [(i, i ^ 1) for i in range(count)])
    return outer, inner


def in_order(outer, inner):
    first = lax.axis_index("core") == 0
    return jnp.where(first, outer, inner), jnp.where(first, inner, outer)


def exchanged(parts, axes):
    return lax.all_to_all(parts, axes, 0, 0, tiled=True)


def joined(parts):
    return parts.reshape(-1, C)


def local(volume, fine_weight, coarse_weight, cotangent):
    sizes = {axis: lax.axis_size(axis) for axis in AXES}
    plane, along = (sizes["gx"] * sizes["y"], sizes["gy"] * sizes["zh"])
    peers = [sizes["gx"], sizes["gy"], sizes["y"] * sizes["zh"] * 2]
    place = [lax.axis_index(axis) for axis in ("gx", "gy", WIDTH, "core")]
    place = jnp.stack([p.astype(jnp.int32) for p in place])
    fine_sizes = [8 * n for n in peers]
    coarse_sizes = [4 * n for n in peers]

    fine_rows = fine_weight.reshape(27 * C, C)

    packed = jnp.concatenate([volume.reshape(512, C), cotangent.reshape(64, C)], axis=0)
    before, after = in_order(*along_width(packed, peers[2]))
    before_cells, after_cells = (b[:512].reshape(8, 8, 8, C) for b in (before, after))
    slabs = [
        jnp.concatenate([before_cells[:, at], volume[:, at], after_cells[:, at]], axis=2)
        for at in (slice(5, 8), slice(0, 3))
    ]
    below, above = beside(slabs[0], slabs[1], "gy", peers[1])
    own = jnp.concatenate([before_cells, volume, after_cells], axis=2)
    incoming = jnp.concatenate(
        [
            before[512:].reshape(4, 4, 4, C)[:, :, 2:],
            cotangent,
            after[512:].reshape(4, 4, 4, C)[:, :, :2],
        ],
        axis=2,
    ).astype(F32)
    sides = [
        jnp.concatenate([below[at], own[at], above[at]], axis=1)
        for at in (slice(5, 8), slice(0, 3))
    ]
    left, right = beside(sides[0], sides[1], "gx", peers[0])
    (middle,) = call(
        middle_kernel,
        [((6, 6, 24, C), F32)],
        [own.reshape(8, 192, C), fine_rows],
        scratch=[((8, 8, 32, C), F32), ((8, 144, 9 * C), BF16)],
        flops=2 * 864 * 27 * C * C,
    )
    across = [own.reshape(8, 192, C), below.reshape(8, 72, C), above.reshape(8, 72, C)]
    (edges,) = call(
        sides_kernel,
        [((6, 6, 24, C), F32)],
        across + [fine_rows],
        scratch=[((8, 10, 32, C), F32), ((8, 144, 9 * C), BF16)],
        flops=2 * 864 * 27 * C * C,
    )
    across = across + [left.reshape(3, 336, C), right.reshape(3, 336, C)]
    coarse, coarse_grad, slope, fine_sum, coarse_sum = call(
        lambda *refs: front_kernel(fine_sizes, coarse_sizes, *refs),
        [
            ((128, C), F32),
            ((128, C), BF16),
            ((12, 12, 24, C), F32),
            ((27 * C, C), BF16),
            ((27 * C, C), BF16),
        ],
        [place, *across, fine_rows, coarse_weight, incoming.reshape(128, C), middle, edges],
        scratch=[
            ((14, 14, 32, C), F32),
            ((10, 288, 9 * C), BF16),
            ((6, 12, 24, C), F32),
            ((6, 24, C), F32),
            ((6, 6, 16, C), F32),
            ((8, 8, 16, C), F32),
            ((6, 6, 16, C), F32),
            ((12, 12, 8, C), F32),
            ((14, 96, 9 * C), BF16),
        ],
        scalars=1,
        flops=2 * 4000 * 27 * C * C,
    )

    first = lax.axis_index("core") == 0
    swap = [(0, 1), (1, 0)]
    cells_fine = fine_sizes[0] * fine_sizes[1] * fine_sizes[2]
    scale = jnp.where(first, 1.0 / math.sqrt(cells_fine), 1.0 / math.sqrt(cells_fine // 8))
    scale = scale.astype(F32).reshape(1)
    mine = jnp.where(first, fine_sum, coarse_sum).astype(F32)
    other = jnp.where(first, coarse_sum, fine_sum)
    mine = mine + lax.ppermute(other, "core", swap).astype(F32)

    grads = coarse_grad.reshape(4, 4, 8, C)
    halo = beside(grads[:, 2:], grads[:, :2], "gy", peers[1])
    coarse_out = jax.nn.silu(coarse.reshape(4, 4, 8, C)[:, :, 2:6]).astype(BF16)
    parts = exchanged(mine.astype(BF16).reshape(plane, -1, C), PLANE)
    parts, halo, coarse_out = lax.optimization_barrier((parts, halo, coarse_out))
    length = parts.shape[1]
    padded = -(-length // (16 * along)) * 16 * along
    (part,) = call(plane_sum_kernel, [((padded, C), BF16)], [parts])
    parts = exchanged(part.reshape(along, padded // along, C), LINE)
    (parts,) = call(line_sum_kernel, [(parts.shape, BF16)], [scale, parts], scalars=1)
    parts = exchanged(parts, LINE)
    parts, halo = lax.optimization_barrier((parts, halo))
    part = joined(parts)[:length]
    grads = jnp.concatenate([halo[0], grads, halo[1]], axis=1)
    halo = beside(grads[2:], grads[:2], "gx", peers[0])
    around = jnp.concatenate([halo[0], grads, halo[1]], axis=0)
    (grad_volume,) = call(
        volume_kernel,
        [((512, C), BF16)],
        [around.reshape(512, C), coarse_weight, slope, fine_weight],
        scratch=[((8, 8, 16, C), F32), ((6, 6, 16, C), F32), ((10, 10, 16, C), F32)],
        flops=2 * 800 * 27 * C * C,
    )
    parts = exchanged(jnp.broadcast_to(part[None], (plane, length, C)), PLANE)
    parts, grad_volume = lax.optimization_barrier((parts, grad_volume))
    mine = joined(parts)
    other = lax.ppermute(mine, "core", swap)
    fine_done, coarse_done = placed(place[3:], mine, other)
    return (
        coarse_out,
        grad_volume.reshape(8, 8, 8, C),
        fine_done.reshape(27, C, C),
        coarse_done.reshape(27, C, C),
    )


def solution(mesh):
    shape = mesh.devices.shape
    inner = Mesh(mesh.devices.reshape(shape[0], shape[1], shape[2] // 4, 2, 2), AXES)
    cells = P("gx", "gy", WIDTH, None)
    return jax.shard_map(
        local,
        mesh=inner,
        in_specs=(cells, P(), P(), cells),
        out_specs=(cells, cells, P(), P()),
        check_vma=False,
    )
```

```python
import math

import jax
import jax.numpy as jnp
from jax import lax
from jax.experimental import pallas as pl
from jax.experimental.pallas import tpu as pltpu
from jax.sharding import Mesh, PartitionSpec as P

AXES = ("gx", "gy", "y", "zh", "core")
WIDTH = ("y", "zh", "core")
PLANE = ("gx", "y")
LINE = ("gy", "zh")
C = 128
F32 = jnp.float32
BF16 = jnp.bfloat16


def silu_slope(values):
    sigma = 1.0 / (1.0 + jnp.exp(-values))
    return sigma * (1.0 + values * (1.0 - sigma))


def inside(shape, starts, sizes):
    keep = None
    for dim in range(3):
        at = starts[dim] + lax.broadcasted_iota(jnp.int32, shape, dim)
        ok = (at >= 0) & (at < sizes[dim])
        keep = ok if keep is None else keep & ok
    return keep


def taps():
    return [(i, j, k) for i in range(3) for j in range(3) for k in range(3)]


def flat(values):
    return values.reshape(-1, C).astype(BF16)


def weight_terms(turned, cells, sum_ref, at):
    terms = jnp.dot(turned, cells, preferred_element_type=F32)
    for t in range(9):
        row = (at + t) * C
        sum_ref[row : row + C] = terms[:, t * C : (t + 1) * C].T.astype(BF16)


def back_conv(grads, weights):
    cells = jnp.concatenate(
        [flat(grads[2 - i : 8 - i, 2 - j : 8 - j, 2 - k : 10 - k]) for i, j, k in taps()], axis=1
    )
    turned = jnp.concatenate([weights[t] for t in range(27)], axis=1)
    back = lax.dot_general(cells, turned, (((1,), (1,)), ((), ())), preferred_element_type=F32)
    return back.reshape(6, 6, 8, C)


def gather(wide, patches, planes, columns=12):
    def plane(x, carry):
        for k in range(3):
            line = wide[x, :, 1 + k : 25 + k]
            for j in range(3):
                at = (3 * j + k) * C
                patches[x, :, at : at + C] = flat(line[j : j + columns])
        return carry

    lax.fori_loop(0, planes, plane, 0)


def fine_conv(patches, weights, at, planes, columns=12):
    rows = planes * columns * 24
    total = jnp.zeros((rows, C), F32)
    for i in range(3):
        cells = patches[pl.ds(at + i, planes)].reshape(rows, 9 * C)
        total = total + jnp.dot(
            cells, weights[9 * C * i : 9 * C * (i + 1)], preferred_element_type=F32
        )
    return total.reshape(planes, columns, 24, C)


def fill(wide, at, x, own, below, above):
    wide[at, 3:11, :24] = own[x].astype(F32).reshape(8, 24, C)
    wide[at, :3, :24] = below[x].astype(F32).reshape(3, 24, C)
    wide[at, 11:, :24] = above[x].astype(F32).reshape(3, 24, C)


def middle_kernel(own, weights, hidden_ref, wide, patches):
    for x in range(8):
        wide[x, :, :24] = own[x].astype(F32).reshape(8, 24, C)
    gather(wide, patches, 8, 6)
    hidden_ref[...] = fine_conv(patches, weights, 0, 6, 6)


def sides_kernel(own, below, above, weights, hidden_ref, wide, patches):
    for x in range(8):
        rows = own[x].astype(F32).reshape(8, 24, C)
        wide[x, :3, :24] = below[x].astype(F32).reshape(3, 24, C)
        wide[x, 3:5, :24] = rows[:2]
        wide[x, 5:7, :24] = rows[6:]
        wide[x, 7:, :24] = above[x].astype(F32).reshape(3, 24, C)

    def plane(x, carry):
        for k in range(3):
            line = wide[x, :, 1 + k : 25 + k]
            for j in range(3):
                at = (3 * j + k) * C
                cells = jnp.concatenate([line[j : j + 3], line[5 + j : 8 + j]], axis=0)
                patches[x, :, at : at + C] = flat(cells)
        return carry

    lax.fori_loop(0, 8, plane, 0)
    hidden_ref[...] = fine_conv(patches, weights, 0, 6, 6)


def front_kernel(
    fine_sizes, coarse_sizes, place, own, below, above, left, right, weights, coarse_weights, incoming,
    middle, sides,
    coarse_ref, grad_ref, slope_ref, fine_ref, coarse_sum_ref,
    wide, patches, outer, pairs, pooled, grads, spread, shares, near,
):
    order = [0, 1, 2, 3, 4, 10, 11, 12, 13, 5, 6, 7, 8, 9]
    for x in range(3):
        wide[x, :, :24] = left[x].astype(F32).reshape(14, 24, C)
        wide[order[11 + x], :, :24] = right[x].astype(F32).reshape(14, 24, C)
    for x in range(8):
        fill(wide, order[3 + x], x, own, below, above)
    gather(wide, patches, 10)
    for part in range(2):
        outer[3 * part : 3 * part + 3] = fine_conv(patches, weights, 5 * part, 3)

    for x in range(6):
        active = None
        for at in (2 * x, 2 * x + 1):
            if 3 <= at < 9:
                edges = sides[at - 3]
                value = jnp.concatenate([edges[:3], middle[at - 3], edges[3:]], axis=0)
            else:
                value = outer[at if at < 3 else at - 6]
            sigma = 1.0 / (1.0 + jnp.exp(-value))
            slope = sigma * (1.0 + value * (1.0 - sigma)) * 0.125
            starts = [8 * place[0] - 2 + at, 8 * place[1] - 2, 8 * place[2] - 6]
            keep = inside((1, 12, 24, C), starts, fine_sizes)[0]
            slope_ref[at] = jnp.where(keep, slope, 0.0)
            value = value * sigma
            active = value if active is None else active + value
        active = active.reshape(6, 2, 24, C)
        pairs[...] = active[:, 0] + active[:, 1]
        mean = (pairs[:, pl.ds(0, 12, 2)] + pairs[:, pl.ds(1, 12, 2)]) * 0.125
        starts = [4 * place[0] - 1 + x, 4 * place[1] - 1, 4 * place[2] - 3]
        keep = inside((1, 6, 12, C), starts, coarse_sizes)[0]
        pooled[x, :, :12] = jnp.where(keep, mean, 0.0)
        pooled[x, :, 12:] = jnp.zeros((6, 4, C), F32)

    cells = [flat(pooled[i : i + 4, j : j + 4, k : k + 8]) for i, j, k in taps()]
    coarse = jnp.dot(
        jnp.concatenate(cells, axis=1),
        coarse_weights[...].reshape(27 * C, C),
        preferred_element_type=F32,
    )
    coarse_ref[...] = coarse
    grad = (incoming[...] * silu_slope(coarse)).astype(BF16)
    grad_ref[...] = grad
    grad = grad.astype(F32)

    grads[...] = jnp.zeros((8, 8, 16, C), F32)
    grads[2:6, 2:6, :8] = grad.reshape(4, 4, 8, C)
    back = back_conv(grads, coarse_weights)
    spread[:, :, pl.ds(0, 8, 2)] = back
    spread[:, :, pl.ds(1, 8, 2)] = back
    for x in range(12):
        for y in range(12):
            shares[x, y] = spread[x // 2, y // 2, 2:10] * slope_ref[x, y, 6:14]
    turned = shares[...].reshape(1152, C).T.astype(BF16)
    for x in range(14):
        for k in range(3):
            line = wide[order[x], :, 7 + k : 15 + k]
            for j in range(3):
                at = (3 * j + k) * C
                near[x, :, at : at + C] = flat(line[j : j + 12])
    for i in range(3):
        weight_terms(turned, near[i : i + 12].reshape(1152, 9 * C), fine_ref, 9 * i)

    at = lax.broadcasted_iota(jnp.int32, (C, C), 0) % 8
    turned = jnp.where((at >= 2) & (at < 6), grad, 0.0).T.astype(BF16)
    for i in range(3):
        weight_terms(
            turned, jnp.concatenate(cells[9 * i : 9 * i + 9], axis=1), coarse_sum_ref, 9 * i
        )


def volume_kernel(around, coarse_weights, slope, weights, out_ref, grads, spread, fine):
    for x in range(8):
        grads[x, :, :8] = around[64 * x : 64 * x + 64].astype(F32).reshape(8, 8, C)
    back = back_conv(grads, coarse_weights)
    spread[:, :, pl.ds(0, 8, 2)] = back
    spread[:, :, pl.ds(1, 8, 2)] = back
    for x in range(10):
        for y in range(10):
            fine[x, y] = spread[(x + 1) // 2, (y + 1) // 2] * slope[x + 1, y + 1, 4:20]
    total = jnp.zeros((512, C), F32)
    for i in range(3):
        cells = jnp.concatenate(
            [
                flat(fine[2 - i : 10 - i, 2 - j : 10 - j, 3 - k : 11 - k])
                for j in range(3)
                for k in range(3)
            ],
            axis=1,
        )
        turned = jnp.concatenate([weights[9 * i + t] for t in range(9)], axis=1)
        total = total + lax.dot_general(
            cells, turned, (((1,), (1,)), ((), ())), preferred_element_type=F32
        )
    out_ref[...] = total.astype(BF16)


def plane_sum_kernel(parts, out_ref):
    total = parts[0].astype(F32)
    for at in range(1, parts.shape[0]):
        total = total + parts[at].astype(F32)
    rows = out_ref.shape[0] - total.shape[0]
    out_ref[...] = jnp.concatenate([total, jnp.zeros((rows, C), F32)], axis=0).astype(BF16)


def line_sum_kernel(scale, parts, out_ref):
    total = parts[0].astype(F32)
    for at in range(1, parts.shape[0]):
        total = total + parts[at].astype(F32)
    total = (total * scale[0]).astype(BF16)
    for at in range(out_ref.shape[0]):
        out_ref[at] = total


def call(kernel, outs, inputs, scratch=(), scalars=0, flops=0):
    in_specs = [
        pl.BlockSpec(memory_space=pltpu.SMEM if n < scalars else pltpu.VMEM)
        for n in range(len(inputs))
    ]
    moved = sum(a.size * a.dtype.itemsize for a in inputs)
    moved += sum(math.prod(s) * jnp.dtype(t).itemsize for s, t in outs)
    return pl.pallas_call(
        kernel,
        out_shape=[jax.ShapeDtypeStruct(s, t) for s, t in outs],
        in_specs=in_specs,
        out_specs=[pl.BlockSpec(memory_space=pltpu.VMEM) for _ in outs],
        scratch_shapes=[pltpu.VMEM(s, t) for s, t in scratch],
        compiler_params=pltpu.CompilerParams(vmem_limit_bytes=40 * 1024 * 1024),
        cost_estimate=pl.CostEstimate(flops=flops, bytes_accessed=moved, transcendentals=0),
    )(*inputs)


def line(count, step):
    return [(i, i + step) for i in range(count) if 0 <= i + step < count]


def beside(last, leading, axis, count):
    before = lax.ppermute(last, axis, line(count, 1))
    after = lax.ppermute(leading, axis, line(count, -1))
    return before, after


def along_width(x, count):
    outer = lax.ppermute(x, WIDTH, [(i, i - 1 + 2 * (i % 2)) for i in range(1, count - 1)])
    inner = lax.ppermute(x, WIDTH, [(i, i ^ 1) for i in range(count)])
    return outer, inner


def in_order(outer, inner):
    first = lax.axis_index("core") == 0
    return jnp.where(first, outer, inner), jnp.where(first, inner, outer)


def exchanged(parts, axes):
    return lax.all_to_all(parts, axes, 0, 0, tiled=True)


def joined(parts):
    return parts.reshape(-1, C)


def local(volume, fine_weight, coarse_weight, cotangent):
    sizes = {axis: lax.axis_size(axis) for axis in AXES}
    plane, along = (sizes["gx"] * sizes["y"], sizes["gy"] * sizes["zh"])
    peers = [sizes["gx"], sizes["gy"], sizes["y"] * sizes["zh"] * 2]
    place = [lax.axis_index(axis) for axis in ("gx", "gy", WIDTH)]
    place = jnp.stack([p.astype(jnp.int32) for p in place])
    fine_sizes = [8 * n for n in peers]
    coarse_sizes = [4 * n for n in peers]

    fine_rows = fine_weight.reshape(27 * C, C)

    packed = jnp.concatenate([volume.reshape(512, C), cotangent.reshape(64, C)], axis=0)
    before, after = in_order(*along_width(packed, peers[2]))
    before_cells, after_cells = (b[:512].reshape(8, 8, 8, C) for b in (before, after))
    slabs = [
        jnp.concatenate([before_cells[:, at], volume[:, at], after_cells[:, at]], axis=2)
        for at in (slice(5, 8), slice(0, 3))
    ]
    below, above = beside(slabs[0], slabs[1], "gy", peers[1])
    own = jnp.concatenate([before_cells, volume, after_cells], axis=2)
    incoming = jnp.concatenate(
        [
            before[512:].reshape(4, 4, 4, C)[:, :, 2:],
            cotangent,
            after[512:].reshape(4, 4, 4, C)[:, :, :2],
        ],
        axis=2,
    ).astype(F32)
    sides = [
        jnp.concatenate([below[at], own[at], above[at]], axis=1)
        for at in (slice(5, 8), slice(0, 3))
    ]
    left, right = beside(sides[0], sides[1], "gx", peers[0])
    (middle,) = call(
        middle_kernel,
        [((6, 6, 24, C), F32)],
        [own.reshape(8, 192, C), fine_rows],
        scratch=[((8, 8, 32, C), F32), ((8, 144, 9 * C), BF16)],
        flops=2 * 864 * 27 * C * C,
    )
    across = [own.reshape(8, 192, C), below.reshape(8, 72, C), above.reshape(8, 72, C)]
    (edges,) = call(
        sides_kernel,
        [((6, 6, 24, C), F32)],
        across + [fine_rows],
        scratch=[((8, 10, 32, C), F32), ((8, 144, 9 * C), BF16)],
        flops=2 * 864 * 27 * C * C,
    )
    across = across + [left.reshape(3, 336, C), right.reshape(3, 336, C)]
    coarse, coarse_grad, slope, fine_sum, coarse_sum = call(
        lambda *refs: front_kernel(fine_sizes, coarse_sizes, *refs),
        [
            ((128, C), F32),
            ((128, C), BF16),
            ((12, 12, 24, C), F32),
            ((27 * C, C), BF16),
            ((27 * C, C), BF16),
        ],
        [place, *across, fine_rows, coarse_weight, incoming.reshape(128, C), middle, edges],
        scratch=[
            ((14, 14, 32, C), F32),
            ((10, 288, 9 * C), BF16),
            ((6, 12, 24, C), F32),
            ((6, 24, C), F32),
            ((6, 6, 16, C), F32),
            ((8, 8, 16, C), F32),
            ((6, 6, 16, C), F32),
            ((12, 12, 8, C), F32),
            ((14, 96, 9 * C), BF16),
        ],
        scalars=1,
        flops=2 * 4000 * 27 * C * C,
    )

    first = lax.axis_index("core") == 0
    swap = [(0, 1), (1, 0)]
    cells_fine = fine_sizes[0] * fine_sizes[1] * fine_sizes[2]
    scale = jnp.where(first, 1.0 / math.sqrt(cells_fine), 1.0 / math.sqrt(cells_fine // 8))
    scale = scale.astype(F32).reshape(1)
    mine = jnp.where(first, fine_sum, coarse_sum).astype(F32)
    other = jnp.where(first, coarse_sum, fine_sum)
    mine = mine + lax.ppermute(other, "core", swap).astype(F32)

    grads = coarse_grad.reshape(4, 4, 8, C)
    halo = beside(grads[:, 2:], grads[:, :2], "gy", peers[1])
    coarse_out = jax.nn.silu(coarse.reshape(4, 4, 8, C)[:, :, 2:6]).astype(BF16)
    parts = exchanged(mine.astype(BF16).reshape(plane, -1, C), PLANE)
    parts, halo, coarse_out = lax.optimization_barrier((parts, halo, coarse_out))
    length = parts.shape[1]
    padded = -(-length // (16 * along)) * 16 * along
    (part,) = call(plane_sum_kernel, [((padded, C), BF16)], [parts])
    parts = exchanged(part.reshape(along, padded // along, C), LINE)
    (parts,) = call(line_sum_kernel, [(parts.shape, BF16)], [scale, parts], scalars=1)
    parts = exchanged(parts, LINE)
    parts, halo = lax.optimization_barrier((parts, halo))
    part = joined(parts)[:length]
    grads = jnp.concatenate([halo[0], grads, halo[1]], axis=1)
    halo = beside(grads[2:], grads[:2], "gx", peers[0])
    around = jnp.concatenate([halo[0], grads, halo[1]], axis=0)
    parts = exchanged(jnp.broadcast_to(part[None], (plane, length, C)), PLANE)
    parts, around = lax.optimization_barrier((parts, around))
    (grad_volume,) = call(
        volume_kernel,
        [((512, C), BF16)],
        [around.reshape(512, C), coarse_weight, slope, fine_weight],
        scratch=[((8, 8, 16, C), F32), ((6, 6, 16, C), F32), ((10, 10, 16, C), F32)],
        flops=2 * 800 * 27 * C * C,
    )
    mine = joined(parts)
    other = lax.ppermute(mine, "core", swap)
    fine_done = jnp.where(first, mine, other)
    coarse_done = jnp.where(first, other, mine)
    return (
        coarse_out,
        grad_volume.reshape(8, 8, 8, C),
        fine_done.reshape(27, C, C),
        coarse_done.reshape(27, C, C),
    )


def solution(mesh):
    shape = mesh.devices.shape
    inner = Mesh(mesh.devices.reshape(shape[0], shape[1], shape[2] // 4, 2, 2), AXES)
    cells = P("gx", "gy", WIDTH, None)
    return jax.shard_map(
        local,
        mesh=inner,
        in_specs=(cells, P(), P(), cells),
        out_specs=(cells, cells, P(), P()),
        check_vma=False,
    )
```

```python
import math

import jax
import jax.numpy as jnp
from jax import lax
from jax.experimental import pallas as pl
from jax.experimental.pallas import tpu as pltpu
from jax.sharding import Mesh, PartitionSpec as P

AXES = ("gx", "gy", "y", "zh", "core")
WIDTH = ("y", "zh", "core")
PLANE = ("gx", "y")
LINE = ("gy", "zh")
C = 128
F32 = jnp.float32
BF16 = jnp.bfloat16


def silu_slope(values):
    sigma = 1.0 / (1.0 + jnp.exp(-values))
    return sigma * (1.0 + values * (1.0 - sigma))


def inside(shape, starts, sizes):
    keep = None
    for dim in range(3):
        at = starts[dim] + lax.broadcasted_iota(jnp.int32, shape, dim)
        ok = (at >= 0) & (at < sizes[dim])
        keep = ok if keep is None else keep & ok
    return keep


def taps():
    return [(i, j, k) for i in range(3) for j in range(3) for k in range(3)]


def flat(values):
    return values.reshape(-1, C).astype(BF16)


def weight_terms(turned, cells, sum_ref, at):
    terms = jnp.dot(turned, cells, preferred_element_type=F32)
    for t in range(9):
        row = (at + t) * C
        sum_ref[row : row + C] = terms[:, t * C : (t + 1) * C].T.astype(BF16)


def back_conv(grads, weights):
    cells = jnp.concatenate(
        [flat(grads[2 - i : 8 - i, 2 - j : 8 - j, 2 - k : 10 - k]) for i, j, k in taps()], axis=1
    )
    turned = jnp.concatenate([weights[t] for t in range(27)], axis=1)
    back = lax.dot_general(cells, turned, (((1,), (1,)), ((), ())), preferred_element_type=F32)
    return back.reshape(6, 6, 8, C)


def gather(wide, patches, planes, columns=12):
    def plane(x, carry):
        for k in range(3):
            line = wide[x, :, 1 + k : 25 + k]
            for j in range(3):
                at = (3 * j + k) * C
                patches[x, :, at : at + C] = flat(line[j : j + columns])
        return carry

    lax.fori_loop(0, planes, plane, 0)


def fine_conv(patches, weights, at, planes, columns=12):
    rows = planes * columns * 24
    total = jnp.zeros((rows, C), F32)
    for i in range(3):
        cells = patches[pl.ds(at + i, planes)].reshape(rows, 9 * C)
        total = total + jnp.dot(
            cells, weights[9 * C * i : 9 * C * (i + 1)], preferred_element_type=F32
        )
    return total.reshape(planes, columns, 24, C)


def fill(wide, at, x, own, below, above):
    wide[at, 3:11, :24] = own[x].astype(F32).reshape(8, 24, C)
    wide[at, :3, :24] = below[x].astype(F32).reshape(3, 24, C)
    wide[at, 11:, :24] = above[x].astype(F32).reshape(3, 24, C)


def middle_kernel(own, weights, hidden_ref, wide, patches):
    for x in range(8):
        wide[x, :, :24] = own[x].astype(F32).reshape(8, 24, C)
    gather(wide, patches, 8, 6)
    hidden_ref[...] = fine_conv(patches, weights, 0, 6, 6)


def sides_kernel(own, below, above, weights, hidden_ref, wide, patches):
    for x in range(8):
        rows = own[x].astype(F32).reshape(8, 24, C)
        wide[x, :3, :24] = below[x].astype(F32).reshape(3, 24, C)
        wide[x, 3:5, :24] = rows[:2]
        wide[x, 5:7, :24] = rows[6:]
        wide[x, 7:, :24] = above[x].astype(F32).reshape(3, 24, C)

    def plane(x, carry):
        for k in range(3):
            line = wide[x, :, 1 + k : 25 + k]
            for j in range(3):
                at = (3 * j + k) * C
                cells = jnp.concatenate([line[j : j + 3], line[5 + j : 8 + j]], axis=0)
                patches[x, :, at : at + C] = flat(cells)
        return carry

    lax.fori_loop(0, 8, plane, 0)
    hidden_ref[...] = fine_conv(patches, weights, 0, 6, 6)


def front_kernel(
    fine_sizes, coarse_sizes, place, own, below, above, left, right, weights, coarse_weights, incoming,
    middle, sides,
    coarse_ref, grad_ref, slope_ref, fine_ref, coarse_sum_ref,
    wide, patches, outer, pairs, pooled, grads, spread, shares, near,
):
    order = [0, 1, 2, 3, 4, 10, 11, 12, 13, 5, 6, 7, 8, 9]
    for x in range(3):
        wide[x, :, :24] = left[x].astype(F32).reshape(14, 24, C)
        wide[order[11 + x], :, :24] = right[x].astype(F32).reshape(14, 24, C)
    for x in range(8):
        fill(wide, order[3 + x], x, own, below, above)
    gather(wide, patches, 10)
    for part in range(2):
        outer[3 * part : 3 * part + 3] = fine_conv(patches, weights, 5 * part, 3)

    for x in range(6):
        active = None
        for at in (2 * x, 2 * x + 1):
            if 3 <= at < 9:
                edges = sides[at - 3]
                value = jnp.concatenate([edges[:3], middle[at - 3], edges[3:]], axis=0)
            else:
                value = outer[at if at < 3 else at - 6]
            sigma = 1.0 / (1.0 + jnp.exp(-value))
            slope = sigma * (1.0 + value * (1.0 - sigma)) * 0.125
            starts = [8 * place[0] - 2 + at, 8 * place[1] - 2, 8 * place[2] - 6]
            keep = inside((1, 12, 24, C), starts, fine_sizes)[0]
            slope_ref[at] = jnp.where(keep, slope, 0.0)
            value = value * sigma
            active = value if active is None else active + value
        active = active.reshape(6, 2, 24, C)
        pairs[...] = active[:, 0] + active[:, 1]
        mean = (pairs[:, pl.ds(0, 12, 2)] + pairs[:, pl.ds(1, 12, 2)]) * 0.125
        starts = [4 * place[0] - 1 + x, 4 * place[1] - 1, 4 * place[2] - 3]
        keep = inside((1, 6, 12, C), starts, coarse_sizes)[0]
        pooled[x, :, :12] = jnp.where(keep, mean, 0.0)
        pooled[x, :, 12:] = jnp.zeros((6, 4, C), F32)

    cells = [flat(pooled[i : i + 4, j : j + 4, k : k + 8]) for i, j, k in taps()]
    coarse = jnp.dot(
        jnp.concatenate(cells, axis=1),
        coarse_weights[...].reshape(27 * C, C),
        preferred_element_type=F32,
    )
    coarse_ref[...] = coarse
    grad = (incoming[...] * silu_slope(coarse)).astype(BF16)
    grad_ref[...] = grad
    grad = grad.astype(F32)

    grads[...] = jnp.zeros((8, 8, 16, C), F32)
    grads[2:6, 2:6, :8] = grad.reshape(4, 4, 8, C)
    back = back_conv(grads, coarse_weights)
    spread[:, :, pl.ds(0, 8, 2)] = back
    spread[:, :, pl.ds(1, 8, 2)] = back
    for x in range(12):
        for y in range(12):
            shares[x, y] = spread[x // 2, y // 2, 2:10] * slope_ref[x, y, 6:14]
    turned = shares[...].reshape(1152, C).T.astype(BF16)
    for x in range(14):
        for k in range(3):
            line = wide[order[x], :, 7 + k : 15 + k]
            for j in range(3):
                at = (3 * j + k) * C
                near[x, :, at : at + C] = flat(line[j : j + 12])
    for i in range(3):
        weight_terms(turned, near[i : i + 12].reshape(1152, 9 * C), fine_ref, 9 * i)

    at = lax.broadcasted_iota(jnp.int32, (C, C), 0) % 8
    turned = jnp.where((at >= 2) & (at < 6), grad, 0.0).T.astype(BF16)
    for i in range(3):
        weight_terms(
            turned, jnp.concatenate(cells[9 * i : 9 * i + 9], axis=1), coarse_sum_ref, 9 * i
        )


def fine_grad_kernel(left, middle, right, coarse_weights, slope, fine_ref, grads, spread):
    for x in range(2):
        for at, part in ((x, left), (6 + x, right)):
            grads[at, :, :8] = part[64 * x : 64 * x + 64].astype(F32).reshape(8, 8, C)
    for x in range(4):
        grads[2 + x, :, :8] = middle[64 * x : 64 * x + 64].astype(F32).reshape(8, 8, C)
    back = back_conv(grads, coarse_weights)
    spread[:, :, pl.ds(0, 8, 2)] = back
    spread[:, :, pl.ds(1, 8, 2)] = back
    for x in range(10):
        for y in range(10):
            fine_ref[x, y] = spread[(x + 1) // 2, (y + 1) // 2] * slope[x + 1, y + 1, 4:20]


def volume_kernel(fine, weights, out_ref):
    total = jnp.zeros((512, C), F32)
    for i in range(3):
        cells = jnp.concatenate(
            [
                flat(fine[2 - i : 10 - i, 2 - j : 10 - j, 3 - k : 11 - k])
                for j in range(3)
                for k in range(3)
            ],
            axis=1,
        )
        turned = jnp.concatenate([weights[9 * i + t] for t in range(9)], axis=1)
        total = total + lax.dot_general(
            cells, turned, (((1,), (1,)), ((), ())), preferred_element_type=F32
        )
    out_ref[...] = total.astype(BF16)


def plane_sum_kernel(parts, out_ref):
    total = parts[0].astype(F32)
    for at in range(1, parts.shape[0]):
        total = total + parts[at].astype(F32)
    rows = out_ref.shape[0] - total.shape[0]
    out_ref[...] = jnp.concatenate([total, jnp.zeros((rows, C), F32)], axis=0).astype(BF16)


def line_sum_kernel(scale, parts, out_ref):
    total = parts[0].astype(F32)
    for at in range(1, parts.shape[0]):
        total = total + parts[at].astype(F32)
    total = (total * scale[0]).astype(BF16)
    for at in range(out_ref.shape[0]):
        out_ref[at] = total


def call(kernel, outs, inputs, scratch=(), scalars=0, flops=0):
    in_specs = [
        pl.BlockSpec(memory_space=pltpu.SMEM if n < scalars else pltpu.VMEM)
        for n in range(len(inputs))
    ]
    moved = sum(a.size * a.dtype.itemsize for a in inputs)
    moved += sum(math.prod(s) * jnp.dtype(t).itemsize for s, t in outs)
    return pl.pallas_call(
        kernel,
        out_shape=[jax.ShapeDtypeStruct(s, t) for s, t in outs],
        in_specs=in_specs,
        out_specs=[pl.BlockSpec(memory_space=pltpu.VMEM) for _ in outs],
        scratch_shapes=[pltpu.VMEM(s, t) for s, t in scratch],
        compiler_params=pltpu.CompilerParams(vmem_limit_bytes=40 * 1024 * 1024),
        cost_estimate=pl.CostEstimate(flops=flops, bytes_accessed=moved, transcendentals=0),
    )(*inputs)


def line(count, step):
    return [(i, i + step) for i in range(count) if 0 <= i + step < count]


def beside(last, leading, axis, count):
    before = lax.ppermute(last, axis, line(count, 1))
    after = lax.ppermute(leading, axis, line(count, -1))
    return before, after


def along_width(x, count):
    outer = lax.ppermute(x, WIDTH, [(i, i - 1 + 2 * (i % 2)) for i in range(1, count - 1)])
    inner = lax.ppermute(x, WIDTH, [(i, i ^ 1) for i in range(count)])
    return outer, inner


def in_order(outer, inner):
    first = lax.axis_index("core") == 0
    return jnp.where(first, outer, inner), jnp.where(first, inner, outer)


def exchanged(parts, axes):
    return lax.all_to_all(parts, axes, 0, 0, tiled=True)


def joined(parts):
    return parts.reshape(-1, C)


def local(volume, fine_weight, coarse_weight, cotangent):
    sizes = {axis: lax.axis_size(axis) for axis in AXES}
    plane, along = (sizes["gx"] * sizes["y"], sizes["gy"] * sizes["zh"])
    peers = [sizes["gx"], sizes["gy"], sizes["y"] * sizes["zh"] * 2]
    place = [lax.axis_index(axis) for axis in ("gx", "gy", WIDTH)]
    place = jnp.stack([p.astype(jnp.int32) for p in place])
    fine_sizes = [8 * n for n in peers]
    coarse_sizes = [4 * n for n in peers]

    fine_rows = fine_weight.reshape(27 * C, C)

    packed = jnp.concatenate([volume.reshape(512, C), cotangent.reshape(64, C)], axis=0)
    before, after = in_order(*along_width(packed, peers[2]))
    before_cells, after_cells = (b[:512].reshape(8, 8, 8, C) for b in (before, after))
    slabs = [
        jnp.concatenate([before_cells[:, at], volume[:, at], after_cells[:, at]], axis=2)
        for at in (slice(5, 8), slice(0, 3))
    ]
    below, above = beside(slabs[0], slabs[1], "gy", peers[1])
    own = jnp.concatenate([before_cells, volume, after_cells], axis=2)
    incoming = jnp.concatenate(
        [
            before[512:].reshape(4, 4, 4, C)[:, :, 2:],
            cotangent,
            after[512:].reshape(4, 4, 4, C)[:, :, :2],
        ],
        axis=2,
    ).astype(F32)
    sides = [
        jnp.concatenate([below[at], own[at], above[at]], axis=1)
        for at in (slice(5, 8), slice(0, 3))
    ]
    left, right = beside(sides[0], sides[1], "gx", peers[0])
    (middle,) = call(
        middle_kernel,
        [((6, 6, 24, C), F32)],
        [own.reshape(8, 192, C), fine_rows],
        scratch=[((8, 8, 32, C), F32), ((8, 144, 9 * C), BF16)],
        flops=2 * 864 * 27 * C * C,
    )
    across = [own.reshape(8, 192, C), below.reshape(8, 72, C), above.reshape(8, 72, C)]
    (edges,) = call(
        sides_kernel,
        [((6, 6, 24, C), F32)],
        across + [fine_rows],
        scratch=[((8, 10, 32, C), F32), ((8, 144, 9 * C), BF16)],
        flops=2 * 864 * 27 * C * C,
    )
    across = across + [left.reshape(3, 336, C), right.reshape(3, 336, C)]
    coarse, coarse_grad, slope, fine_sum, coarse_sum = call(
        lambda *refs: front_kernel(fine_sizes, coarse_sizes, *refs),
        [
            ((128, C), F32),
            ((128, C), BF16),
            ((12, 12, 24, C), F32),
            ((27 * C, C), BF16),
            ((27 * C, C), BF16),
        ],
        [place, *across, fine_rows, coarse_weight, incoming.reshape(128, C), middle, edges],
        scratch=[
            ((14, 14, 32, C), F32),
            ((10, 288, 9 * C), BF16),
            ((6, 12, 24, C), F32),
            ((6, 24, C), F32),
            ((6, 6, 16, C), F32),
            ((8, 8, 16, C), F32),
            ((6, 6, 16, C), F32),
            ((12, 12, 8, C), F32),
            ((14, 96, 9 * C), BF16),
        ],
        scalars=1,
        flops=2 * 4000 * 27 * C * C,
    )

    first = lax.axis_index("core") == 0
    swap = [(0, 1), (1, 0)]
    cells_fine = fine_sizes[0] * fine_sizes[1] * fine_sizes[2]
    scale = jnp.where(first, 1.0 / math.sqrt(cells_fine), 1.0 / math.sqrt(cells_fine // 8))
    scale = scale.astype(F32).reshape(1)
    mine = jnp.where(first, fine_sum, coarse_sum).astype(F32)
    other = jnp.where(first, coarse_sum, fine_sum)
    mine = mine + lax.ppermute(other, "core", swap).astype(F32)

    grads = coarse_grad.reshape(4, 4, 8, C)
    halo = beside(grads[:, 2:], grads[:, :2], "gy", peers[1])
    coarse_out = jax.nn.silu(coarse.reshape(4, 4, 8, C)[:, :, 2:6]).astype(BF16)
    parts = exchanged(mine.astype(BF16).reshape(plane, -1, C), PLANE)
    parts, halo, coarse_out = lax.optimization_barrier((parts, halo, coarse_out))
    length = parts.shape[1]
    padded = -(-length // (16 * along)) * 16 * along
    (part,) = call(plane_sum_kernel, [((padded, C), BF16)], [parts])
    parts = exchanged(part.reshape(along, padded // along, C), LINE)
    (parts,) = call(line_sum_kernel, [(parts.shape, BF16)], [scale, parts], scalars=1)
    parts = exchanged(parts, LINE)
    parts, halo = lax.optimization_barrier((parts, halo))
    part = joined(parts)[:length]
    grads = jnp.concatenate([halo[0], grads, halo[1]], axis=1)
    halo = beside(grads[2:], grads[:2], "gx", peers[0])
    (fine_grad,) = call(
        fine_grad_kernel,
        [((10, 10, 16, C), F32)],
        [
            halo[0].reshape(128, C),
            grads.reshape(256, C),
            halo[1].reshape(128, C),
            coarse_weight,
            slope,
        ],
        scratch=[((8, 8, 16, C), F32), ((6, 6, 16, C), F32)],
        flops=2 * 288 * 27 * C * C,
    )
    parts = exchanged(jnp.broadcast_to(part[None], (plane, length, C)), PLANE)
    parts, fine_grad = lax.optimization_barrier((parts, fine_grad))
    (grad_volume,) = call(
        volume_kernel,
        [((512, C), BF16)],
        [fine_grad, fine_weight],
        flops=2 * 512 * 27 * C * C,
    )
    mine = joined(parts)
    other = lax.ppermute(mine, "core", swap)
    fine_done = jnp.where(first, mine, other)
    coarse_done = jnp.where(first, other, mine)
    return (
        coarse_out,
        grad_volume.reshape(8, 8, 8, C),
        fine_done.reshape(27, C, C),
        coarse_done.reshape(27, C, C),
    )


def solution(mesh):
    shape = mesh.devices.shape
    inner = Mesh(mesh.devices.reshape(shape[0], shape[1], shape[2] // 4, 2, 2), AXES)
    cells = P("gx", "gy", WIDTH, None)
    return jax.shard_map(
        local,
        mesh=inner,
        in_specs=(cells, P(), P(), cells),
        out_specs=(cells, cells, P(), P()),
        check_vma=False,
    )
```

```python
import math

import jax
import jax.numpy as jnp
from jax import lax
from jax.experimental import pallas as pl
from jax.experimental.pallas import tpu as pltpu
from jax.sharding import Mesh, PartitionSpec as P

AXES = ("gx", "gy", "y", "zh", "core")
WIDTH = ("y", "zh", "core")
PLANE = ("gx", "y")
LINE = ("gy", "zh")
C = 128
F32 = jnp.float32
BF16 = jnp.bfloat16


def silu_slope(values):
    sigma = 1.0 / (1.0 + jnp.exp(-values))
    return sigma * (1.0 + values * (1.0 - sigma))


def inside(shape, starts, sizes):
    keep = None
    for dim in range(3):
        at = starts[dim] + lax.broadcasted_iota(jnp.int32, shape, dim)
        ok = (at >= 0) & (at < sizes[dim])
        keep = ok if keep is None else keep & ok
    return keep


def taps():
    return [(i, j, k) for i in range(3) for j in range(3) for k in range(3)]


def flat(values):
    return values.reshape(-1, C).astype(BF16)


def weight_terms(turned, cells, sum_ref, at):
    terms = jnp.dot(turned, cells, preferred_element_type=F32)
    for t in range(9):
        row = (at + t) * C
        sum_ref[row : row + C] = terms[:, t * C : (t + 1) * C].T.astype(BF16)


def back_conv(grads, weights):
    cells = jnp.concatenate(
        [flat(grads[2 - i : 8 - i, 2 - j : 8 - j, 2 - k : 10 - k]) for i, j, k in taps()], axis=1
    )
    turned = jnp.concatenate([weights[t] for t in range(27)], axis=1)
    back = lax.dot_general(cells, turned, (((1,), (1,)), ((), ())), preferred_element_type=F32)
    return back.reshape(6, 6, 8, C)


def gather(wide, patches, planes, columns=12):
    def plane(x, carry):
        for k in range(3):
            line = wide[x, :, 1 + k : 25 + k]
            for j in range(3):
                at = (3 * j + k) * C
                patches[x, :, at : at + C] = flat(line[j : j + columns])
        return carry

    lax.fori_loop(0, planes, plane, 0)


def fine_conv(patches, weights, at, planes, columns=12):
    rows = planes * columns * 24
    total = jnp.zeros((rows, C), F32)
    for i in range(3):
        cells = patches[pl.ds(at + i, planes)].reshape(rows, 9 * C)
        total = total + jnp.dot(
            cells, weights[9 * C * i : 9 * C * (i + 1)], preferred_element_type=F32
        )
    return total.reshape(planes, columns, 24, C)


def fill(wide, at, x, own, below, above):
    wide[at, 3:11, :24] = own[x].astype(F32).reshape(8, 24, C)
    wide[at, :3, :24] = below[x].astype(F32).reshape(3, 24, C)
    wide[at, 11:, :24] = above[x].astype(F32).reshape(3, 24, C)


def middle_kernel(own, weights, hidden_ref, wide, patches):
    for x in range(8):
        wide[x, :, :24] = own[x].astype(F32).reshape(8, 24, C)
    gather(wide, patches, 8, 6)
    hidden_ref[...] = fine_conv(patches, weights, 0, 6, 6)


def sides_kernel(own, below, above, weights, hidden_ref, wide, patches):
    for x in range(8):
        rows = own[x].astype(F32).reshape(8, 24, C)
        wide[x, :3, :24] = below[x].astype(F32).reshape(3, 24, C)
        wide[x, 3:5, :24] = rows[:2]
        wide[x, 5:7, :24] = rows[6:]
        wide[x, 7:, :24] = above[x].astype(F32).reshape(3, 24, C)

    def plane(x, carry):
        for k in range(3):
            line = wide[x, :, 1 + k : 25 + k]
            for j in range(3):
                at = (3 * j + k) * C
                cells = jnp.concatenate([line[j : j + 3], line[5 + j : 8 + j]], axis=0)
                patches[x, :, at : at + C] = flat(cells)
        return carry

    lax.fori_loop(0, 8, plane, 0)
    hidden_ref[...] = fine_conv(patches, weights, 0, 6, 6)


def front_kernel(
    fine_sizes, coarse_sizes, place, own, below, above, left, right, weights, coarse_weights, incoming,
    middle, sides,
    coarse_ref, grad_ref, slope_ref, fine_ref, coarse_sum_ref,
    wide, patches, outer, pairs, pooled, grads, spread, shares, near,
):
    order = [0, 1, 2, 3, 4, 10, 11, 12, 13, 5, 6, 7, 8, 9]
    for x in range(3):
        wide[x, :, :24] = left[x].astype(F32).reshape(14, 24, C)
        wide[order[11 + x], :, :24] = right[x].astype(F32).reshape(14, 24, C)
    for x in range(8):
        fill(wide, order[3 + x], x, own, below, above)
    gather(wide, patches, 10)
    for part in range(2):
        outer[3 * part : 3 * part + 3] = fine_conv(patches, weights, 5 * part, 3)

    for x in range(6):
        active = None
        for at in (2 * x, 2 * x + 1):
            if 3 <= at < 9:
                edges = sides[at - 3]
                value = jnp.concatenate([edges[:3], middle[at - 3], edges[3:]], axis=0)
            else:
                value = outer[at if at < 3 else at - 6]
            sigma = 1.0 / (1.0 + jnp.exp(-value))
            slope = sigma * (1.0 + value * (1.0 - sigma)) * 0.125
            starts = [8 * place[0] - 2 + at, 8 * place[1] - 2, 8 * place[2] - 6]
            keep = inside((1, 12, 24, C), starts, fine_sizes)[0]
            slope_ref[at] = jnp.where(keep, slope, 0.0)
            value = value * sigma
            active = value if active is None else active + value
        active = active.reshape(6, 2, 24, C)
        pairs[...] = active[:, 0] + active[:, 1]
        mean = (pairs[:, pl.ds(0, 12, 2)] + pairs[:, pl.ds(1, 12, 2)]) * 0.125
        starts = [4 * place[0] - 1 + x, 4 * place[1] - 1, 4 * place[2] - 3]
        keep = inside((1, 6, 12, C), starts, coarse_sizes)[0]
        pooled[x, :, :12] = jnp.where(keep, mean, 0.0)
        pooled[x, :, 12:] = jnp.zeros((6, 4, C), F32)

    cells = [flat(pooled[i : i + 4, j : j + 4, k : k + 8]) for i, j, k in taps()]
    coarse = jnp.dot(
        jnp.concatenate(cells, axis=1),
        coarse_weights[...].reshape(27 * C, C),
        preferred_element_type=F32,
    )
    coarse_ref[...] = coarse
    grad = (incoming[...] * silu_slope(coarse)).astype(BF16)
    grad_ref[...] = grad
    grad = grad.astype(F32)

    grads[...] = jnp.zeros((8, 8, 16, C), F32)
    grads[2:6, 2:6, :8] = grad.reshape(4, 4, 8, C)
    back = back_conv(grads, coarse_weights)
    spread[:, :, pl.ds(0, 8, 2)] = back
    spread[:, :, pl.ds(1, 8, 2)] = back
    for x in range(12):
        for y in range(12):
            shares[x, y] = spread[x // 2, y // 2, 2:10] * slope_ref[x, y, 6:14]
    turned = shares[...].reshape(1152, C).T.astype(BF16)
    for x in range(14):
        for k in range(3):
            line = wide[order[x], :, 7 + k : 15 + k]
            for j in range(3):
                at = (3 * j + k) * C
                near[x, :, at : at + C] = flat(line[j : j + 12])
    for i in range(3):
        weight_terms(turned, near[i : i + 12].reshape(1152, 9 * C), fine_ref, 9 * i)

    at = lax.broadcasted_iota(jnp.int32, (C, C), 0) % 8
    turned = jnp.where((at >= 2) & (at < 6), grad, 0.0).T.astype(BF16)
    for i in range(3):
        weight_terms(
            turned, jnp.concatenate(cells[9 * i : 9 * i + 9], axis=1), coarse_sum_ref, 9 * i
        )


def fine_grad_kernel(left, middle, right, coarse_weights, slope, fine_ref, grads, spread):
    for x in range(2):
        for at, part in ((x, left), (6 + x, right)):
            grads[at, :, :8] = part[64 * x : 64 * x + 64].astype(F32).reshape(8, 8, C)
    for x in range(4):
        grads[2 + x, :, :8] = middle[64 * x : 64 * x + 64].astype(F32).reshape(8, 8, C)
    back = back_conv(grads, coarse_weights)
    spread[:, :, pl.ds(0, 8, 2)] = back
    spread[:, :, pl.ds(1, 8, 2)] = back
    for x in range(10):
        for y in range(10):
            fine_ref[x, y] = spread[(x + 1) // 2, (y + 1) // 2] * slope[x + 1, y + 1, 4:20]


def volume_kernel(fine, weights, out_ref):
    total = jnp.zeros((512, C), F32)
    for i in range(3):
        cells = jnp.concatenate(
            [
                flat(fine[2 - i : 10 - i, 2 - j : 10 - j, 3 - k : 11 - k])
                for j in range(3)
                for k in range(3)
            ],
            axis=1,
        )
        turned = jnp.concatenate(
            [weights[(9 * i + t) * C : (9 * i + t + 1) * C] for t in range(9)], axis=1
        )
        total = total + lax.dot_general(
            cells, turned, (((1,), (1,)), ((), ())), preferred_element_type=F32
        )
    out_ref[...] = total.astype(BF16)


def plane_sum_kernel(parts, out_ref):
    total = parts[0].astype(F32)
    for at in range(1, parts.shape[0]):
        total = total + parts[at].astype(F32)
    rows = out_ref.shape[0] - total.shape[0]
    out_ref[...] = jnp.concatenate([total, jnp.zeros((rows, C), F32)], axis=0).astype(BF16)


def line_sum_kernel(scale, parts, out_ref):
    total = parts[0].astype(F32)
    for at in range(1, parts.shape[0]):
        total = total + parts[at].astype(F32)
    total = (total * scale[0]).astype(BF16)
    for at in range(out_ref.shape[0]):
        out_ref[at] = total


def call(kernel, outs, inputs, scratch=(), scalars=0, flops=0):
    in_specs = [
        pl.BlockSpec(memory_space=pltpu.SMEM if n < scalars else pltpu.VMEM)
        for n in range(len(inputs))
    ]
    moved = sum(a.size * a.dtype.itemsize for a in inputs)
    moved += sum(math.prod(s) * jnp.dtype(t).itemsize for s, t in outs)
    return pl.pallas_call(
        kernel,
        out_shape=[jax.ShapeDtypeStruct(s, t) for s, t in outs],
        in_specs=in_specs,
        out_specs=[pl.BlockSpec(memory_space=pltpu.VMEM) for _ in outs],
        scratch_shapes=[pltpu.VMEM(s, t) for s, t in scratch],
        compiler_params=pltpu.CompilerParams(vmem_limit_bytes=28 * 1024 * 1024),
        cost_estimate=pl.CostEstimate(flops=flops, bytes_accessed=moved, transcendentals=0),
    )(*inputs)


def line(count, step):
    return [(i, i + step) for i in range(count) if 0 <= i + step < count]


def beside(last, leading, axis, count):
    before = lax.ppermute(last, axis, line(count, 1))
    after = lax.ppermute(leading, axis, line(count, -1))
    return before, after


def along_width(x, count):
    outer = lax.ppermute(x, WIDTH, [(i, i - 1 + 2 * (i % 2)) for i in range(1, count - 1)])
    inner = lax.ppermute(x, WIDTH, [(i, i ^ 1) for i in range(count)])
    return outer, inner


def in_order(outer, inner):
    first = lax.axis_index("core") == 0
    return jnp.where(first, outer, inner), jnp.where(first, inner, outer)


def exchanged(parts, axes):
    return lax.all_to_all(parts, axes, 0, 0, tiled=True)


def joined(parts):
    return parts.reshape(-1, C)


def local(volume, fine_weight, coarse_weight, cotangent):
    sizes = {axis: lax.axis_size(axis) for axis in AXES}
    plane, along = (sizes["gx"] * sizes["y"], sizes["gy"] * sizes["zh"])
    peers = [sizes["gx"], sizes["gy"], sizes["y"] * sizes["zh"] * 2]
    place = [lax.axis_index(axis) for axis in ("gx", "gy", WIDTH)]
    place = jnp.stack([p.astype(jnp.int32) for p in place])
    fine_sizes = [8 * n for n in peers]
    coarse_sizes = [4 * n for n in peers]

    fine_rows = fine_weight.reshape(27 * C, C)

    halo = along_width(volume, peers[2])
    cots = along_width(cotangent, peers[2])
    halo, cots = lax.optimization_barrier((halo, cots))
    before_cells, after_cells = in_order(*halo)
    slabs = [
        jnp.concatenate([before_cells[:, at], volume[:, at], after_cells[:, at]], axis=2)
        for at in (slice(5, 8), slice(0, 3))
    ]
    below, above = beside(slabs[0], slabs[1], "gy", peers[1])
    own = jnp.concatenate([before_cells, volume, after_cells], axis=2)
    before, after = in_order(*cots)
    incoming = jnp.concatenate([before[:, :, 2:], cotangent, after[:, :, :2]], axis=2).astype(F32)
    sides = [
        jnp.concatenate([below[at], own[at], above[at]], axis=1)
        for at in (slice(5, 8), slice(0, 3))
    ]
    left, right = beside(sides[0], sides[1], "gx", peers[0])
    (middle,) = call(
        middle_kernel,
        [((6, 6, 24, C), F32)],
        [own.reshape(8, 192, C), fine_rows],
        scratch=[((8, 8, 32, C), F32), ((8, 144, 9 * C), BF16)],
        flops=2 * 864 * 27 * C * C,
    )
    across = [own.reshape(8, 192, C), below.reshape(8, 72, C), above.reshape(8, 72, C)]
    (edges,) = call(
        sides_kernel,
        [((6, 6, 24, C), F32)],
        across + [fine_rows],
        scratch=[((8, 10, 32, C), F32), ((8, 144, 9 * C), BF16)],
        flops=2 * 864 * 27 * C * C,
    )
    across = across + [left.reshape(3, 336, C), right.reshape(3, 336, C)]
    coarse, coarse_grad, slope, fine_sum, coarse_sum = call(
        lambda *refs: front_kernel(fine_sizes, coarse_sizes, *refs),
        [
            ((128, C), F32),
            ((128, C), BF16),
            ((12, 12, 24, C), F32),
            ((27 * C, C), BF16),
            ((27 * C, C), BF16),
        ],
        [place, *across, fine_rows, coarse_weight, incoming.reshape(128, C), middle, edges],
        scratch=[
            ((14, 14, 32, C), F32),
            ((10, 288, 9 * C), BF16),
            ((6, 12, 24, C), F32),
            ((6, 24, C), F32),
            ((6, 6, 16, C), F32),
            ((8, 8, 16, C), F32),
            ((6, 6, 16, C), F32),
            ((12, 12, 8, C), F32),
            ((14, 96, 9 * C), BF16),
        ],
        scalars=1,
        flops=2 * 4000 * 27 * C * C,
    )

    first = lax.axis_index("core") == 0
    swap = [(0, 1), (1, 0)]
    cells_fine = fine_sizes[0] * fine_sizes[1] * fine_sizes[2]
    scale = jnp.where(first, 1.0 / math.sqrt(cells_fine), 1.0 / math.sqrt(cells_fine // 8))
    scale = scale.astype(F32).reshape(1)
    mine = jnp.where(first, fine_sum, coarse_sum).astype(F32)
    other = jnp.where(first, coarse_sum, fine_sum)
    mine = mine + lax.ppermute(other, "core", swap).astype(F32)

    grads = coarse_grad.reshape(4, 4, 8, C)
    halo = beside(grads[:, 2:], grads[:, :2], "gy", peers[1])
    coarse_out = jax.nn.silu(coarse.reshape(4, 4, 8, C)[:, :, 2:6]).astype(BF16)
    parts = exchanged(mine.astype(BF16).reshape(plane, -1, C), PLANE)
    parts, halo, coarse_out = lax.optimization_barrier((parts, halo, coarse_out))
    length = parts.shape[1]
    padded = -(-length // (16 * along)) * 16 * along
    (part,) = call(plane_sum_kernel, [((padded, C), BF16)], [parts])
    parts = exchanged(part.reshape(along, padded // along, C), LINE)
    (parts,) = call(line_sum_kernel, [(parts.shape, BF16)], [scale, parts], scalars=1)
    parts = exchanged(parts, LINE)
    parts, halo = lax.optimization_barrier((parts, halo))
    part = joined(parts)[:length]
    grads = jnp.concatenate([halo[0], grads, halo[1]], axis=1)
    halo = beside(grads[2:], grads[:2], "gx", peers[0])
    (fine_grad,) = call(
        fine_grad_kernel,
        [((10, 10, 16, C), F32)],
        [
            halo[0].reshape(128, C),
            grads.reshape(256, C),
            halo[1].reshape(128, C),
            coarse_weight,
            slope,
        ],
        scratch=[((8, 8, 16, C), F32), ((6, 6, 16, C), F32)],
        flops=2 * 288 * 27 * C * C,
    )
    parts = exchanged(jnp.broadcast_to(part[None], (plane, length, C)), PLANE)
    parts, fine_grad = lax.optimization_barrier((parts, fine_grad))
    (grad_volume,) = call(
        volume_kernel,
        [((512, C), BF16)],
        [fine_grad, fine_rows],
        flops=2 * 512 * 27 * C * C,
    )
    mine = joined(parts)
    other = lax.ppermute(mine, "core", swap)
    fine_done = jnp.where(first, mine, other)
    coarse_done = jnp.where(first, other, mine)
    return (
        coarse_out,
        grad_volume.reshape(8, 8, 8, C),
        fine_done.reshape(27, C, C),
        coarse_done.reshape(27, C, C),
    )


def solution(mesh):
    shape = mesh.devices.shape
    inner = Mesh(mesh.devices.reshape(shape[0], shape[1], shape[2] // 4, 2, 2), AXES)
    cells = P("gx", "gy", WIDTH, None)
    return jax.shard_map(
        local,
        mesh=inner,
        in_specs=(cells, P(), P(), cells),
        out_specs=(cells, cells, P(), P()),
        check_vma=False,
    )
```

```python
import math

import jax
import jax.numpy as jnp
from jax import lax
from jax.experimental import pallas as pl
from jax.experimental.pallas import tpu as pltpu
from jax.sharding import Mesh, PartitionSpec as P

AXES = ("gx", "gy", "y", "zh", "core")
WIDTH = ("y", "zh", "core")
PLANE = ("gx", "y")
LINE = ("gy", "zh")
C = 128
F32 = jnp.float32
BF16 = jnp.bfloat16


def silu_slope(values):
    sigma = 1.0 / (1.0 + jnp.exp(-values))
    return sigma * (1.0 + values * (1.0 - sigma))


def inside(shape, starts, sizes):
    keep = None
    for dim in range(3):
        at = starts[dim] + lax.broadcasted_iota(jnp.int32, shape, dim)
        ok = (at >= 0) & (at < sizes[dim])
        keep = ok if keep is None else keep & ok
    return keep


def taps():
    return [(i, j, k) for i in range(3) for j in range(3) for k in range(3)]


def flat(values):
    return values.reshape(-1, C).astype(BF16)


def weight_terms(turned, cells, sum_ref, at):
    terms = jnp.dot(turned, cells, preferred_element_type=F32)
    for t in range(9):
        row = (at + t) * C
        sum_ref[row : row + C] = terms[:, t * C : (t + 1) * C].T.astype(BF16)


def back_conv(grads, weights):
    cells = jnp.concatenate(
        [flat(grads[2 - i : 8 - i, 2 - j : 8 - j, 2 - k : 10 - k]) for i, j, k in taps()], axis=1
    )
    turned = jnp.concatenate([weights[t] for t in range(27)], axis=1)
    back = lax.dot_general(cells, turned, (((1,), (1,)), ((), ())), preferred_element_type=F32)
    return back.reshape(6, 6, 8, C)


def gather(wide, patches, planes, columns=12):
    def plane(x, carry):
        for k in range(3):
            line = wide[x, :, 1 + k : 25 + k]
            for j in range(3):
                at = (3 * j + k) * C
                patches[x, :, at : at + C] = flat(line[j : j + columns])
        return carry

    lax.fori_loop(0, planes, plane, 0)


def fine_conv(patches, weights, at, planes, columns=12):
    rows = planes * columns * 24
    total = jnp.zeros((rows, C), F32)
    for i in range(3):
        cells = patches[pl.ds(at + i, planes)].reshape(rows, 9 * C)
        total = total + jnp.dot(
            cells, weights[9 * C * i : 9 * C * (i + 1)], preferred_element_type=F32
        )
    return total.reshape(planes, columns, 24, C)


def fill(wide, at, x, own, below, above):
    wide[at, 3:11, :24] = own[x].astype(F32).reshape(8, 24, C)
    wide[at, :3, :24] = below[x].astype(F32).reshape(3, 24, C)
    wide[at, 11:, :24] = above[x].astype(F32).reshape(3, 24, C)


def middle_kernel(own, weights, hidden_ref, wide, patches):
    for x in range(8):
        wide[x, :, :24] = own[x].astype(F32).reshape(8, 24, C)
    gather(wide, patches, 8, 6)
    hidden_ref[...] = fine_conv(patches, weights, 0, 6, 6)


def sides_kernel(own, below, above, weights, hidden_ref, wide, patches):
    for x in range(8):
        rows = own[x].astype(F32).reshape(8, 24, C)
        wide[x, :3, :24] = below[x].astype(F32).reshape(3, 24, C)
        wide[x, 3:5, :24] = rows[:2]
        wide[x, 5:7, :24] = rows[6:]
        wide[x, 7:, :24] = above[x].astype(F32).reshape(3, 24, C)

    def plane(x, carry):
        for k in range(3):
            line = wide[x, :, 1 + k : 25 + k]
            for j in range(3):
                at = (3 * j + k) * C
                cells = jnp.concatenate([line[j : j + 3], line[5 + j : 8 + j]], axis=0)
                patches[x, :, at : at + C] = flat(cells)
        return carry

    lax.fori_loop(0, 8, plane, 0)
    hidden_ref[...] = fine_conv(patches, weights, 0, 6, 6)


def front_kernel(
    fine_sizes, coarse_sizes, place, own, below, above, left, right, weights, coarse_weights, incoming,
    middle, sides,
    coarse_ref, grad_ref, slope_ref, fine_ref, coarse_sum_ref,
    wide, patches, outer, pairs, pooled, grads, spread, shares, near,
):
    order = [0, 1, 2, 3, 4, 10, 11, 12, 13, 5, 6, 7, 8, 9]
    for x in range(3):
        wide[x, :, :24] = left[x].astype(F32).reshape(14, 24, C)
        wide[order[11 + x], :, :24] = right[x].astype(F32).reshape(14, 24, C)
    for x in range(8):
        fill(wide, order[3 + x], x, own, below, above)
    gather(wide, patches, 10)
    for part in range(2):
        outer[3 * part : 3 * part + 3] = fine_conv(patches, weights, 5 * part, 3)

    for x in range(6):
        active = None
        for at in (2 * x, 2 * x + 1):
            if 3 <= at < 9:
                edges = sides[at - 3]
                value = jnp.concatenate([edges[:3], middle[at - 3], edges[3:]], axis=0)
            else:
                value = outer[at if at < 3 else at - 6]
            sigma = 1.0 / (1.0 + jnp.exp(-value))
            slope = sigma * (1.0 + value * (1.0 - sigma)) * 0.125
            starts = [8 * place[0] - 2 + at, 8 * place[1] - 2, 8 * place[2] - 6]
            keep = inside((1, 12, 24, C), starts, fine_sizes)[0]
            slope_ref[at] = jnp.where(keep, slope, 0.0)
            value = value * sigma
            active = value if active is None else active + value
        active = active.reshape(6, 2, 24, C)
        pairs[...] = active[:, 0] + active[:, 1]
        mean = (pairs[:, pl.ds(0, 12, 2)] + pairs[:, pl.ds(1, 12, 2)]) * 0.125
        starts = [4 * place[0] - 1 + x, 4 * place[1] - 1, 4 * place[2] - 3]
        keep = inside((1, 6, 12, C), starts, coarse_sizes)[0]
        pooled[x, :, :12] = jnp.where(keep, mean, 0.0)
        pooled[x, :, 12:] = jnp.zeros((6, 4, C), F32)

    cells = [flat(pooled[i : i + 4, j : j + 4, k : k + 8]) for i, j, k in taps()]
    coarse = jnp.dot(
        jnp.concatenate(cells, axis=1),
        coarse_weights[...].reshape(27 * C, C),
        preferred_element_type=F32,
    )
    coarse_ref[...] = coarse
    grad = (incoming[...] * silu_slope(coarse)).astype(BF16)
    grad_ref[...] = grad
    grad = grad.astype(F32)

    grads[...] = jnp.zeros((8, 8, 16, C), F32)
    grads[2:6, 2:6, :8] = grad.reshape(4, 4, 8, C)
    back = back_conv(grads, coarse_weights)
    spread[:, :, pl.ds(0, 8, 2)] = back
    spread[:, :, pl.ds(1, 8, 2)] = back
    for x in range(12):
        for y in range(12):
            shares[x, y] = spread[x // 2, y // 2, 2:10] * slope_ref[x, y, 6:14]
    turned = shares[...].reshape(1152, C).T.astype(BF16)
    for x in range(14):
        for k in range(3):
            line = wide[order[x], :, 7 + k : 15 + k]
            for j in range(3):
                at = (3 * j + k) * C
                near[x, :, at : at + C] = flat(line[j : j + 12])
    for i in range(3):
        weight_terms(turned, near[i : i + 12].reshape(1152, 9 * C), fine_ref, 9 * i)

    at = lax.broadcasted_iota(jnp.int32, (C, C), 0) % 8
    turned = jnp.where((at >= 2) & (at < 6), grad, 0.0).T.astype(BF16)
    for i in range(3):
        weight_terms(
            turned, jnp.concatenate(cells[9 * i : 9 * i + 9], axis=1), coarse_sum_ref, 9 * i
        )


def fine_grad_kernel(left, middle, right, coarse_weights, slope, fine_ref, grads, spread):
    for x in range(2):
        for at, part in ((x, left), (6 + x, right)):
            grads[at, :, :8] = part[64 * x : 64 * x + 64].astype(F32).reshape(8, 8, C)
    for x in range(4):
        grads[2 + x, :, :8] = middle[64 * x : 64 * x + 64].astype(F32).reshape(8, 8, C)
    back = back_conv(grads, coarse_weights)
    spread[:, :, pl.ds(0, 8, 2)] = back
    spread[:, :, pl.ds(1, 8, 2)] = back
    for x in range(10):
        for y in range(10):
            fine_ref[x, y] = spread[(x + 1) // 2, (y + 1) // 2] * slope[x + 1, y + 1, 4:20]


def volume_kernel(fine, weights, out_ref):
    total = jnp.zeros((512, C), F32)
    for i in range(3):
        cells = jnp.concatenate(
            [
                flat(fine[2 - i : 10 - i, 2 - j : 10 - j, 3 - k : 11 - k])
                for j in range(3)
                for k in range(3)
            ],
            axis=1,
        )
        turned = jnp.concatenate(
            [weights[(9 * i + t) * C : (9 * i + t + 1) * C] for t in range(9)], axis=1
        )
        total = total + lax.dot_general(
            cells, turned, (((1,), (1,)), ((), ())), preferred_element_type=F32
        )
    out_ref[...] = total.astype(BF16)


def plane_sum_kernel(parts, out_ref):
    total = parts[0].astype(F32)
    for at in range(1, parts.shape[0]):
        total = total + parts[at].astype(F32)
    rows = out_ref.shape[0] - total.shape[0]
    out_ref[...] = jnp.concatenate([total, jnp.zeros((rows, C), F32)], axis=0).astype(BF16)


def line_sum_kernel(scale, parts, out_ref):
    total = parts[0].astype(F32)
    for at in range(1, parts.shape[0]):
        total = total + parts[at].astype(F32)
    total = (total * scale[0]).astype(BF16)
    for at in range(out_ref.shape[0]):
        out_ref[at] = total


def call(kernel, outs, inputs, scratch=(), scalars=0, flops=0):
    in_specs = [
        pl.BlockSpec(memory_space=pltpu.SMEM if n < scalars else pltpu.VMEM)
        for n in range(len(inputs))
    ]
    moved = sum(a.size * a.dtype.itemsize for a in inputs)
    moved += sum(math.prod(s) * jnp.dtype(t).itemsize for s, t in outs)
    return pl.pallas_call(
        kernel,
        out_shape=[jax.ShapeDtypeStruct(s, t) for s, t in outs],
        in_specs=in_specs,
        out_specs=[pl.BlockSpec(memory_space=pltpu.VMEM) for _ in outs],
        scratch_shapes=[pltpu.VMEM(s, t) for s, t in scratch],
        compiler_params=pltpu.CompilerParams(vmem_limit_bytes=28 * 1024 * 1024),
        cost_estimate=pl.CostEstimate(flops=flops, bytes_accessed=moved, transcendentals=0),
    )(*inputs)


def line(count, step):
    return [(i, i + step) for i in range(count) if 0 <= i + step < count]


def beside(last, leading, axis, count):
    before = lax.ppermute(last, axis, line(count, 1))
    after = lax.ppermute(leading, axis, line(count, -1))
    return before, after


def along_width(x, count):
    outer = lax.ppermute(x, WIDTH, [(i, i - 1 + 2 * (i % 2)) for i in range(1, count - 1)])
    inner = lax.ppermute(x, WIDTH, [(i, i ^ 1) for i in range(count)])
    return outer, inner


def in_order(outer, inner):
    first = lax.axis_index("core") == 0
    return jnp.where(first, outer, inner), jnp.where(first, inner, outer)


def exchanged(parts, axes):
    return lax.all_to_all(parts, axes, 0, 0, tiled=True)


def joined(parts):
    return parts.reshape(-1, C)


def local(volume, fine_weight, coarse_weight, cotangent):
    sizes = {axis: lax.axis_size(axis) for axis in AXES}
    plane, along = (sizes["gx"] * sizes["y"], sizes["gy"] * sizes["zh"])
    peers = [sizes["gx"], sizes["gy"], sizes["y"] * sizes["zh"] * 2]
    place = [lax.axis_index(axis) for axis in ("gx", "gy", WIDTH)]
    place = jnp.stack([p.astype(jnp.int32) for p in place])
    fine_sizes = [8 * n for n in peers]
    coarse_sizes = [4 * n for n in peers]

    fine_rows = fine_weight.reshape(27 * C, C)

    halo = along_width(volume, peers[2])
    cots = along_width(cotangent, peers[2])
    before_cells, after_cells = in_order(*halo)
    slabs = [
        jnp.concatenate([before_cells[:, at], volume[:, at], after_cells[:, at]], axis=2)
        for at in (slice(5, 8), slice(0, 3))
    ]
    below, above = beside(slabs[0], slabs[1], "gy", peers[1])
    (below, above), cots = lax.optimization_barrier(((below, above), cots))
    own = jnp.concatenate([before_cells, volume, after_cells], axis=2)
    before, after = in_order(*cots)
    incoming = jnp.concatenate([before[:, :, 2:], cotangent, after[:, :, :2]], axis=2).astype(F32)
    sides = [
        jnp.concatenate([below[at], own[at], above[at]], axis=1)
        for at in (slice(5, 8), slice(0, 3))
    ]
    left, right = beside(sides[0], sides[1], "gx", peers[0])
    (middle,) = call(
        middle_kernel,
        [((6, 6, 24, C), F32)],
        [own.reshape(8, 192, C), fine_rows],
        scratch=[((8, 8, 32, C), F32), ((8, 144, 9 * C), BF16)],
        flops=2 * 864 * 27 * C * C,
    )
    across = [own.reshape(8, 192, C), below.reshape(8, 72, C), above.reshape(8, 72, C)]
    (edges,) = call(
        sides_kernel,
        [((6, 6, 24, C), F32)],
        across + [fine_rows],
        scratch=[((8, 10, 32, C), F32), ((8, 144, 9 * C), BF16)],
        flops=2 * 864 * 27 * C * C,
    )
    across = across + [left.reshape(3, 336, C), right.reshape(3, 336, C)]
    coarse, coarse_grad, slope, fine_sum, coarse_sum = call(
        lambda *refs: front_kernel(fine_sizes, coarse_sizes, *refs),
        [
            ((128, C), F32),
            ((128, C), BF16),
            ((12, 12, 24, C), F32),
            ((27 * C, C), BF16),
            ((27 * C, C), BF16),
        ],
        [place, *across, fine_rows, coarse_weight, incoming.reshape(128, C), middle, edges],
        scratch=[
            ((14, 14, 32, C), F32),
            ((10, 288, 9 * C), BF16),
            ((6, 12, 24, C), F32),
            ((6, 24, C), F32),
            ((6, 6, 16, C), F32),
            ((8, 8, 16, C), F32),
            ((6, 6, 16, C), F32),
            ((12, 12, 8, C), F32),
            ((14, 96, 9 * C), BF16),
        ],
        scalars=1,
        flops=2 * 4000 * 27 * C * C,
    )

    first = lax.axis_index("core") == 0
    swap = [(0, 1), (1, 0)]
    cells_fine = fine_sizes[0] * fine_sizes[1] * fine_sizes[2]
    scale = jnp.where(first, 1.0 / math.sqrt(cells_fine), 1.0 / math.sqrt(cells_fine // 8))
    scale = scale.astype(F32).reshape(1)
    mine = jnp.where(first, fine_sum, coarse_sum).astype(F32)
    other = jnp.where(first, coarse_sum, fine_sum)
    mine = mine + lax.ppermute(other, "core", swap).astype(F32)

    grads = coarse_grad.reshape(4, 4, 8, C)
    halo = beside(grads[:, 2:], grads[:, :2], "gy", peers[1])
    coarse_out = jax.nn.silu(coarse.reshape(4, 4, 8, C)[:, :, 2:6]).astype(BF16)
    parts = exchanged(mine.astype(BF16).reshape(plane, -1, C), PLANE)
    parts, halo, coarse_out = lax.optimization_barrier((parts, halo, coarse_out))
    length = parts.shape[1]
    padded = -(-length // (16 * along)) * 16 * along
    (part,) = call(plane_sum_kernel, [((padded, C), BF16)], [parts])
    parts = exchanged(part.reshape(along, padded // along, C), LINE)
    (parts,) = call(line_sum_kernel, [(parts.shape, BF16)], [scale, parts], scalars=1)
    parts = exchanged(parts, LINE)
    parts, halo = lax.optimization_barrier((parts, halo))
    part = joined(parts)[:length]
    grads = jnp.concatenate([halo[0], grads, halo[1]], axis=1)
    halo = beside(grads[2:], grads[:2], "gx", peers[0])
    (fine_grad,) = call(
        fine_grad_kernel,
        [((10, 10, 16, C), F32)],
        [
            halo[0].reshape(128, C),
            grads.reshape(256, C),
            halo[1].reshape(128, C),
            coarse_weight,
            slope,
        ],
        scratch=[((8, 8, 16, C), F32), ((6, 6, 16, C), F32)],
        flops=2 * 288 * 27 * C * C,
    )
    parts = exchanged(jnp.broadcast_to(part[None], (plane, length, C)), PLANE)
    parts, fine_grad = lax.optimization_barrier((parts, fine_grad))
    (grad_volume,) = call(
        volume_kernel,
        [((512, C), BF16)],
        [fine_grad, fine_rows],
        flops=2 * 512 * 27 * C * C,
    )
    mine = joined(parts)
    other = lax.ppermute(mine, "core", swap)
    fine_done = jnp.where(first, mine, other)
    coarse_done = jnp.where(first, other, mine)
    return (
        coarse_out,
        grad_volume.reshape(8, 8, 8, C),
        fine_done.reshape(27, C, C),
        coarse_done.reshape(27, C, C),
    )


def solution(mesh):
    shape = mesh.devices.shape
    inner = Mesh(mesh.devices.reshape(shape[0], shape[1], shape[2] // 4, 2, 2), AXES)
    cells = P("gx", "gy", WIDTH, None)
    return jax.shard_map(
        local,
        mesh=inner,
        in_specs=(cells, P(), P(), cells),
        out_specs=(cells, cells, P(), P()),
        check_vma=False,
    )
```

```python
import math

import jax
import jax.numpy as jnp
from jax import lax
from jax.experimental import pallas as pl
from jax.experimental.pallas import tpu as pltpu
from jax.sharding import Mesh, PartitionSpec as P

AXES = ("gx", "gy", "y", "zh", "core")
WIDTH = ("y", "zh", "core")
PLANE = ("gx", "y")
LINE = ("gy", "zh")
C = 128
F32 = jnp.float32
BF16 = jnp.bfloat16


def silu_slope(values):
    sigma = 1.0 / (1.0 + jnp.exp(-values))
    return sigma * (1.0 + values * (1.0 - sigma))


def inside(shape, starts, sizes):
    keep = None
    for dim in range(3):
        at = starts[dim] + lax.broadcasted_iota(jnp.int32, shape, dim)
        ok = (at >= 0) & (at < sizes[dim])
        keep = ok if keep is None else keep & ok
    return keep


def taps():
    return [(i, j, k) for i in range(3) for j in range(3) for k in range(3)]


def flat(values):
    return values.reshape(-1, C).astype(BF16)


def weight_terms(turned, cells, sum_ref, at):
    terms = jnp.dot(turned, cells, preferred_element_type=F32)
    for t in range(9):
        row = (at + t) * C
        sum_ref[row : row + C] = terms[:, t * C : (t + 1) * C].T.astype(BF16)


def back_conv(grads, weights):
    cells = jnp.concatenate(
        [flat(grads[2 - i : 8 - i, 2 - j : 8 - j, 2 - k : 10 - k]) for i, j, k in taps()], axis=1
    )
    turned = jnp.concatenate([weights[t] for t in range(27)], axis=1)
    back = lax.dot_general(cells, turned, (((1,), (1,)), ((), ())), preferred_element_type=F32)
    return back.reshape(6, 6, 8, C)


def gather(wide, patches, planes, columns=12):
    def plane(x, carry):
        for k in range(3):
            line = wide[x, :, 1 + k : 25 + k]
            for j in range(3):
                at = (3 * j + k) * C
                patches[x, :, at : at + C] = flat(line[j : j + columns])
        return carry

    lax.fori_loop(0, planes, plane, 0)


def fine_conv(patches, weights, at, planes, columns=12):
    rows = planes * columns * 24
    total = jnp.zeros((rows, C), F32)
    for i in range(3):
        cells = patches[pl.ds(at + i, planes)].reshape(rows, 9 * C)
        total = total + jnp.dot(
            cells, weights[9 * C * i : 9 * C * (i + 1)], preferred_element_type=F32
        )
    return total.reshape(planes, columns, 24, C)


def fill(wide, at, x, own, below, above):
    wide[at, 3:11, :24] = own[x].astype(F32).reshape(8, 24, C)
    wide[at, :3, :24] = below[x].astype(F32).reshape(3, 24, C)
    wide[at, 11:, :24] = above[x].astype(F32).reshape(3, 24, C)


def middle_kernel(own, weights, hidden_ref, wide, patches):
    for x in range(8):
        wide[x, :, :24] = own[x].astype(F32).reshape(8, 24, C)
    gather(wide, patches, 8, 6)
    hidden_ref[...] = fine_conv(patches, weights, 0, 6, 6)


def sides_kernel(own, below, above, weights, hidden_ref, wide, patches):
    for x in range(8):
        rows = own[x].astype(F32).reshape(8, 24, C)
        wide[x, :3, :24] = below[x].astype(F32).reshape(3, 24, C)
        wide[x, 3:5, :24] = rows[:2]
        wide[x, 5:7, :24] = rows[6:]
        wide[x, 7:, :24] = above[x].astype(F32).reshape(3, 24, C)

    def plane(x, carry):
        for k in range(3):
            line = wide[x, :, 1 + k : 25 + k]
            for j in range(3):
                at = (3 * j + k) * C
                cells = jnp.concatenate([line[j : j + 3], line[5 + j : 8 + j]], axis=0)
                patches[x, :, at : at + C] = flat(cells)
        return carry

    lax.fori_loop(0, 8, plane, 0)
    hidden_ref[...] = fine_conv(patches, weights, 0, 6, 6)


def front_kernel(
    fine_sizes, coarse_sizes, place, own, below, above, left, right, weights, coarse_weights, incoming,
    middle, sides,
    coarse_ref, grad_ref, slope_ref, fine_ref, coarse_sum_ref,
    wide, patches, outer, pairs, pooled, grads, spread, shares, near,
):
    order = [0, 1, 2, 3, 4, 10, 11, 12, 13, 5, 6, 7, 8, 9]
    for x in range(3):
        wide[x, :, :24] = left[x].astype(F32).reshape(14, 24, C)
        wide[order[11 + x], :, :24] = right[x].astype(F32).reshape(14, 24, C)
    for x in range(8):
        fill(wide, order[3 + x], x, own, below, above)
    gather(wide, patches, 10)
    for part in range(2):
        outer[3 * part : 3 * part + 3] = fine_conv(patches, weights, 5 * part, 3)

    for x in range(6):
        active = None
        for at in (2 * x, 2 * x + 1):
            if 3 <= at < 9:
                edges = sides[at - 3]
                value = jnp.concatenate([edges[:3], middle[at - 3], edges[3:]], axis=0)
            else:
                value = outer[at if at < 3 else at - 6]
            sigma = 1.0 / (1.0 + jnp.exp(-value))
            slope = sigma * (1.0 + value * (1.0 - sigma)) * 0.125
            starts = [8 * place[0] - 2 + at, 8 * place[1] - 2, 8 * place[2] - 6]
            keep = inside((1, 12, 24, C), starts, fine_sizes)[0]
            slope_ref[at] = jnp.where(keep, slope, 0.0)
            value = value * sigma
            active = value if active is None else active + value
        active = active.reshape(6, 2, 24, C)
        pairs[...] = active[:, 0] + active[:, 1]
        mean = (pairs[:, pl.ds(0, 12, 2)] + pairs[:, pl.ds(1, 12, 2)]) * 0.125
        starts = [4 * place[0] - 1 + x, 4 * place[1] - 1, 4 * place[2] - 3]
        keep = inside((1, 6, 12, C), starts, coarse_sizes)[0]
        pooled[x, :, :12] = jnp.where(keep, mean, 0.0)
        pooled[x, :, 12:] = jnp.zeros((6, 4, C), F32)

    cells = [flat(pooled[i : i + 4, j : j + 4, k : k + 8]) for i, j, k in taps()]
    coarse = jnp.dot(
        jnp.concatenate(cells, axis=1),
        coarse_weights[...].reshape(27 * C, C),
        preferred_element_type=F32,
    )
    coarse_ref[...] = coarse
    grad = (incoming[...] * silu_slope(coarse)).astype(BF16)
    grad_ref[...] = grad
    grad = grad.astype(F32)

    grads[...] = jnp.zeros((8, 8, 16, C), F32)
    grads[2:6, 2:6, :8] = grad.reshape(4, 4, 8, C)
    back = back_conv(grads, coarse_weights)
    spread[:, :, pl.ds(0, 8, 2)] = back
    spread[:, :, pl.ds(1, 8, 2)] = back
    for x in range(12):
        for y in range(12):
            shares[x, y] = spread[x // 2, y // 2, 2:10] * slope_ref[x, y, 6:14]
    turned = shares[...].reshape(1152, C).T.astype(BF16)
    for x in range(14):
        for k in range(3):
            line = wide[order[x], :, 7 + k : 15 + k]
            for j in range(3):
                at = (3 * j + k) * C
                near[x, :, at : at + C] = flat(line[j : j + 12])
    for i in range(3):
        weight_terms(turned, near[i : i + 12].reshape(1152, 9 * C), fine_ref, 9 * i)

    at = lax.broadcasted_iota(jnp.int32, (C, C), 0) % 8
    turned = jnp.where((at >= 2) & (at < 6), grad, 0.0).T.astype(BF16)
    for i in range(3):
        weight_terms(
            turned, jnp.concatenate(cells[9 * i : 9 * i + 9], axis=1), coarse_sum_ref, 9 * i
        )


def fine_grad_kernel(left, middle, right, coarse_weights, slope, weights, fine_ref, begun_ref, grads, spread):
    for x in range(2):
        for at, part in ((x, left), (6 + x, right)):
            grads[at, :, :8] = part[64 * x : 64 * x + 64].astype(F32).reshape(8, 8, C)
    for x in range(4):
        grads[2 + x, :, :8] = middle[64 * x : 64 * x + 64].astype(F32).reshape(8, 8, C)
    back = back_conv(grads, coarse_weights)
    spread[:, :, pl.ds(0, 8, 2)] = back
    spread[:, :, pl.ds(1, 8, 2)] = back
    for x in range(10):
        for y in range(10):
            fine_ref[x, y] = spread[(x + 1) // 2, (y + 1) // 2] * slope[x + 1, y + 1, 4:20]
    begun_ref[...] = volume_terms(fine_ref, weights, 0)


def volume_terms(fine, weights, i):
    cells = jnp.concatenate(
        [
            flat(fine[2 - i : 10 - i, 2 - j : 10 - j, 3 - k : 11 - k])
            for j in range(3)
            for k in range(3)
        ],
        axis=1,
    )
    turned = jnp.concatenate([weights[9 * i + t] for t in range(9)], axis=1)
    return lax.dot_general(cells, turned, (((1,), (1,)), ((), ())), preferred_element_type=F32)


def volume_kernel(fine, begun, weights, out_ref):
    total = begun[...] + volume_terms(fine, weights, 1) + volume_terms(fine, weights, 2)
    out_ref[...] = total.astype(BF16)


def plane_sum_kernel(parts, out_ref):
    total = parts[0].astype(F32)
    for at in range(1, parts.shape[0]):
        total = total + parts[at].astype(F32)
    rows = out_ref.shape[0] - total.shape[0]
    out_ref[...] = jnp.concatenate([total, jnp.zeros((rows, C), F32)], axis=0).astype(BF16)


def line_sum_kernel(scale, parts, out_ref):
    total = parts[0].astype(F32)
    for at in range(1, parts.shape[0]):
        total = total + parts[at].astype(F32)
    total = (total * scale[0]).astype(BF16)
    for at in range(out_ref.shape[0]):
        out_ref[at] = total


def call(kernel, outs, inputs, scratch=(), scalars=0, flops=0):
    in_specs = [
        pl.BlockSpec(memory_space=pltpu.SMEM if n < scalars else pltpu.VMEM)
        for n in range(len(inputs))
    ]
    moved = sum(a.size * a.dtype.itemsize for a in inputs)
    moved += sum(math.prod(s) * jnp.dtype(t).itemsize for s, t in outs)
    return pl.pallas_call(
        kernel,
        out_shape=[jax.ShapeDtypeStruct(s, t) for s, t in outs],
        in_specs=in_specs,
        out_specs=[pl.BlockSpec(memory_space=pltpu.VMEM) for _ in outs],
        scratch_shapes=[pltpu.VMEM(s, t) for s, t in scratch],
        compiler_params=pltpu.CompilerParams(vmem_limit_bytes=40 * 1024 * 1024),
        cost_estimate=pl.CostEstimate(flops=flops, bytes_accessed=moved, transcendentals=0),
    )(*inputs)


def line(count, step):
    return [(i, i + step) for i in range(count) if 0 <= i + step < count]


def beside(last, leading, axis, count):
    before = lax.ppermute(last, axis, line(count, 1))
    after = lax.ppermute(leading, axis, line(count, -1))
    return before, after


def along_width(x, count):
    outer = lax.ppermute(x, WIDTH, [(i, i - 1 + 2 * (i % 2)) for i in range(1, count - 1)])
    inner = lax.ppermute(x, WIDTH, [(i, i ^ 1) for i in range(count)])
    return outer, inner


def in_order(outer, inner):
    first = lax.axis_index("core") == 0
    return jnp.where(first, outer, inner), jnp.where(first, inner, outer)


def exchanged(parts, axes):
    return lax.all_to_all(parts, axes, 0, 0, tiled=True)


def joined(parts):
    return parts.reshape(-1, C)


def local(volume, fine_weight, coarse_weight, cotangent):
    sizes = {axis: lax.axis_size(axis) for axis in AXES}
    plane, along = (sizes["gx"] * sizes["y"], sizes["gy"] * sizes["zh"])
    peers = [sizes["gx"], sizes["gy"], sizes["y"] * sizes["zh"] * 2]
    place = [lax.axis_index(axis) for axis in ("gx", "gy", WIDTH)]
    place = jnp.stack([p.astype(jnp.int32) for p in place])
    fine_sizes = [8 * n for n in peers]
    coarse_sizes = [4 * n for n in peers]

    fine_rows = fine_weight.reshape(27 * C, C)

    packed = jnp.concatenate([volume.reshape(512, C), cotangent.reshape(64, C)], axis=0)
    before, after = in_order(*along_width(packed, peers[2]))
    before_cells, after_cells = (b[:512].reshape(8, 8, 8, C) for b in (before, after))
    slabs = [
        jnp.concatenate([before_cells[:, at], volume[:, at], after_cells[:, at]], axis=2)
        for at in (slice(5, 8), slice(0, 3))
    ]
    below, above = beside(slabs[0], slabs[1], "gy", peers[1])
    own = jnp.concatenate([before_cells, volume, after_cells], axis=2)
    incoming = jnp.concatenate(
        [
            before[512:].reshape(4, 4, 4, C)[:, :, 2:],
            cotangent,
            after[512:].reshape(4, 4, 4, C)[:, :, :2],
        ],
        axis=2,
    ).astype(F32)
    sides = [
        jnp.concatenate([below[at], own[at], above[at]], axis=1)
        for at in (slice(5, 8), slice(0, 3))
    ]
    left, right = beside(sides[0], sides[1], "gx", peers[0])
    (middle,) = call(
        middle_kernel,
        [((6, 6, 24, C), F32)],
        [own.reshape(8, 192, C), fine_rows],
        scratch=[((8, 8, 32, C), F32), ((8, 144, 9 * C), BF16)],
        flops=2 * 864 * 27 * C * C,
    )
    across = [own.reshape(8, 192, C), below.reshape(8, 72, C), above.reshape(8, 72, C)]
    (edges,) = call(
        sides_kernel,
        [((6, 6, 24, C), F32)],
        across + [fine_rows],
        scratch=[((8, 10, 32, C), F32), ((8, 144, 9 * C), BF16)],
        flops=2 * 864 * 27 * C * C,
    )
    across = across + [left.reshape(3, 336, C), right.reshape(3, 336, C)]
    coarse, coarse_grad, slope, fine_sum, coarse_sum = call(
        lambda *refs: front_kernel(fine_sizes, coarse_sizes, *refs),
        [
            ((128, C), F32),
            ((128, C), BF16),
            ((12, 12, 24, C), F32),
            ((27 * C, C), BF16),
            ((27 * C, C), BF16),
        ],
        [place, *across, fine_rows, coarse_weight, incoming.reshape(128, C), middle, edges],
        scratch=[
            ((14, 14, 32, C), F32),
            ((10, 288, 9 * C), BF16),
            ((6, 12, 24, C), F32),
            ((6, 24, C), F32),
            ((6, 6, 16, C), F32),
            ((8, 8, 16, C), F32),
            ((6, 6, 16, C), F32),
            ((12, 12, 8, C), F32),
            ((14, 96, 9 * C), BF16),
        ],
        scalars=1,
        flops=2 * 4000 * 27 * C * C,
    )

    first = lax.axis_index("core") == 0
    swap = [(0, 1), (1, 0)]
    cells_fine = fine_sizes[0] * fine_sizes[1] * fine_sizes[2]
    scale = jnp.where(first, 1.0 / math.sqrt(cells_fine), 1.0 / math.sqrt(cells_fine // 8))
    scale = scale.astype(F32).reshape(1)
    mine = jnp.where(first, fine_sum, coarse_sum).astype(F32)
    other = jnp.where(first, coarse_sum, fine_sum)
    mine = mine + lax.ppermute(other, "core", swap).astype(F32)

    grads = coarse_grad.reshape(4, 4, 8, C)
    halo = beside(grads[:, 2:], grads[:, :2], "gy", peers[1])
    coarse_out = jax.nn.silu(coarse.reshape(4, 4, 8, C)[:, :, 2:6]).astype(BF16)
    parts = exchanged(mine.astype(BF16).reshape(plane, -1, C), PLANE)
    parts, halo, coarse_out = lax.optimization_barrier((parts, halo, coarse_out))
    length = parts.shape[1]
    padded = -(-length // (16 * along)) * 16 * along
    (part,) = call(plane_sum_kernel, [((padded, C), BF16)], [parts])
    parts = exchanged(part.reshape(along, padded // along, C), LINE)
    (parts,) = call(line_sum_kernel, [(parts.shape, BF16)], [scale, parts], scalars=1)
    parts = exchanged(parts, LINE)
    parts, halo = lax.optimization_barrier((parts, halo))
    part = joined(parts)[:length]
    grads = jnp.concatenate([halo[0], grads, halo[1]], axis=1)
    halo = beside(grads[2:], grads[:2], "gx", peers[0])
    fine_grad, begun = call(
        fine_grad_kernel,
        [((10, 10, 16, C), F32), ((512, C), F32)],
        [
            halo[0].reshape(128, C),
            grads.reshape(256, C),
            halo[1].reshape(128, C),
            coarse_weight,
            slope,
            fine_weight,
        ],
        scratch=[((8, 8, 16, C), F32), ((6, 6, 16, C), F32)],
        flops=2 * 460 * 27 * C * C,
    )
    parts = exchanged(jnp.broadcast_to(part[None], (plane, length, C)), PLANE)
    parts, fine_grad, begun = lax.optimization_barrier((parts, fine_grad, begun))
    (grad_volume,) = call(
        volume_kernel,
        [((512, C), BF16)],
        [fine_grad, begun, fine_weight],
        flops=2 * 342 * 27 * C * C,
    )
    mine = joined(parts)
    other = lax.ppermute(mine, "core", swap)
    fine_done = jnp.where(first, mine, other)
    coarse_done = jnp.where(first, other, mine)
    return (
        coarse_out,
        grad_volume.reshape(8, 8, 8, C),
        fine_done.reshape(27, C, C),
        coarse_done.reshape(27, C, C),
    )


def solution(mesh):
    shape = mesh.devices.shape
    inner = Mesh(mesh.devices.reshape(shape[0], shape[1], shape[2] // 4, 2, 2), AXES)
    cells = P("gx", "gy", WIDTH, None)
    return jax.shard_map(
        local,
        mesh=inner,
        in_specs=(cells, P(), P(), cells),
        out_specs=(cells, cells, P(), P()),
        check_vma=False,
    )
```

```python
import math

import jax
import jax.numpy as jnp
from jax import lax
from jax.experimental import pallas as pl
from jax.experimental.pallas import tpu as pltpu
from jax.sharding import Mesh, PartitionSpec as P

AXES = ("gx", "gy", "y", "zh", "core")
WIDTH = ("y", "zh", "core")
PLANE = ("gx", "y")
LINE = ("gy", "zh")
C = 128
F32 = jnp.float32
BF16 = jnp.bfloat16


def silu_slope(values):
    sigma = 1.0 / (1.0 + jnp.exp(-values))
    return sigma * (1.0 + values * (1.0 - sigma))


def inside(shape, starts, sizes):
    keep = None
    for dim in range(3):
        at = starts[dim] + lax.broadcasted_iota(jnp.int32, shape, dim)
        ok = (at >= 0) & (at < sizes[dim])
        keep = ok if keep is None else keep & ok
    return keep


def taps():
    return [(i, j, k) for i in range(3) for j in range(3) for k in range(3)]


def flat(values):
    return values.reshape(-1, C).astype(BF16)


def weight_terms(turned, cells, sum_ref, at):
    terms = jnp.dot(turned, cells, preferred_element_type=F32)
    for t in range(9):
        row = (at + t) * C
        sum_ref[row : row + C] = terms[:, t * C : (t + 1) * C].T.astype(BF16)


def back_conv(grads, weights):
    cells = jnp.concatenate(
        [flat(grads[2 - i : 8 - i, 2 - j : 8 - j, 2 - k : 10 - k]) for i, j, k in taps()], axis=1
    )
    turned = jnp.concatenate([weights[t] for t in range(27)], axis=1)
    back = lax.dot_general(cells, turned, (((1,), (1,)), ((), ())), preferred_element_type=F32)
    return back.reshape(6, 6, 8, C)


def gather(wide, patches, planes, columns=12):
    def plane(x, carry):
        for k in range(3):
            line = wide[x, :, 1 + k : 25 + k]
            for j in range(3):
                at = (3 * j + k) * C
                patches[x, :, at : at + C] = flat(line[j : j + columns])
        return carry

    lax.fori_loop(0, planes, plane, 0)


def fine_conv(patches, weights, at, planes, columns=12):
    rows = planes * columns * 24
    total = jnp.zeros((rows, C), F32)
    for i in range(3):
        cells = patches[pl.ds(at + i, planes)].reshape(rows, 9 * C)
        total = total + jnp.dot(
            cells, weights[9 * C * i : 9 * C * (i + 1)], preferred_element_type=F32
        )
    return total.reshape(planes, columns, 24, C)


def fill(wide, at, x, own, below, above):
    wide[at, 3:11, :24] = own[x].astype(F32).reshape(8, 24, C)
    wide[at, :3, :24] = below[x].astype(F32).reshape(3, 24, C)
    wide[at, 11:, :24] = above[x].astype(F32).reshape(3, 24, C)


def middle_kernel(own, weights, hidden_ref, wide, patches):
    for x in range(8):
        wide[x, :, :24] = own[x].astype(F32).reshape(8, 24, C)
    gather(wide, patches, 8, 6)
    hidden_ref[...] = fine_conv(patches, weights, 0, 6, 6)


def sides_kernel(own, below, above, weights, hidden_ref, wide, patches):
    for x in range(8):
        rows = own[x].astype(F32).reshape(8, 24, C)
        wide[x, :3, :24] = below[x].astype(F32).reshape(3, 24, C)
        wide[x, 3:5, :24] = rows[:2]
        wide[x, 5:7, :24] = rows[6:]
        wide[x, 7:, :24] = above[x].astype(F32).reshape(3, 24, C)

    def plane(x, carry):
        for k in range(3):
            line = wide[x, :, 1 + k : 25 + k]
            for j in range(3):
                at = (3 * j + k) * C
                cells = jnp.concatenate([line[j : j + 3], line[5 + j : 8 + j]], axis=0)
                patches[x, :, at : at + C] = flat(cells)
        return carry

    lax.fori_loop(0, 8, plane, 0)
    hidden_ref[...] = fine_conv(patches, weights, 0, 6, 6)


def front_kernel(
    fine_sizes, coarse_sizes, place, own, below, above, left, right, weights, coarse_weights, incoming,
    middle, sides,
    coarse_ref, grad_ref, slope_ref, fine_ref, coarse_sum_ref,
    wide, patches, outer, pairs, pooled, grads, spread, shares, near,
):
    order = [0, 1, 2, 3, 4, 10, 11, 12, 13, 5, 6, 7, 8, 9]
    for x in range(3):
        wide[x, :, :24] = left[x].astype(F32).reshape(14, 24, C)
        wide[order[11 + x], :, :24] = right[x].astype(F32).reshape(14, 24, C)
    for x in range(8):
        fill(wide, order[3 + x], x, own, below, above)
    gather(wide, patches, 10)
    for part in range(2):
        outer[3 * part : 3 * part + 3] = fine_conv(patches, weights, 5 * part, 3)

    for x in range(6):
        active = None
        for at in (2 * x, 2 * x + 1):
            if 3 <= at < 9:
                edges = sides[at - 3]
                value = jnp.concatenate([edges[:3], middle[at - 3], edges[3:]], axis=0)
            else:
                value = outer[at if at < 3 else at - 6]
            sigma = 1.0 / (1.0 + jnp.exp(-value))
            slope = sigma * (1.0 + value * (1.0 - sigma)) * 0.125
            starts = [8 * place[0] - 2 + at, 8 * place[1] - 2, 8 * place[2] - 6]
            keep = inside((1, 12, 24, C), starts, fine_sizes)[0]
            slope_ref[at] = jnp.where(keep, slope, 0.0)
            value = value * sigma
            active = value if active is None else active + value
        active = active.reshape(6, 2, 24, C)
        pairs[...] = active[:, 0] + active[:, 1]
        mean = (pairs[:, pl.ds(0, 12, 2)] + pairs[:, pl.ds(1, 12, 2)]) * 0.125
        starts = [4 * place[0] - 1 + x, 4 * place[1] - 1, 4 * place[2] - 3]
        keep = inside((1, 6, 12, C), starts, coarse_sizes)[0]
        pooled[x, :, :12] = jnp.where(keep, mean, 0.0)
        pooled[x, :, 12:] = jnp.zeros((6, 4, C), F32)

    cells = [flat(pooled[i : i + 4, j : j + 4, k : k + 8]) for i, j, k in taps()]
    coarse = jnp.dot(
        jnp.concatenate(cells, axis=1),
        coarse_weights[...].reshape(27 * C, C),
        preferred_element_type=F32,
    )
    coarse_ref[...] = coarse
    grad = (incoming[...] * silu_slope(coarse)).astype(BF16)
    grad_ref[...] = grad
    grad = grad.astype(F32)

    grads[...] = jnp.zeros((8, 8, 16, C), F32)
    grads[2:6, 2:6, :8] = grad.reshape(4, 4, 8, C)
    back = back_conv(grads, coarse_weights)
    spread[:, :, pl.ds(0, 8, 2)] = back
    spread[:, :, pl.ds(1, 8, 2)] = back
    for x in range(12):
        for y in range(12):
            shares[x, y] = spread[x // 2, y // 2, 2:10] * slope_ref[x, y, 6:14]
    turned = shares[...].reshape(1152, C).T.astype(BF16)
    for x in range(14):
        for k in range(3):
            line = wide[order[x], :, 7 + k : 15 + k]
            for j in range(3):
                at = (3 * j + k) * C
                near[x, :, at : at + C] = flat(line[j : j + 12])
    for i in range(3):
        weight_terms(turned, near[i : i + 12].reshape(1152, 9 * C), fine_ref, 9 * i)

    at = lax.broadcasted_iota(jnp.int32, (C, C), 0) % 8
    turned = jnp.where((at >= 2) & (at < 6), grad, 0.0).T.astype(BF16)
    for i in range(3):
        weight_terms(
            turned, jnp.concatenate(cells[9 * i : 9 * i + 9], axis=1), coarse_sum_ref, 9 * i
        )


def fine_grad_kernel(left, middle, right, coarse_weights, slope, weights, fine_ref, begun_ref, grads, spread):
    for x in range(2):
        for at, part in ((x, left), (6 + x, right)):
            grads[at, :, :8] = part[64 * x : 64 * x + 64].astype(F32).reshape(8, 8, C)
    for x in range(4):
        grads[2 + x, :, :8] = middle[64 * x : 64 * x + 64].astype(F32).reshape(8, 8, C)
    back = back_conv(grads, coarse_weights)
    spread[:, :, pl.ds(0, 8, 2)] = back
    spread[:, :, pl.ds(1, 8, 2)] = back
    for x in range(10):
        for y in range(10):
            fine_ref[x, y] = spread[(x + 1) // 2, (y + 1) // 2] * slope[x + 1, y + 1, 4:20]
    begun_ref[...] = volume_terms(fine_ref, weights, 0)


def volume_terms(fine, weights, i):
    cells = jnp.concatenate(
        [
            flat(fine[2 - i : 10 - i, 2 - j : 10 - j, 3 - k : 11 - k])
            for j in range(3)
            for k in range(3)
        ],
        axis=1,
    )
    turned = jnp.concatenate([weights[9 * i + t] for t in range(9)], axis=1)
    return lax.dot_general(cells, turned, (((1,), (1,)), ((), ())), preferred_element_type=F32)


def volume_kernel(fine, begun, weights, out_ref):
    total = begun[...] + volume_terms(fine, weights, 1) + volume_terms(fine, weights, 2)
    out_ref[...] = total.astype(BF16)


def plane_sum_kernel(parts, out_ref):
    total = parts[0].astype(F32)
    for at in range(1, parts.shape[0]):
        total = total + parts[at].astype(F32)
    rows = out_ref.shape[0] - total.shape[0]
    out_ref[...] = jnp.concatenate([total, jnp.zeros((rows, C), F32)], axis=0).astype(BF16)


def line_sum_kernel(scale, parts, out_ref):
    total = parts[0].astype(F32)
    for at in range(1, parts.shape[0]):
        total = total + parts[at].astype(F32)
    total = (total * scale[0]).astype(BF16)
    for at in range(out_ref.shape[0]):
        out_ref[at] = total


def call(kernel, outs, inputs, scratch=(), scalars=0, flops=0):
    in_specs = [
        pl.BlockSpec(memory_space=pltpu.SMEM if n < scalars else pltpu.VMEM)
        for n in range(len(inputs))
    ]
    moved = sum(a.size * a.dtype.itemsize for a in inputs)
    moved += sum(math.prod(s) * jnp.dtype(t).itemsize for s, t in outs)
    return pl.pallas_call(
        kernel,
        out_shape=[jax.ShapeDtypeStruct(s, t) for s, t in outs],
        in_specs=in_specs,
        out_specs=[pl.BlockSpec(memory_space=pltpu.VMEM) for _ in outs],
        scratch_shapes=[pltpu.VMEM(s, t) for s, t in scratch],
        compiler_params=pltpu.CompilerParams(vmem_limit_bytes=40 * 1024 * 1024),
        cost_estimate=pl.CostEstimate(flops=flops, bytes_accessed=moved, transcendentals=0),
    )(*inputs)


def line(count, step):
    return [(i, i + step) for i in range(count) if 0 <= i + step < count]


def beside(last, leading, axis, count):
    before = lax.ppermute(last, axis, line(count, 1))
    after = lax.ppermute(leading, axis, line(count, -1))
    return before, after


def along_width(x, count):
    outer = lax.ppermute(x, WIDTH, [(i, i - 1 + 2 * (i % 2)) for i in range(1, count - 1)])
    inner = lax.ppermute(x, WIDTH, [(i, i ^ 1) for i in range(count)])
    return outer, inner


def in_order(outer, inner):
    first = lax.axis_index("core") == 0
    return jnp.where(first, outer, inner), jnp.where(first, inner, outer)


def exchanged(parts, axes):
    return lax.all_to_all(parts, axes, 0, 0, tiled=True)


def joined(parts):
    return parts.reshape(-1, C)


def local(volume, fine_weight, coarse_weight, cotangent):
    sizes = {axis: lax.axis_size(axis) for axis in AXES}
    plane, along = (sizes["gx"] * sizes["y"], sizes["gy"] * sizes["zh"])
    peers = [sizes["gx"], sizes["gy"], sizes["y"] * sizes["zh"] * 2]
    place = [lax.axis_index(axis) for axis in ("gx", "gy", WIDTH)]
    place = jnp.stack([p.astype(jnp.int32) for p in place])
    fine_sizes = [8 * n for n in peers]
    coarse_sizes = [4 * n for n in peers]

    fine_rows = fine_weight.reshape(27 * C, C)

    packed = jnp.concatenate([volume.reshape(512, C), cotangent.reshape(64, C)], axis=0)
    before, after = in_order(*along_width(packed, peers[2]))
    before_cells, after_cells = (b[:512].reshape(8, 8, 8, C) for b in (before, after))
    slabs = [
        jnp.concatenate([before_cells[:, at], volume[:, at], after_cells[:, at]], axis=2)
        for at in (slice(5, 8), slice(0, 3))
    ]
    below, above = beside(slabs[0], slabs[1], "gy", peers[1])
    own = jnp.concatenate([before_cells, volume, after_cells], axis=2)
    incoming = jnp.concatenate(
        [
            before[512:].reshape(4, 4, 4, C)[:, :, 2:],
            cotangent,
            after[512:].reshape(4, 4, 4, C)[:, :, :2],
        ],
        axis=2,
    ).astype(F32)
    sides = [
        jnp.concatenate([below[at], own[at], above[at]], axis=1)
        for at in (slice(5, 8), slice(0, 3))
    ]
    left, right = beside(sides[0], sides[1], "gx", peers[0])
    (middle,) = call(
        middle_kernel,
        [((6, 6, 24, C), F32)],
        [own.reshape(8, 192, C), fine_rows],
        scratch=[((8, 8, 32, C), F32), ((8, 144, 9 * C), BF16)],
        flops=2 * 864 * 27 * C * C,
    )
    across = [own.reshape(8, 192, C), below.reshape(8, 72, C), above.reshape(8, 72, C)]
    (edges,) = call(
        sides_kernel,
        [((6, 6, 24, C), F32)],
        across + [fine_rows],
        scratch=[((8, 10, 32, C), F32), ((8, 144, 9 * C), BF16)],
        flops=2 * 864 * 27 * C * C,
    )
    across = across + [left.reshape(3, 336, C), right.reshape(3, 336, C)]
    coarse, coarse_grad, slope, fine_sum, coarse_sum = call(
        lambda *refs: front_kernel(fine_sizes, coarse_sizes, *refs),
        [
            ((128, C), F32),
            ((128, C), BF16),
            ((12, 12, 24, C), F32),
            ((27 * C, C), BF16),
            ((27 * C, C), BF16),
        ],
        [place, *across, fine_rows, coarse_weight, incoming.reshape(128, C), middle, edges],
        scratch=[
            ((14, 14, 32, C), F32),
            ((10, 288, 9 * C), BF16),
            ((6, 12, 24, C), F32),
            ((6, 24, C), F32),
            ((6, 6, 16, C), F32),
            ((8, 8, 16, C), F32),
            ((6, 6, 16, C), F32),
            ((12, 12, 8, C), F32),
            ((14, 96, 9 * C), BF16),
        ],
        scalars=1,
        flops=2 * 4000 * 27 * C * C,
    )

    first = lax.axis_index("core") == 0
    swap = [(0, 1), (1, 0)]
    cells_fine = fine_sizes[0] * fine_sizes[1] * fine_sizes[2]
    scale = jnp.where(first, 1.0 / math.sqrt(cells_fine), 1.0 / math.sqrt(cells_fine // 8))
    scale = scale.astype(F32).reshape(1)
    mine = jnp.where(first, fine_sum, coarse_sum).astype(F32)
    other = jnp.where(first, coarse_sum, fine_sum)
    mine = mine + lax.ppermute(other, "core", swap).astype(F32)

    grads = coarse_grad.reshape(4, 4, 8, C)
    halo = beside(grads[:, 2:], grads[:, :2], "gy", peers[1])
    coarse_out = jax.nn.silu(coarse.reshape(4, 4, 8, C)[:, :, 2:6]).astype(BF16)
    parts = exchanged(mine.astype(BF16).reshape(plane, -1, C), PLANE)
    parts, halo, coarse_out = lax.optimization_barrier((parts, halo, coarse_out))
    length = parts.shape[1]
    padded = -(-length // (16 * along)) * 16 * along
    (part,) = call(plane_sum_kernel, [((padded, C), BF16)], [parts])
    parts = exchanged(part.reshape(along, padded // along, C), LINE)
    (parts,) = call(line_sum_kernel, [(parts.shape, BF16)], [scale, parts], scalars=1)
    parts = exchanged(parts, LINE)
    parts, halo = lax.optimization_barrier((parts, halo))
    part = joined(parts)[:length]
    grads = jnp.concatenate([halo[0], grads, halo[1]], axis=1)
    halo = beside(grads[2:], grads[:2], "gx", peers[0])
    fine_grad, begun = call(
        fine_grad_kernel,
        [((10, 10, 16, C), F32), ((512, C), F32)],
        [
            halo[0].reshape(128, C),
            grads.reshape(256, C),
            halo[1].reshape(128, C),
            coarse_weight,
            slope,
            fine_weight,
        ],
        scratch=[((8, 8, 16, C), F32), ((6, 6, 16, C), F32)],
        flops=2 * 460 * 27 * C * C,
    )
    parts = exchanged(jnp.broadcast_to(part[None], (plane, length, C)), PLANE)
    parts, fine_grad = lax.optimization_barrier((parts, fine_grad))
    (grad_volume,) = call(
        volume_kernel,
        [((512, C), BF16)],
        [fine_grad, begun, fine_weight],
        flops=2 * 342 * 27 * C * C,
    )
    mine = joined(parts)
    other = lax.ppermute(mine, "core", swap)
    fine_done = jnp.where(first, mine, other)
    coarse_done = jnp.where(first, other, mine)
    return (
        coarse_out,
        grad_volume.reshape(8, 8, 8, C),
        fine_done.reshape(27, C, C),
        coarse_done.reshape(27, C, C),
    )


def solution(mesh):
    shape = mesh.devices.shape
    inner = Mesh(mesh.devices.reshape(shape[0], shape[1], shape[2] // 4, 2, 2), AXES)
    cells = P("gx", "gy", WIDTH, None)
    return jax.shard_map(
        local,
        mesh=inner,
        in_specs=(cells, P(), P(), cells),
        out_specs=(cells, cells, P(), P()),
        check_vma=False,
    )
```
